32 devices in a mesh: dp: 16 (over z, x, core), tensor: 2 (over y).
Axes of the slice: x: 2, y: 2, z: 4, core: 2. Of those that a mesh axis runs over, the one named last changes fastest.
Arguments:
- layer_input: bfloat16 [32768, 512], P(('dp', 'tensor')), may hold values from -6 to 6
- gene_known: int32 [32768], P('dp'), may hold values 0 or 1
- cell_genes: int32 [16, 4], P('dp'), may hold values from 0 to 2048, as said below
- w_qkv: bfloat16 [512, 3, 512], P(None, None, 'tensor'), may hold values from -0.25 to 0.25
- bias_qv: bfloat16 [2, 512], P(None, 'tensor'), may hold values from -3 to 3
- w_out: bfloat16 [512, 512], P('tensor'), may hold values from -4 to 4
- b_out: float32 [512], replicated, may hold values from -3 to 3
- ln1_gain: float32 [512], replicated, may hold values from 0.1 to 1.9
- ln1_bias: float32 [512], replicated, may hold values from -2 to 2
- w_up: bfloat16 [512, 512], P(None, 'tensor'), may hold values from -0.25 to 0.25
- b_up: bfloat16 [512], P('tensor'), may hold values from -3 to 3
- w_down: bfloat16 [512, 512], P('tensor'), may hold values from -0.25 to 0.25
- b_down: float32 [512], replicated, may hold values from -3 to 3
- ln2_gain: float32 [512], replicated, may hold values from 0.1 to 1.9
- ln2_bias: float32 [512], replicated, may hold values from -2 to 2
- cotangent: bfloat16 [32768, 512], P(('dp', 'tensor')), may hold values from -6 to 6
Outputs:
- activations: bfloat16 [32768, 512], P(('dp', 'tensor'))
- input_grad: float32 [32768, 512], P(('dp', 'tensor'))
- w_qkv_grad: float32 [512, 3, 512], P(None, None, 'tensor')
- bias_qv_grad: float32 [2, 512], P(None, 'tensor')
- w_out_grad: float32 [512, 512], P('tensor')
- b_out_grad: float32 [512], replicated
- ln1_gain_grad: float32 [512], replicated
- ln1_bias_grad: float32 [512], replicated
- w_up_grad: float32 [512, 512], P(None, 'tensor')
- b_up_grad: float32 [512], P('tensor')
- w_down_grad: float32 [512, 512], P('tensor')
- b_down_grad: float32 [512], replicated
- ln2_gain_grad: float32 [512], replicated
- ln2_bias_grad: float32 [512], replicated
The draws below stay inside these ranges and needn't reach their ends.
Inputs may be any that keep to these rules, and one draw needn't show every extreme that they name: `cell_genes`: each row sums to 2048; a row is either 2048 followed by 4 - 1 zeros, or 4 positive lengths; at least one group holds a single cell.
All inputs are finite; a program needn't handle non-finite values. No bound on the sum of `gene_known` on one device may be relied on, other than what follows from the above.
Results may differ from the reference program's by a relative error of at most 0.019.
Values may be sent and summed in bfloat16 or wider, within the bound.
No kernel may reach another device: no remote copies, remote signals or barrier semaphores. Data moves between devices by JAX's collectives and lax.ppermute only.
A program may use at most 128 MiB of HBM per device.

```python
import jax
import jax.numpy as jnp
from jax import lax

D = 512
HEADS = 8
FF = 512
TOK_DP = 2048
HD = 64
TOKENS = 32768


def draw_cell_genes(key, part):
    key = jax.random.fold_in(key, 11)
    groups = TOKENS // TOK_DP
    keys_split = jax.random.split(key, 5)
    quarter = TOK_DP // 4
    eighth = TOK_DP // 8
    sixteenth = TOK_DP // 16
    first_shift = jax.random.randint(keys_split[0], (groups,), -eighth, eighth + 1)
    cross_shift = jax.random.randint(keys_split[1], (groups,), sixteenth, eighth + 1)
    third_shift = jax.random.randint(keys_split[2], (groups,), -sixteenth, sixteenth + 1)
    short_rows = jnp.stack([quarter + first_shift, quarter + cross_shift - first_shift, quarter + third_shift, quarter - cross_shift - third_shift], axis=1)
    long_rows = jnp.zeros((groups, 4), jnp.int32).at[:, 0].set(TOK_DP)
    single = jax.random.randint(keys_split[3], (groups,), 0, 2)
    forced = jax.random.randint(keys_split[4], (), 0, groups)
    single = jnp.where(jnp.arange(groups) == forced, 1, single)
    return jnp.where(single[:, None] == 1, long_rows, short_rows).astype(jnp.int32)


def set_ends(values, key, least, high):
    shape = values.shape
    index_at = [jax.random.randint(jax.random.fold_in(key, axis), (), 0, shape[axis]) for axis in range(len(shape))]
    values = values.at[tuple(index_at)].set(least)
    longest = shape.index(max(shape))
    index_at[longest] = (index_at[longest] + 1) % shape[longest]
    return values.at[tuple(index_at)].set(high)


def block_levels(rng, dims, shards, least, top_value):
    def one(position, blocks):
        heights = jax.random.uniform(jax.random.fold_in(jax.random.fold_in(rng, 6), position), (blocks,), jnp.float32, least / len(shards), top_value / len(shards))
        return jnp.repeat(jnp.exp(heights), dims[position] // blocks).reshape((-1,) + (1,) * (len(dims) - position - 1))

    gain = one(*shards[0])
    for cut in shards[1:]:
        gain = gain * one(*cut)
    return gain


def normal_values(own_key, extent, deviation, bound, pieces=(), kind=jnp.bfloat16):
    factor_of = block_levels(own_key, extent, pieces, -0.22, 0.18) if pieces else 1.0
    values = jax.random.normal(own_key, extent, jnp.float32) * deviation * factor_of
    return jnp.minimum(jnp.maximum(values, -bound), bound).astype(kind)


def setup_inputs(seed: int = 0) -> dict:
    seeds = jax.random.split(jax.random.key(seed), 17)
    layer_input = normal_values(seeds[0], (TOKENS, D), 1.0, 6.0, ((0, 32),))
    gene_known = set_ends((jax.random.randint(seeds[1], (TOKENS,), 0, 4) < 3).astype(jnp.int32), jax.random.fold_in(seeds[1], 1), 0, 1)
    cell_genes = draw_cell_genes(jax.random.fold_in(seeds[16], 71), 0)
    w_qkv = normal_values(seeds[3], (D, 3, D), D ** -0.5, 0.25, ((2, 2),))
    bias_qv = normal_values(seeds[4], (2, D), 0.5, 3.0, ((1, 2),))
    w_out = normal_values(seeds[5], (D, D), 2 ** -0.5, 4.0, ((0, 2),))
    b_out = normal_values(seeds[6], (D,), 0.5, 3.0, (), jnp.float32)
    ln1_gain = jnp.clip(1.0 + 0.18 * jax.random.normal(seeds[7], (D,), jnp.float32), 0.1, 1.9)
    ln1_bias = normal_values(seeds[8], (D,), 0.3, 2.0, (), jnp.float32)
    w_up = normal_values(seeds[9], (D, FF), D ** -0.5, 0.25, ((1, 2),))
    b_up = normal_values(seeds[10], (FF,), 0.5, 3.0, ((0, 2),))
    w_down = normal_values(seeds[11], (FF, D), FF ** -0.5, 0.25, ((0, 2),))
    b_down = normal_values(seeds[12], (D,), 0.5, 3.0, (), jnp.float32)
    ln2_gain = jnp.clip(1.0 + 0.18 * jax.random.normal(seeds[13], (D,), jnp.float32), 0.1, 1.9)
    ln2_bias = normal_values(seeds[14], (D,), 0.3, 2.0, (), jnp.float32)
    cotangent = normal_values(seeds[15], (TOKENS, D), 1.0, 6.0, ((0, 32),))
    return {"layer_input": layer_input, "gene_known": gene_known, "cell_genes": cell_genes, "w_qkv": w_qkv, "bias_qv": bias_qv, "w_out": w_out, "b_out": b_out, "ln1_gain": ln1_gain, "ln1_bias": ln1_bias, "w_up": w_up, "b_up": b_up, "w_down": w_down, "b_down": b_down, "ln2_gain": ln2_gain, "ln2_bias": ln2_bias, "cotangent": cotangent}


@jax.custom_vjp
def low(v):
    return lax.optimization_barrier(v.astype(jnp.bfloat16)).astype(jnp.float32)

@jax.custom_vjp
def low_back(v):
    return v

def low_keep(v):
    return (low(v), None)

def low_pass(kept, grad):
    return (grad,)

def back_keep(v):
    return (v, None)

def back_low(kept, grad):
    return (low(grad),)
low.defvjp(low_keep, low_pass)
low_back.defvjp(back_keep, back_low)
NORM_EPS = 1e-05
MASKED = -1e+30

def cell_layout(known_row, lengths):
    positions = jnp.arange(known_row.shape[0], dtype=jnp.int32)
    ends = jnp.cumsum(lengths).astype(jnp.int32)
    starts = (ends - lengths).astype(jnp.int32)
    cell_of = lax.optimization_barrier(jnp.sum((positions[:, None] >= ends[None, :]).astype(jnp.int32), axis=1))
    opening = jnp.any((positions[:, None] == starts[None, :]) & (lengths[None, :] > 0), axis=1)
    key_live = (known_row > 0) | opening
    return (key_live, cell_of)

def layer_norm(values, gain_vec, shift_vec):
    average = lax.optimization_barrier(jnp.mean(values, axis=-1, keepdims=True))
    centered = values - average
    variance = lax.optimization_barrier(jnp.mean(centered * centered, axis=-1, keepdims=True))
    return centered * lax.rsqrt(variance + NORM_EPS) * gain_vec + shift_vec

def attend_group(group_qkv, key_live, cell_of):
    queries = group_qkv[:, :D].reshape(TOK_DP, HEADS, HD)
    keys_all = group_qkv[:, D:2 * D].reshape(TOK_DP, HEADS, HD)
    values_all = group_qkv[:, 2 * D:].reshape(TOK_DP, HEADS, HD)
    block_rows = min(512, TOK_DP)
    blocks = TOK_DP // block_rows

    def one_block(inputs_pair):
        query_block, cell_block = inputs_pair
        logits = low_back(jnp.einsum('qhd,khd->hqk', query_block, keys_all, precision=lax.Precision.HIGHEST))
        allowed = (cell_block[:, None] == cell_of[None, :]) & key_live[None, :]
        scores = jnp.where(allowed[None], logits * HD ** (-0.5), MASKED)
        peak = lax.optimization_barrier(jnp.max(scores, axis=-1, keepdims=True))
        expo = jnp.exp(scores - peak)
        probs = low(expo / lax.optimization_barrier(jnp.sum(expo, axis=-1, keepdims=True)))
        return jnp.einsum('hqk,khd->qhd', probs, values_all, precision=lax.Precision.HIGHEST)
    mixed = lax.map(jax.checkpoint(one_block), (queries.reshape(blocks, block_rows, HEADS, HD), cell_of.reshape(blocks, block_rows)))
    return mixed.reshape(TOK_DP, D)

def reference(layer_input, gene_known, cell_genes, w_qkv, bias_qv, w_out, b_out, ln1_gain, ln1_bias, w_up, b_up, w_down, b_down, ln2_gain, ln2_bias, cotangent):
    groups = TOKENS // TOK_DP
    key_live, cell_of = jax.vmap(cell_layout)(gene_known.reshape(groups, TOK_DP), cell_genes)

    def group_step(triple):
        return attend_group(triple[0], triple[1], triple[2])

    def forward(inputs_f, qkv_f, bias_f, out_f, out_bias_f, gain_one, shift_one, up_f, up_bias_f, down_f, down_bias_f, gain_two, shift_two):
        entry = low(inputs_f)
        bias_flat = jnp.concatenate([bias_f[0], jnp.zeros((D,), jnp.float32), bias_f[1]])
        projected = low_back(low(jnp.dot(entry, qkv_f.reshape(D, 3 * D), precision=lax.Precision.HIGHEST) + bias_flat))
        attended = lax.map(jax.checkpoint(group_step), (projected.reshape(groups, TOK_DP, 3 * D), key_live, cell_of))
        attended = low_back(low(attended.reshape(TOKENS, D)))
        attn_branch = low_back(jnp.dot(attended, out_f, precision=lax.Precision.HIGHEST))
        first_norm = layer_norm(inputs_f + attn_branch + out_bias_f, gain_one, shift_one)
        hidden_pre = low_back(jnp.dot(low(first_norm), up_f, precision=lax.Precision.HIGHEST) + up_bias_f)
        hidden = low(jax.nn.gelu(hidden_pre, approximate=False))
        ffn_branch = low_back(jnp.dot(hidden, down_f, precision=lax.Precision.HIGHEST))
        return layer_norm(first_norm + ffn_branch + down_bias_f, gain_two, shift_two)
    floats = (layer_input.astype(jnp.float32), w_qkv.astype(jnp.float32), bias_qv.astype(jnp.float32), w_out.astype(jnp.float32), b_out.astype(jnp.float32), ln1_gain.astype(jnp.float32), ln1_bias.astype(jnp.float32), w_up.astype(jnp.float32), b_up.astype(jnp.float32), w_down.astype(jnp.float32), b_down.astype(jnp.float32), ln2_gain.astype(jnp.float32), ln2_bias.astype(jnp.float32))
    result, backward = jax.vjp(forward, *floats)
    grads = backward(cotangent.astype(jnp.float32))
    return (result.astype(jnp.bfloat16), grads[0], grads[1], grads[2], grads[3], grads[4], grads[5], grads[6], grads[7], grads[8], grads[9], grads[10], grads[11], grads[12])
```

```python
import functools

import jax
import jax.numpy as jnp
from jax import lax
from jax.experimental import pallas as pl
from jax.experimental.pallas import tpu as pltpu
from jax.sharding import PartitionSpec as P

HD = 64
LANES = 128
NORM_EPS = 1e-05
MASK_BIG = 2.0**100
LOG2E = 1.4426950408889634
VMEM_BYTES = 58 * 2**20
BF = jnp.bfloat16
F32 = jnp.float32
VMEM = pl.BlockSpec(memory_space=pltpu.VMEM)
HBM = pl.BlockSpec(memory_space=pl.ANY)


def dot(left, right, left_dim, right_dim):
    return lax.dot_general(
        left, right, (((left_dim,), (right_dim,)), ((), ())), preferred_element_type=F32
    )


def params():
    return pltpu.CompilerParams(vmem_limit_bytes=VMEM_BYTES)


def cost(macs, moved):
    return pl.CostEstimate(flops=2 * macs, bytes_accessed=moved, transcendentals=0)


def key_value_blocks(x_block, w_k, w_v, bias_v, extra_k, extra_v, k_ref, v_ref, rows):
    heads = k_ref.shape[0]
    low = lax.broadcasted_iota(jnp.int32, extra_k.shape, 1) < HD
    keys = dot(x_block, w_k, 1, 0)
    values = dot(x_block, w_v, 1, 0) + bias_v
    for h in range(heads):
        pair = slice((h // 2) * LANES, (h // 2 + 1) * LANES)
        k_pair, v_pair = keys[:, pair], values[:, pair]
        if h % 2:
            k_pair, v_pair = pltpu.roll(k_pair, HD, 1), pltpu.roll(v_pair, HD, 1)
        k_ref[h, rows, :] = jnp.where(low, k_pair, extra_k).astype(BF)
        v_ref[h, rows, :] = jnp.where(low, v_pair, extra_v).astype(BF)


def project_kernel(block, x_ref, w_ref, bias_v_ref, extra_k_ref, k_ref, v_ref):
    width = x_ref.shape[1]
    w_k, w_v = w_ref[:, width : 2 * width], w_ref[:, 2 * width :]
    lane = lax.broadcasted_iota(jnp.int32, (block, LANES), 1)
    extra_v = jnp.where((lane == HD) | (lane == HD + 1), 1.0, 0.0)

    @pl.loop(0, x_ref.shape[0] // block)
    def _(i):
        rows = pl.ds(pl.multiple_of(i * block, block), block)
        key_value_blocks(
            x_ref[rows, :], w_k, w_v, bias_v_ref[...], extra_k_ref[rows, :], extra_v, k_ref, v_ref, rows
        )


def project(x, w_qkv, bias_v, extra_k):
    tokens, width = x.shape
    heads = width // HD
    out = jax.ShapeDtypeStruct((heads, tokens, LANES), BF)
    return pl.pallas_call(
        functools.partial(project_kernel, 256),
        out_shape=(out, out),
        in_specs=[VMEM] * 4,
        out_specs=(VMEM, VMEM),
        compiler_params=params(),
        cost_estimate=cost(2 * tokens * width * width, 8 * tokens * width),
        name="project_kv",
    )(x, w_qkv, bias_v, extra_k)


def query_kernel(x_ref, w_ref, bias_ref, bias_col_ref, extra_ref, qt_ref, q_ref):
    width = x_ref.shape[1]
    w_q = w_ref[:, :width]
    q_ref[...] = (dot(x_ref[...], w_q, 1, 0) + bias_ref[...]).astype(BF)
    for h in range(width // HD):
        head = slice(h * HD, (h + 1) * HD)
        turned = dot(w_ref[:, head], x_ref[...], 0, 1) + bias_col_ref[head, :]
        qt_ref[h, :HD, :] = turned.astype(BF)
        qt_ref[h, HD:, :] = extra_ref[...]


def project_queries(x, w_qkv, bias, bias_col, extra):
    tokens, width = x.shape
    return pl.pallas_call(
        query_kernel,
        out_shape=(
            jax.ShapeDtypeStruct((width // HD, LANES, tokens), BF),
            jax.ShapeDtypeStruct((tokens, width), BF),
        ),
        in_specs=[VMEM] * 5,
        out_specs=(VMEM, VMEM),
        compiler_params=params(),
        cost_estimate=cost(2 * tokens * width * width, 8 * tokens * width),
        name="project_q",
    )(x, w_qkv, bias, bias_col, extra)


def attend_kernel(
    block, qt_ref, k0_ref, k1_ref, v0_ref, v1_ref, p_hbm, ot_ref, linv_ref,
    s_scr, peak_scr, row_scr, acc_scr, p_scr, sem,
):
    heads, _, queries = qt_ref.shape
    half = k0_ref.shape[1] // block
    blocks = 2 * half

    def copy_out(h, j, slot):
        return pltpu.make_async_copy(
            p_scr.at[slot], p_hbm.at[h, pl.ds(pl.multiple_of(j * block, block), block), :], sem.at[slot]
        )

    def scores(h, keys, j):
        slot = lax.rem(h, 2)
        s = dot(keys, qt_ref[h], 1, 0)
        s_scr[slot, pl.ds(pl.multiple_of(j * block, block), block), :] = s
        top = jnp.max(s.reshape(block // 8, 8, queries), axis=0)
        peak_scr[slot] = jnp.maximum(peak_scr[slot], top)

    def mix(h, values, j):
        slot = lax.rem(j, 2)

        @pl.when((h > 0) | (j > 1))
        def _():
            copy_out(h, j, slot).wait()

        s = s_scr[lax.rem(h, 2), pl.ds(pl.multiple_of(j * block, block), block), :]
        p = jnp.exp2((s - row_scr[...]) * (LOG2E * HD**-0.5)).astype(BF)
        p_scr[slot] = p
        copy_out(h, j, slot).start()
        acc_scr[...] += dot(values, p, 0, 0)

    def at(j):
        return pl.ds(pl.multiple_of(j * block, block), block)

    def over_blocks(h, score, mixing):
        for part, (k_ref, v_ref) in enumerate(((k0_ref, v0_ref), (k1_ref, v1_ref))):

            @pl.loop(0, half)
            def _(i):
                j = part * half + i
                if score:
                    scores(h + 1, k_ref[h + 1, at(i), :], j)
                if mixing:
                    mix(h, v_ref[h, at(i), :], j)

    def open_scores(h):
        peak_scr[lax.rem(h, 2)] = jnp.full((8, queries), -jnp.inf, F32)

    def open_mix(h):
        row_scr[...] = jnp.max(peak_scr[lax.rem(h, 2)], axis=0, keepdims=True)
        acc_scr[...] = jnp.zeros_like(acc_scr)

    def close_mix(h):
        inverse = 1.0 / acc_scr[HD : HD + 1, :]
        linv_ref[h] = inverse
        ot_ref[h] = acc_scr[:HD, :] * inverse

    open_scores(0)
    over_blocks(-1, True, False)

    @pl.loop(0, heads - 1)
    def _(h):
        open_scores(h + 1)
        open_mix(h)
        over_blocks(h, True, True)
        close_mix(h)

    open_mix(heads - 1)
    over_blocks(heads - 1, False, True)
    close_mix(heads - 1)
    for slot in range(2):
        copy_out(heads - 1, blocks - 2 + slot, slot).wait()


def attend(qt, k_own, k_oth, v_own, v_oth):
    heads, _, queries = qt.shape
    keys = 2 * k_own.shape[1]
    block = 256
    return pl.pallas_call(
        functools.partial(attend_kernel, block),
        out_shape=(
            jax.ShapeDtypeStruct((heads, keys, queries), BF),
            jax.ShapeDtypeStruct((heads, HD, queries), F32),
            jax.ShapeDtypeStruct((heads, 1, queries), F32),
        ),
        in_specs=[VMEM] * 5,
        out_specs=(HBM, VMEM, VMEM),
        scratch_shapes=[
            pltpu.VMEM((2, keys, queries), F32),
            pltpu.VMEM((2, 8, queries), F32),
            pltpu.VMEM((1, queries), F32),
            pltpu.VMEM((LANES, queries), F32),
            pltpu.VMEM((2, block, queries), BF),
            pltpu.SemaphoreType.DMA((2,)),
        ],
        compiler_params=params(),
        cost_estimate=cost(heads * keys * queries * 512, 2 * heads * keys * queries),
        name="attend",
    )(qt, k_own, k_oth, v_own, v_oth)


def normalize(values):
    mean = jnp.mean(values, axis=-1, keepdims=True)
    centered = values - mean
    inverse = lax.rsqrt(jnp.mean(centered * centered, axis=-1, keepdims=True) + NORM_EPS)
    return centered * inverse, inverse


def norm_back(e, normed, inverse):
    return inverse * (
        e - jnp.mean(e, axis=-1, keepdims=True) - normed * jnp.mean(e * normed, axis=-1, keepdims=True)
    )


def middle_kernel(
    block, x_ref, cot_ref, ot_ref, linv_ref, w_out_ref, w_up_ref, w_down_ref, b_up_ref,
    vec_ref, act_ref, res_ref, dot_ref, dnat_ref, gw_ref, small_ref, att_scr,
):
    tokens, width = x_ref.shape
    heads = width // HD
    b_out, gain1, bias1, b_down, gain2, bias2 = (vec_ref[i : i + 1, :] for i in range(6))
    gw_ref[...] = jnp.zeros_like(gw_ref)
    small_ref[...] = jnp.zeros_like(small_ref)

    def col_sum(row, values):
        small_ref[row : row + 1, :] += jnp.sum(values, axis=0, keepdims=True)

    @pl.loop(0, tokens // block)
    def _(i):
        rows = pl.ds(pl.multiple_of(i * block, block), block)
        for h in range(heads):
            att_scr[h * HD : (h + 1) * HD, :] = ot_ref[h, :, rows].astype(BF)
        att = att_scr[...]
        first_sum = x_ref[rows, :].astype(F32) + dot(att, w_out_ref[...], 0, 0) + b_out
        n1, inv1 = normalize(first_sum)
        first = n1 * gain1 + bias1
        first_low = first.astype(BF)
        pre = dot(first_low, w_up_ref[...], 1, 0) + b_up_ref[...]
        cdf = 0.5 * (1.0 + lax.erf(pre * 0.5**0.5))
        hidden = (pre * cdf).astype(BF)
        slope = cdf + pre * (0.3989422804014327 * jnp.exp(-0.5 * pre * pre))
        n2, inv2 = normalize(first + dot(hidden, w_down_ref[...], 1, 0) + b_down)
        act_ref[rows, :] = (n2 * gain2 + bias2).astype(BF)
        cot = cot_ref[rows, :].astype(F32)
        two = norm_back(cot * gain2, n2, inv2)
        col_sum(3, two)
        col_sum(4, cot * n2)
        col_sum(5, cot)
        two_low = two.astype(BF)
        gw_ref[2] += dot(hidden, two_low, 0, 0)
        pre_grad = (dot(two_low, w_down_ref[...], 1, 1) * slope).astype(BF)
        gw_ref[1] += dot(first_low, pre_grad, 0, 0)
        col_sum(6, pre_grad.astype(F32))
        one = two + dot(pre_grad, w_up_ref[...], 1, 1)
        col_sum(1, one * n1)
        col_sum(2, one)
        res = norm_back(one * gain1, n1, inv1)
        col_sum(0, res)
        res_ref[rows, :] = res
        res_low = res.astype(BF)
        gw_ref[0] += dot(att, res_low, 1, 0)
        for h in range(heads):
            head = slice(h * HD, (h + 1) * HD)
            grad = dot(w_out_ref[head, :], res_low, 1, 1).astype(BF).astype(F32)
            grad = (grad * linv_ref[h, :, rows]).astype(BF)
            dot_ref[h, :HD, rows] = grad
            inner = -jnp.sum(grad.astype(F32) * ot_ref[h, :, rows], axis=0, keepdims=True)
            high = inner.astype(BF).astype(F32)
            pick = lax.broadcasted_iota(jnp.int32, (HD, block), 0)
            dot_ref[h, HD:, rows] = jnp.where(
                pick == 0, high, jnp.where(pick == 1, inner - high, 0.0)
            ).astype(BF)
            att_scr[head, :] = grad
        dnat_ref[rows, :] = att_scr[...].T


def middle(x, cot, ot, linv, w_out, w_up, w_down, b_up, vectors):
    tokens, width = x.shape
    heads = width // HD
    block = 256
    return pl.pallas_call(
        functools.partial(middle_kernel, block),
        out_shape=(
            jax.ShapeDtypeStruct((tokens, width), BF),
            jax.ShapeDtypeStruct((tokens, width), F32),
            jax.ShapeDtypeStruct((heads, LANES, tokens), BF),
            jax.ShapeDtypeStruct((tokens, width), BF),
            jax.ShapeDtypeStruct((3, width, width), F32),
            jax.ShapeDtypeStruct((8, width), F32),
        ),
        in_specs=[VMEM] * 9,
        out_specs=(VMEM,) * 6,
        scratch_shapes=[pltpu.VMEM((width, block), BF)],
        compiler_params=params(),
        cost_estimate=cost(9 * tokens * width * width, 20 * tokens * width),
        name="middle",
    )(x, cot, ot, linv, w_out, w_up, w_down, b_up, vectors)


def backward_kernel(
    block, p_hbm, dot_ref, dnat_ref, q_ref, k0_ref, k1_ref, v0_ref, v1_ref,
    dqt_ref, dk_ref, dv_ref, acc_scr, p_scr, sem,
):
    heads, _, queries = dot_ref.shape
    half = k0_ref.shape[1] // block
    blocks = 2 * half
    pairs = heads // 2
    low = lax.broadcasted_iota(jnp.int32, (block, LANES), 1) < HD

    def at(j):
        return pl.ds(pl.multiple_of(j * block, block), block)

    def copy_in(p, j, slot):
        return pltpu.make_async_copy(p_hbm.at[pl.ds(2 * p, 2), at(j), :], p_scr.at[slot], sem.at[slot])

    copy_in(0, 0, 0).start()

    @pl.loop(0, pairs)
    def _(p):
        lanes = pl.ds(pl.multiple_of(p * LANES, LANES), LANES)
        acc_scr[...] = jnp.zeros_like(acc_scr)
        for part, (k_ref, v_ref) in enumerate(((k0_ref, v0_ref), (k1_ref, v1_ref))):

            @pl.loop(0, half)
            def _(i):
                j = part * half + i
                slot = lax.rem(j, 2)
                copy_in(p, j, slot).wait()
                wrap = (j + 1) // blocks

                @pl.when(p * blocks + j + 1 < pairs * blocks)
                def _():
                    copy_in(p + wrap, lax.rem(j + 1, blocks), 1 - slot).start()

                dks, dvs = [], []
                for side in range(2):
                    h = 2 * p + side
                    prob = p_scr[slot, side]
                    slope = dot(v_ref[h, at(i), :], dot_ref[h], 1, 0)
                    dvs.append(dot(prob, dnat_ref[:, lanes], 1, 0))
                    ds = (prob.astype(F32) * slope).astype(BF)
                    dks.append(dot(ds, q_ref[:, lanes], 1, 0))
                    acc_scr[side] += dot(k_ref[h, at(i), :], ds, 0, 0)
                dk_ref[at(j), lanes] = (jnp.where(low, dks[0], dks[1]) * HD**-0.5).astype(BF)
                dv_ref[at(j), lanes] = jnp.where(low, dvs[0], dvs[1]).astype(BF)

        for side in range(2):
            dqt_ref[2 * p + side] = (acc_scr[side, :HD, :] * HD**-0.5).astype(BF)


def attend_backward(probs, dot_turned, dnat, q, k_own, k_oth, v_own, v_oth):
    heads, keys, queries = probs.shape
    width = heads * HD
    block = 256
    return pl.pallas_call(
        functools.partial(backward_kernel, block),
        out_shape=(
            jax.ShapeDtypeStruct((heads, HD, queries), BF),
            jax.ShapeDtypeStruct((keys, width), BF),
            jax.ShapeDtypeStruct((keys, width), BF),
        ),
        in_specs=[HBM] + [VMEM] * 7,
        out_specs=(VMEM,) * 3,
        scratch_shapes=[
            pltpu.VMEM((2, LANES, queries), F32),
            pltpu.VMEM((2, 2, block, queries), BF),
            pltpu.SemaphoreType.DMA((2,)),
        ],
        compiler_params=params(),
        cost_estimate=cost(heads * keys * queries * 1024, 2 * heads * keys * queries),
        name="attend_back",
    )(probs, dot_turned, dnat, q, k_own, k_oth, v_own, v_oth)


def finish_kernel(block, x0_ref, x1_ref, res_ref, dqt_ref, dk_ref, dv_ref, w_ref, own_ref, oth_ref, gw_ref, bias_ref):
    tokens, width = x0_ref.shape
    half = tokens // block
    gw_ref[...] = jnp.zeros_like(gw_ref)
    bias_ref[...] = jnp.zeros_like(bias_ref)
    w_q, w_k, w_v = (w_ref[:, i * width : (i + 1) * width] for i in range(3))

    @pl.loop(0, half)
    def _(i):
        rows = pl.ds(pl.multiple_of(i * block, block), block)
        after = pl.ds(pl.multiple_of((half + i) * block, block), block)
        dq = dqt_ref[:, rows].T
        dk, dv = dk_ref[rows, :], dv_ref[rows, :]
        own_ref[rows, :] = res_ref[rows, :] + dot(dq, w_q, 1, 1) + dot(dk, w_k, 1, 1) + dot(dv, w_v, 1, 1)
        dk1, dv1 = dk_ref[after, :], dv_ref[after, :]
        oth_ref[rows, :] = (dot(dk1, w_k, 1, 1) + dot(dv1, w_v, 1, 1)).astype(BF)
        x0, x1 = x0_ref[rows, :], x1_ref[rows, :]
        gw_ref[:, :width] += dot(x0, dq, 0, 0)
        gw_ref[:, width : 2 * width] += dot(x0, dk, 0, 0) + dot(x1, dk1, 0, 0)
        gw_ref[:, 2 * width :] += dot(x0, dv, 0, 0) + dot(x1, dv1, 0, 0)
        bias_ref[0:1, :] += jnp.sum(dq.astype(F32), axis=0, keepdims=True)
        bias_ref[1:2, :] += jnp.sum(dv.astype(F32) + dv1.astype(F32), axis=0, keepdims=True)


def finish(x_own, x_oth, res, dqt, dk, dv, w_qkv):
    tokens, width = x_own.shape
    return pl.pallas_call(
        functools.partial(finish_kernel, 256),
        out_shape=(
            jax.ShapeDtypeStruct((tokens, width), F32),
            jax.ShapeDtypeStruct((tokens, width), BF),
            jax.ShapeDtypeStruct((width, 3 * width), F32),
            jax.ShapeDtypeStruct((8, width), F32),
        ),
        in_specs=[VMEM] * 7,
        out_specs=(VMEM,) * 4,
        compiler_params=params(),
        cost_estimate=cost(10 * tokens * width * width, 20 * tokens * width),
        name="finish",
    )(x_own, x_oth, res, dqt, dk, dv, w_qkv)


def mask_columns(known, lengths):
    positions = jnp.arange(known.shape[0], dtype=jnp.int32)
    ends = jnp.cumsum(lengths)
    starts = ends - lengths
    inside = (positions[:, None] >= starts[None, :]) & (positions[:, None] < ends[None, :])
    opening = jnp.any((positions[:, None] == starts[None, :]) & (lengths[None, :] > 0), axis=1)
    dead = ~((known > 0) | opening)
    slots = lengths.shape[0]
    keys = jnp.concatenate([inside, dead[:, None]], axis=1).astype(F32)
    keys = jnp.pad(keys, ((0, 0), (HD, LANES - HD - slots - 1)))
    queries = jnp.where(jnp.pad(inside, ((0, 0), (0, 1))), 0.0, -MASK_BIG)
    queries = jnp.pad(queries, ((0, 0), (0, HD - slots - 1))).T.astype(BF)
    return keys, queries


def local(
    layer_input, gene_known, cell_genes, w_qkv, bias_qv, w_out, b_out, ln1_gain, ln1_bias,
    w_up, b_up, w_down, b_down, ln2_gain, ln2_bias, cotangent,
):
    tokens, width = layer_input.shape
    shard = w_qkv.shape[2]
    swap = [(0, 1), (1, 0)]
    side = lax.axis_index("tensor")

    def swapped(values):
        return lax.ppermute(values, "tensor", swap)

    x_oth = swapped(layer_input)
    qkv_oth, bias_oth = swapped(w_qkv), swapped(bias_qv)
    out_oth, up_oth, down_oth, b_up_oth = swapped(w_out), swapped(w_up), swapped(w_down), swapped(b_up)

    w_all = jnp.concatenate([w_qkv, qkv_oth], axis=2).reshape(width, 3 * width)
    bias_all = jnp.concatenate([bias_qv, bias_oth], axis=1).astype(F32)
    w_out_all = jnp.concatenate([w_out, out_oth], axis=0)
    w_up_all = jnp.concatenate([w_up, up_oth], axis=1)
    w_down_all = jnp.concatenate([w_down, down_oth], axis=0)
    b_up_all = jnp.concatenate([b_up, b_up_oth])[None].astype(F32)

    key_cols, query_rows = mask_columns(gene_known, cell_genes[0])
    key_own = lax.dynamic_slice_in_dim(key_cols, side * tokens, tokens, 0)
    key_oth = lax.dynamic_slice_in_dim(key_cols, (1 - side) * tokens, tokens, 0)
    query_own = lax.dynamic_slice_in_dim(query_rows, side * tokens, tokens, 1)

    qt, q = project_queries(layer_input, w_all, bias_all[:1], bias_all[0][:, None], query_own)
    k_own, v_own = project(layer_input, w_all, bias_all[1:], key_own)
    k_oth, v_oth = project(x_oth, w_all, bias_all[1:], key_oth)
    probs, ot, linv = attend(qt, k_own, k_oth, v_own, v_oth)
    vectors = jnp.stack([b_out, ln1_gain, ln1_bias, b_down, ln2_gain, ln2_bias, b_out, b_out])
    activations, res, dot_turned, dnat, gw_mid, small = middle(
        layer_input, cotangent, ot, linv, w_out_all, w_up_all, w_down_all, b_up_all, vectors
    )
    dqt, dk, dv = attend_backward(probs, dot_turned, dnat, q, k_own, k_oth, v_own, v_oth)
    grad_own, grad_oth, gw_qkv, bias_grad = finish(
        layer_input, x_oth, res, dqt.reshape(width, tokens), dk, dv, w_all
    )
    input_grad = grad_own + swapped(grad_oth).astype(F32)

    def shards(values, axis):
        return lax.slice_in_dim(values, 0, shard, axis=axis), lax.slice_in_dim(values, shard, 2 * shard, axis=axis)

    parts = [
        shards(gw_qkv.reshape(width, 3, width), 2),
        shards(bias_grad[:2], 1),
        shards(gw_mid[0], 0),
        shards(gw_mid[1], 1),
        shards(small[6], 0),
        shards(gw_mid[2], 0),
    ]
    got = [swapped(oth.astype(BF)).astype(F32) + own for own, oth in parts]
    qkv_g, bias_g, out_g, up_g, b_up_g, down_g = lax.psum(got, "dp")
    small_g = lax.psum(small[:6], ("dp", "tensor"))
    return (
        activations, input_grad, qkv_g, bias_g, out_g, small_g[0], small_g[1], small_g[2],
        up_g, b_up_g, down_g, small_g[3], small_g[4], small_g[5],
    )


def solution(mesh):
    placed = (
        P(("dp", "tensor"), None),
        P("dp"),
        P("dp", None),
        P(None, None, "tensor"),
        P(None, "tensor"),
        P("tensor", None),
        P(),
        P(),
        P(),
        P(None, "tensor"),
        P("tensor"),
        P("tensor", None),
        P(),
        P(),
        P(),
        P(("dp", "tensor"), None),
    )
    return jax.shard_map(
        local,
        mesh=mesh,
        in_specs=placed,
        out_specs=(
            P(("dp", "tensor"), None),
            P(("dp", "tensor"), None),
            P(None, None, "tensor"),
            P(None, "tensor"),
            P("tensor", None),
            P(),
            P(),
            P(),
            P(None, "tensor"),
            P("tensor"),
            P("tensor", None),
            P(),
            P(),
            P(),
        ),
        check_vma=False,
    )
```

```python
import functools

import jax
import jax.numpy as jnp
from jax import lax
from jax.experimental import pallas as pl
from jax.experimental.pallas import tpu as pltpu
from jax.sharding import PartitionSpec as P

HD = 64
LANES = 128
NORM_EPS = 1e-05
MASK_BIG = 2.0**100
LOG2E = 1.4426950408889634
VMEM_BYTES = 58 * 2**20
BF = jnp.bfloat16
F32 = jnp.float32
VMEM = pl.BlockSpec(memory_space=pltpu.VMEM)
HBM = pl.BlockSpec(memory_space=pl.ANY)


def dot(left, right, left_dim, right_dim):
    return lax.dot_general(
        left, right, (((left_dim,), (right_dim,)), ((), ())), preferred_element_type=F32
    )


def params():
    return pltpu.CompilerParams(vmem_limit_bytes=VMEM_BYTES)


def cost(macs, moved):
    return pl.CostEstimate(flops=2 * macs, bytes_accessed=moved, transcendentals=0)


def values_columns(rows):
    lane = lax.broadcasted_iota(jnp.int32, (rows, LANES), 1)
    return jnp.where((lane == HD) | (lane == HD + 1), 1.0, 0.0)


def key_value_block(x, w_refs, bias_ref, extra_k, k_ref, v_ref, rows):
    shard = w_refs[0].shape[1] // 3
    extra_k = extra_k.astype(F32)
    extra_v = values_columns(x.shape[0])
    low = lax.broadcasted_iota(jnp.int32, extra_k.shape, 1) < HD
    for side, w_ref in enumerate(w_refs):
        mine = slice(side * shard, (side + 1) * shard)
        keys = dot(x, w_ref[:, shard : 2 * shard], 1, 0)
        values = dot(x, w_ref[:, 2 * shard :], 1, 0) + bias_ref[1:2, mine]
        for i in range(shard // HD):
            pair = slice((i // 2) * LANES, (i // 2 + 1) * LANES)
            k_pair, v_pair = keys[:, pair], values[:, pair]
            if i % 2:
                k_pair, v_pair = pltpu.roll(k_pair, HD, 1), pltpu.roll(v_pair, HD, 1)
            h = side * (shard // HD) + i
            k_ref[h, rows, :] = jnp.where(low, k_pair, extra_k).astype(BF)
            v_ref[h, rows, :] = jnp.where(low, v_pair, extra_v).astype(BF)


def project_kernel(x_ref, own_ref, oth_ref, bias_ref, extra_k_ref, extra_q_ref, k_ref, v_ref, qt_ref, q_ref):
    x = x_ref[...]
    shard = own_ref.shape[1] // 3
    key_value_block(x, (own_ref, oth_ref), bias_ref, extra_k_ref[...], k_ref, v_ref, slice(None))
    for side, w_ref in enumerate((own_ref, oth_ref)):
        mine = slice(side * shard, (side + 1) * shard)
        q = (dot(x, w_ref[:, :shard], 1, 0) + bias_ref[0:1, mine]).astype(BF)
        q_ref[:, mine] = q
        turned = q.T
        for i in range(shard // HD):
            h = side * (shard // HD) + i
            qt_ref[h, :HD, :] = turned[i * HD : (i + 1) * HD, :]
            qt_ref[h, HD:, :] = extra_q_ref[...]


def project(x, w_own, w_oth, bias, extra_k, extra_q):
    tokens, width = x.shape
    heads = width // HD
    block = 256
    whole = lambda *shape: pl.BlockSpec(shape, lambda i: (0,) * len(shape))
    per_head = pl.BlockSpec((heads, block, LANES), lambda i: (0, i, 0))
    return pl.pallas_call(
        project_kernel,
        grid=(tokens // block,),
        out_shape=(
            jax.ShapeDtypeStruct((heads, tokens, LANES), BF),
            jax.ShapeDtypeStruct((heads, tokens, LANES), BF),
            jax.ShapeDtypeStruct((heads, LANES, tokens), BF),
            jax.ShapeDtypeStruct((tokens, width), BF),
        ),
        in_specs=[
            pl.BlockSpec((block, width), lambda i: (i, 0)),
            whole(*w_own.shape),
            whole(*w_oth.shape),
            whole(*bias.shape),
            pl.BlockSpec((block, LANES), lambda i: (i, 0)),
            pl.BlockSpec((HD, block), lambda i: (0, i)),
        ],
        out_specs=(
            per_head,
            per_head,
            pl.BlockSpec((heads, LANES, block), lambda i: (0, 0, i)),
            pl.BlockSpec((block, width), lambda i: (i, 0)),
        ),
        compiler_params=params(),
        cost_estimate=cost(3 * tokens * width * width, 12 * tokens * width),
        name="project",
    )(x, w_own, w_oth, bias, extra_k, extra_q)


def attend_kernel(
    sub, chunk, qt_hbm, k_hbm, v_hbm, x_ref, own_ref, oth_ref, bias_ref, extra_ref,
    p_hbm, ot_ref, linv_ref, k_oth_hbm, v_oth_hbm,
    qt_ref, k0_ref, k1_ref, v0_ref, v1_ref,
    s0_scr, s1_scr, peak0_scr, peak1_scr, row_scr, acc_scr, p_scr, sem, in_sem, out_sem,
):
    heads, _, queries = qt_ref.shape
    half = k0_ref.shape[1]
    parts = queries // chunk
    steps = heads * parts
    slots = p_scr.shape[0]

    def copies_in(h):
        return [
            pltpu.make_async_copy(src.at[h], dst.at[h], in_sem.at[h, n])
            for n, (src, dst) in enumerate(((qt_hbm, qt_ref), (k_hbm, k0_ref), (v_hbm, v0_ref)))
        ]

    for h in range(heads):
        for copy in copies_in(h):
            copy.start()

    @pl.loop(0, half // sub)
    def _(i):
        rows = pl.ds(pl.multiple_of(i * sub, sub), sub)
        key_value_block(x_ref[rows, :], (own_ref, oth_ref), bias_ref, extra_ref[rows, :], k1_ref, v1_ref, rows)

    copies_kv = [
        pltpu.make_async_copy(k1_ref, k_oth_hbm, out_sem.at[0]),
        pltpu.make_async_copy(v1_ref, v_oth_hbm, out_sem.at[1]),
    ]
    for copy in copies_kv:
        copy.start()

    def columns(step):
        return pl.ds(pl.multiple_of(lax.rem(step, parts) * chunk, chunk), chunk)

    def copy_out(step):
        slot = lax.rem(step, slots)
        return pltpu.make_async_copy(p_scr.at[slot], p_hbm.at[step // parts, :, columns(step)], sem.at[slot])

    def blocks(first, second):
        for part, ref in enumerate((first, second)):
            for u in range(half // sub):
                yield ref, slice(u * sub, (u + 1) * sub), slice(part * half + u * sub, part * half + (u + 1) * sub)

    def scores(step, s_ref, peak, keys, rows, to):
        s = dot(keys[step // parts, rows, :], qt_ref[step // parts, :, columns(step)], 1, 0)
        s_ref[to, :] = s
        return jnp.maximum(peak, jnp.max(s.reshape(sub // 8, 8, chunk), axis=0))

    def mix(step, s_ref, values, rows, to):
        p = jnp.exp2((s_ref[to, :] - row_scr[...]) * (LOG2E * HD**-0.5)).astype(BF)
        p_scr[lax.rem(step, slots), to, :] = p
        return dot(values[step // parts, rows, :], p, 0, 0)

    def run(step, s_ref, peak_ref, after, s_after, peak_after):
        row_scr[...] = jnp.max(peak_ref[...], axis=0, keepdims=True)

        @pl.when(step >= slots)
        def _():
            copy_out(step - slots).wait()

        peak = jnp.full((8, chunk), -jnp.inf, F32)
        acc = jnp.zeros((LANES, chunk), F32)
        for (k_ref, rows, to), (v_ref, _, _) in zip(blocks(k0_ref, k1_ref), blocks(v0_ref, v1_ref)):
            peak = scores(after, s_after, peak, k_ref, rows, to)
            acc = acc + mix(step, s_ref, v_ref, rows, to)
        peak_after[...] = peak
        acc_scr[...] = acc
        copy_out(step).start()
        inverse = 1.0 / acc_scr[HD : HD + 1, :]
        linv_ref[step // parts, :, columns(step)] = inverse
        ot_ref[step // parts, :, columns(step)] = acc_scr[:HD, :] * inverse

    for copy in copies_in(0):
        copy.wait()
    peak = jnp.full((8, chunk), -jnp.inf, F32)
    for k_ref, rows, to in blocks(k0_ref, k1_ref):
        peak = scores(0, s0_scr, peak, k_ref, rows, to)
    peak0_scr[...] = peak

    @pl.loop(0, steps // 2)
    def _(i):
        run(2 * i, s0_scr, peak0_scr, 2 * i + 1, s1_scr, peak1_scr)
        after = 2 * i + 2

        @pl.when((after < steps) & (lax.rem(after, parts) == 0))
        def _():
            for copy in copies_in(after // parts):
                copy.wait()

        run(2 * i + 1, s1_scr, peak1_scr, jnp.minimum(after, steps - 1), s0_scr, peak0_scr)

    for slot in range(slots):
        copy_out(steps - slots + slot).wait()
    for copy in copies_kv:
        copy.wait()


def attend(qt, k_own, v_own, x_oth, w_own, w_oth, bias, extra):
    heads, _, queries = qt.shape
    keys = 2 * queries
    sub, chunk, slots = 256, 512, 4
    per_head = jax.ShapeDtypeStruct(k_own.shape, BF)
    return pl.pallas_call(
        functools.partial(attend_kernel, sub, chunk),
        out_shape=(
            jax.ShapeDtypeStruct((heads, keys, queries), BF),
            jax.ShapeDtypeStruct((heads, HD, queries), F32),
            jax.ShapeDtypeStruct((heads, 1, queries), F32),
            per_head,
            per_head,
        ),
        in_specs=[HBM] * 3 + [VMEM] * 5,
        out_specs=(HBM, VMEM, VMEM, HBM, HBM),
        scratch_shapes=[
            pltpu.VMEM(qt.shape, BF),
            pltpu.VMEM(k_own.shape, BF),
            pltpu.VMEM(k_own.shape, BF),
            pltpu.VMEM(k_own.shape, BF),
            pltpu.VMEM(k_own.shape, BF),
            pltpu.VMEM((keys, chunk), F32),
            pltpu.VMEM((keys, chunk), F32),
            pltpu.VMEM((8, chunk), F32),
            pltpu.VMEM((8, chunk), F32),
            pltpu.VMEM((1, chunk), F32),
            pltpu.VMEM((LANES, chunk), F32),
            pltpu.VMEM((slots, keys, chunk), BF),
            pltpu.SemaphoreType.DMA((slots,)),
            pltpu.SemaphoreType.DMA((heads, 3)),
            pltpu.SemaphoreType.DMA((2,)),
        ],
        compiler_params=params(),
        cost_estimate=cost(heads * keys * queries * 512, 2 * heads * keys * queries),
        name="attend",
    )(qt, k_own, v_own, x_oth, w_own, w_oth, bias, extra)


def normalize(values):
    mean = jnp.mean(values, axis=-1, keepdims=True)
    centered = values - mean
    inverse = lax.rsqrt(jnp.mean(centered * centered, axis=-1, keepdims=True) + NORM_EPS)
    return centered * inverse, inverse


def norm_back(e, normed, inverse):
    return inverse * (
        e - jnp.mean(e, axis=-1, keepdims=True) - normed * jnp.mean(e * normed, axis=-1, keepdims=True)
    )


def middle_kernel(
    sub, x_ref, cot_ref, ot_ref, linv_ref, w_own_ref, w_oth_ref, vec_ref,
    act_ref, res_ref, dot_ref, dnat_ref, own_ref, oth_ref, small_ref,
    att_scr, w_out_ref, w_up_ref, w_down_ref, b_up_ref, gw_ref,
):
    block, width = x_ref.shape
    heads = width // HD
    shard = width // 2
    b_out, gain1, bias1, b_down, gain2, bias2 = (vec_ref[i : i + 1, :] for i in range(6))

    @pl.when(pl.program_id(0) == 0)
    def _():
        gw_ref[...] = jnp.zeros_like(gw_ref)
        small_ref[...] = jnp.zeros_like(small_ref)
        for side, ref in enumerate((w_own_ref, w_oth_ref)):
            mine = slice(side * shard, (side + 1) * shard)
            w_out_ref[mine, :] = ref[:shard, :]
            w_down_ref[mine, :] = ref[shard : 2 * shard, :]
            w_up_ref[:shard, mine] = ref[2 * shard : 3 * shard, :shard]
            w_up_ref[shard:, mine] = ref[2 * shard : 3 * shard, shard:]
            b_up_ref[:, mine] = ref[3 * shard : 3 * shard + 1, :shard].astype(F32)

    def col_sum(row, values):
        small_ref[row : row + 1, :] += jnp.sum(values, axis=0, keepdims=True)

    def chain(u):
        rows = slice(u * sub, (u + 1) * sub)
        for h in range(heads):
            att_scr[u, h * HD : (h + 1) * HD, :] = ot_ref[h, :, rows].astype(BF)
        branch = dot(att_scr[u], w_out_ref[...], 0, 0)
        yield
        n1, inv1 = normalize(x_ref[rows, :].astype(F32) + branch + b_out)
        first = n1 * gain1 + bias1
        first_low = first.astype(BF)
        yield
        pre = dot(first_low, w_up_ref[...], 1, 0) + b_up_ref[...]
        yield
        cdf = 0.5 * (1.0 + lax.erf(pre * 0.5**0.5))
        hidden = (pre * cdf).astype(BF)
        slope = cdf + pre * (0.3989422804014327 * jnp.exp(-0.5 * pre * pre))
        yield
        branch = dot(hidden, w_down_ref[...], 1, 0)
        yield
        n2, inv2 = normalize(first + branch + b_down)
        act_ref[rows, :] = (n2 * gain2 + bias2).astype(BF)
        cot = cot_ref[rows, :].astype(F32)
        two = norm_back(cot * gain2, n2, inv2)
        two_low = two.astype(BF)
        yield
        back = dot(two_low, w_down_ref[...], 1, 1)
        gw_ref[2] += dot(hidden, two_low, 0, 0)
        col_sum(3, two)
        col_sum(4, cot * n2)
        col_sum(5, cot)
        yield
        pre_grad = (back * slope).astype(BF)
        yield
        back = dot(pre_grad, w_up_ref[...], 1, 1)
        gw_ref[1] += dot(first_low, pre_grad, 0, 0)
        col_sum(6, pre_grad.astype(F32))
        yield
        one = two + back
        res = norm_back(one * gain1, n1, inv1)
        res_ref[rows, :] = res
        res_low = res.astype(BF)
        yield
        turned = dot(w_out_ref[...], res_low, 1, 1)
        gw_ref[0] += dot(att_scr[u], res_low, 1, 0)
        col_sum(1, one * n1)
        col_sum(2, one)
        col_sum(0, res)
        yield
        pick = lax.broadcasted_iota(jnp.int32, (HD, sub), 0)
        for h in range(heads):
            head = slice(h * HD, (h + 1) * HD)
            grad = (turned[head].astype(BF).astype(F32) * linv_ref[h, :, rows]).astype(BF)
            inner = -jnp.sum(grad.astype(F32) * ot_ref[h, :, rows], axis=0, keepdims=True)
            high = inner.astype(BF).astype(F32)
            dot_ref[h, :HD, rows] = grad
            dot_ref[h, HD:, rows] = jnp.where(pick == 0, high, jnp.where(pick == 1, inner - high, 0.0)).astype(BF)
            att_scr[u, head, :] = grad
        dnat_ref[rows, :] = att_scr[u].T
        yield

    for _ in zip(*(chain(u) for u in range(block // sub))):
        pass

    @pl.when(pl.program_id(0) == pl.num_programs(0) - 1)
    def _():
        for ref, mine in ((own_ref, slice(0, shard)), (oth_ref, slice(shard, width))):
            ref[:shard, :] = gw_ref[0, mine, :].astype(ref.dtype)
            ref[shard:width, :] = gw_ref[2, mine, :].astype(ref.dtype)
            ref[width:, :shard] = gw_ref[1, :shard, mine].astype(ref.dtype)
            ref[width:, shard:] = gw_ref[1, shard:, mine].astype(ref.dtype)


def middle(x, cot, ot, linv, w_own, w_oth, vectors):
    tokens, width = x.shape
    heads = width // HD
    block, sub = 512, 256
    whole = lambda *shape: pl.BlockSpec(shape, lambda i: (0,) * len(shape))
    rows = pl.BlockSpec((block, width), lambda i: (i, 0))
    columns = lambda n: pl.BlockSpec((heads, n, block), lambda i: (0, 0, i))
    square = pltpu.VMEM((width, width), BF)
    return pl.pallas_call(
        functools.partial(middle_kernel, sub),
        grid=(tokens // block,),
        out_shape=(
            jax.ShapeDtypeStruct((tokens, width), BF),
            jax.ShapeDtypeStruct((tokens, width), F32),
            jax.ShapeDtypeStruct((heads, LANES, tokens), BF),
            jax.ShapeDtypeStruct((tokens, width), BF),
            jax.ShapeDtypeStruct((3 * width // 2, width), F32),
            jax.ShapeDtypeStruct((3 * width // 2, width), BF),
            jax.ShapeDtypeStruct((8, width), F32),
        ),
        in_specs=[rows, rows, columns(HD), columns(1), whole(*w_own.shape), whole(*w_oth.shape), whole(*vectors.shape)],
        out_specs=(
            rows, rows, columns(LANES), rows,
            whole(3 * width // 2, width), whole(3 * width // 2, width), whole(8, width),
        ),
        scratch_shapes=[
            pltpu.VMEM((block // sub, width, sub), BF), square, square, square,
            pltpu.VMEM((1, width), F32), pltpu.VMEM((3, width, width), F32),
        ],
        compiler_params=params(),
        cost_estimate=cost(9 * tokens * width * width, 20 * tokens * width),
        name="middle",
    )(x, cot, ot, linv, w_own, w_oth, vectors)


def times_weights(grad, own_ref, oth_ref, third):
    shard = own_ref.shape[1] // 3
    mine = slice(third * shard, (third + 1) * shard)
    return dot(grad[:, :shard], own_ref[:, mine], 1, 1) + dot(grad[:, shard:], oth_ref[:, mine], 1, 1)


def backward_kernel(sub, count, part, *refs):
    if part:
        (p_hbm, dot_hbm, dnat_hbm, q_hbm, k_hbm, v_hbm, x_hbm, own_hbm, oth_hbm,
         dq_ref, dx_ref, gw_ref,
         dot_ref, dnat_ref, q_ref, k_ref, v_ref, x_ref, own_ref, oth_ref,
         dk_ref, dv_ref, acc_scr, p_scr, sem, pair_sem, last_sem) = refs
        more = ((own_hbm, own_ref), (oth_hbm, oth_ref))
    else:
        (p_hbm, dot_hbm, dnat_hbm, q_hbm, k_hbm, v_hbm, x_hbm, dq_hbm, gw_hbm,
         pack_ref, bias_ref, dq_out, dk_ref, dv_ref,
         dot_ref, dnat_ref, q_ref, k_ref, v_ref, x_ref, before_ref, gw_ref, dq_ref,
         acc_scr, p_scr, sem, pair_sem, last_sem) = refs
        more = ((dq_hbm, before_ref), (gw_hbm, gw_ref))
    heads, _, queries = dot_ref.shape
    keys = k_ref.shape[1]
    width = heads * HD
    shard = width // 2
    block = sub * count
    blocks = keys // block
    slots = p_scr.shape[0]
    total = heads // 2 * blocks
    low = lax.broadcasted_iota(jnp.int32, (sub, LANES), 1) < HD

    def copy_in(step):
        rows = pl.ds(pl.multiple_of(part * keys + lax.rem(step, blocks) * block, block), block)
        pair = pl.ds(step // blocks * 2, 2)
        slot = lax.rem(step, slots)
        return pltpu.make_async_copy(p_hbm.at[pair, rows, :], p_scr.at[slot], sem.at[slot])

    def pair_copies(p):
        pair = pl.ds(2 * p, 2)
        lanes = pl.ds(pl.multiple_of(p * LANES, LANES), LANES)
        by_head = ((dot_hbm, dot_ref), (k_hbm, k_ref), (v_hbm, v_ref))
        by_lane = ((dnat_hbm, dnat_ref), (q_hbm, q_ref))
        return [
            pltpu.make_async_copy(src.at[pair], dst.at[pair], pair_sem.at[p, n]) for n, (src, dst) in enumerate(by_head)
        ] + [
            pltpu.make_async_copy(src.at[:, lanes], dst.at[:, lanes], pair_sem.at[p, 3 + n])
            for n, (src, dst) in enumerate(by_lane)
        ]

    last = ((x_hbm, x_ref),) + more
    last_copies = [pltpu.make_async_copy(src, dst, last_sem.at[n]) for n, (src, dst) in enumerate(last)]

    for copy in pair_copies(0):
        copy.start()
    for step in range(slots - 1):
        copy_in(step).start()
    for p in range(1, heads // 2):
        for copy in pair_copies(p):
            copy.start()
    for copy in last_copies:
        copy.start()

    @pl.loop(0, heads // 2)
    def _(p):
        lanes = pl.ds(pl.multiple_of(p * LANES, LANES), LANES)
        for copy in pair_copies(p):
            copy.wait()
        acc_scr[...] = jnp.zeros_like(acc_scr)

        @pl.loop(0, blocks)
        def _(j):
            step = p * blocks + j
            slot = lax.rem(step, slots)
            copy_in(step).wait()

            @pl.when(step + slots - 1 < total)
            def _():
                copy_in(step + slots - 1).start()

            acc = [0.0, 0.0]
            for u in range(count):
                here = pl.ds(pl.multiple_of(j * block + u * sub, sub), sub)
                dks, dvs = [], []
                for side in range(2):
                    h = 2 * p + side
                    prob = p_scr[slot, side, u * sub : (u + 1) * sub, :]
                    slope = dot(v_ref[h, here, :], dot_ref[h], 1, 0)
                    dvs.append(dot(prob, dnat_ref[:, lanes], 1, 0))
                    ds = (prob.astype(F32) * slope).astype(BF)
                    dks.append(dot(ds, q_ref[:, lanes], 1, 0))
                    acc[side] = acc[side] + dot(k_ref[h, here, :], ds, 0, 0)
                dk_ref[here, lanes] = (jnp.where(low, dks[0], dks[1]) * HD**-0.5).astype(BF)
                dv_ref[here, lanes] = jnp.where(low, dvs[0], dvs[1]).astype(BF)
            for side in range(2):
                acc_scr[side] += acc[side]

        for side in range(2):
            dq_ref[pl.ds(pl.multiple_of((2 * p + side) * HD, HD), HD), :] = acc_scr[side, :HD, :]

    for copy in last_copies:
        copy.wait()
    if part:
        gw_ref[...] = jnp.zeros_like(gw_ref)
    else:
        bias_ref[...] = jnp.zeros_like(bias_ref)

    @pl.loop(0, keys // sub)
    def _(i):
        rows = pl.ds(pl.multiple_of(i * sub, sub), sub)
        x, dk, dv = x_ref[rows, :], dk_ref[rows, :], dv_ref[rows, :]
        gw_ref[0] += dot(x, dk, 0, 0)
        gw_ref[1] += dot(x, dv, 0, 0)
        if part:
            dx_ref[rows, :] = (times_weights(dk, own_ref, oth_ref, 1) + times_weights(dv, own_ref, oth_ref, 2)).astype(BF)
            gw_ref[2, 0:1, :] += jnp.sum(dv.astype(F32), axis=0, keepdims=True)
        else:
            dq = ((before_ref[:, rows] + dq_ref[:, rows]) * HD**-0.5).astype(BF).T
            dq_out[rows, :] = dq
            gw_ref[2] = jnp.where(i == 0, 0.0, gw_ref[2]) + dot(x, dq, 0, 0)
            bias_ref[0:1, :] += jnp.sum(dq.astype(F32), axis=0, keepdims=True)
            bias_ref[1:2, :] += jnp.sum(dv.astype(F32), axis=0, keepdims=True)

    if not part:
        for cut in range(2):
            for third in range(3):
                row = third * shard + cut * (shard // 2)
                core, at = row // (3 * shard // 2), row % (3 * shard // 2)
                to = slice(at, at + shard // 2)
                grad = gw_ref.at[(2, 0, 1)[third]]
                for side in range(2):
                    mine = slice(side * shard, (side + 1) * shard)
                    for place, start in ((slice(0, shard), 0), (slice(shard, width), shard)):
                        top = slice(start + cut * (shard // 2), start + (cut + 1) * (shard // 2))
                        pack_ref[core, side, to, place] = grad[top, mine].astype(BF)


def attend_backward(part, probs, dot_turned, dnat, q, k, v, x, *more):
    heads, keys, queries = probs.shape
    width = heads * HD
    sub, count, slots = 256, 2, 4
    sums = jax.ShapeDtypeStruct((3, width, width), F32)
    turned = jax.ShapeDtypeStruct((width, queries), F32)
    grad = jax.ShapeDtypeStruct((queries, width), BF)
    inputs = (dot_turned, dnat, q, k, v, x) + more
    held = [pltpu.VMEM(a.shape, a.dtype) for a in inputs]
    if part:
        out_shape = (turned, grad, sums)
        held += [pltpu.VMEM(grad.shape, BF)] * 2
    else:
        out_shape = (
            jax.ShapeDtypeStruct((2, 2, 3 * width // 4, width), BF),
            jax.ShapeDtypeStruct((2, width), F32),
            grad,
            grad,
            grad,
        )
        held = held[:6] + [pltpu.VMEM(turned.shape, F32), pltpu.VMEM(sums.shape, F32), pltpu.VMEM(turned.shape, F32)]
    return pl.pallas_call(
        functools.partial(backward_kernel, sub, count, part),
        out_shape=out_shape,
        in_specs=[HBM] * (1 + len(inputs)),
        out_specs=(VMEM,) * len(out_shape),
        scratch_shapes=held
        + [
            pltpu.VMEM((2, LANES, queries), F32),
            pltpu.VMEM((slots, 2, sub * count, queries), BF),
            pltpu.SemaphoreType.DMA((slots,)),
            pltpu.SemaphoreType.DMA((heads // 2, 5)),
            pltpu.SemaphoreType.DMA((1 + len(more),)),
        ],
        compiler_params=params(),
        cost_estimate=cost(heads * keys * queries * 512, heads * keys * queries),
        name="attend_back_own" if not part else "attend_back_other",
    )(probs, *inputs)


def input_kernel(res_ref, got_ref, dq_ref, dk_ref, dv_ref, own_ref, oth_ref, dx_ref):
    dx = res_ref[...] + got_ref[...].astype(F32)
    for third, ref in enumerate((dq_ref, dk_ref, dv_ref)):
        dx = dx + times_weights(ref[...], own_ref, oth_ref, third)
    dx_ref[...] = dx


def input_gradient(res, got, dq, dk, dv, w_own, w_oth):
    tokens, width = res.shape
    rows = pl.BlockSpec((256, width), lambda i: (i, 0))
    whole = pl.BlockSpec(w_own.shape, lambda i: (0, 0))
    return pl.pallas_call(
        input_kernel,
        grid=(tokens // 256,),
        out_shape=jax.ShapeDtypeStruct((tokens, width), F32),
        in_specs=[rows] * 5 + [whole] * 2,
        out_specs=rows,
        compiler_params=params(),
        cost_estimate=cost(3 * tokens * width * width, 16 * tokens * width),
        name="input_gradient",
    )(res, got, dq, dk, dv, w_own, w_oth)


def two_halves(values):
    high = values.astype(BF)
    return jnp.concatenate([high, (values - high.astype(F32)).astype(BF)], axis=0)


def one_value(halves):
    return halves[:8].astype(F32) + halves[8:].astype(F32)


def take(values, which):
    return lax.dynamic_index_in_dim(values, which, 0, False)


def in_order(mine, theirs, which):
    return jnp.concatenate([jnp.where(which == 0, mine, theirs), jnp.where(which == 0, theirs, mine)])


def sum_gradients(packed, small_own, small_oth, mid, devices):
    index = lax.axis_index("dp")
    core, near = lax.rem(index, 2), lax.rem(index // 2, 2)
    rows = packed.shape[2]

    def across(values, bit):
        return lax.ppermute(values, "dp", [(i, i ^ bit) for i in range(devices)])

    own_two, oth_two = two_halves(small_own), two_halves(small_oth)
    sent = jnp.concatenate([take(packed, 1 - core).reshape(2 * rows, -1), own_two, oth_two])
    got = across(sent, 1)
    kept = take(packed, core).reshape(2 * rows, -1).astype(F32) + got[: 2 * rows].astype(F32)
    small_own = one_value(own_two) + one_value(got[2 * rows : 2 * rows + 16])
    small_oth = one_value(oth_two) + one_value(got[2 * rows + 16 :])
    halves = mid.reshape(2, rows // 2, -1)
    mid = take(halves, core) + across(take(halves, 1 - core).astype(BF), 1).astype(F32)

    own_two, oth_two = two_halves(small_own), two_halves(small_oth)
    got = lax.ppermute(jnp.concatenate([kept[rows:].astype(BF), oth_two]), "tensor", [(0, 1), (1, 0)])
    kept = kept[:rows] + got[:rows].astype(F32)
    small = one_value(own_two) + one_value(got[rows:])

    halves = kept.reshape(2, rows // 2, -1)
    two = two_halves(small)
    got = across(jnp.concatenate([take(halves, 1 - near).astype(BF), two]), 2)
    kept = take(halves, near) + got[: rows // 2].astype(F32)
    small = one_value(two) + one_value(got[rows // 2 :])

    bit = 4
    while bit < devices:
        low = mid.astype(BF)
        mid = low.astype(F32) + across(low, bit).astype(F32)
        sent = jnp.concatenate([kept.astype(BF), two_halves(small)])
        got = across(sent, bit)
        kept = sent[: rows // 2].astype(F32) + got[: rows // 2].astype(F32)
        small = one_value(sent[rows // 2 :]) + one_value(got[rows // 2 :])
        bit *= 2

    mid = mid.astype(BF)
    mid = in_order(mid, across(mid, 1), core)
    mid = in_order(mid, across(mid, 2), near)
    kept = kept.astype(BF)
    kept = in_order(kept, across(kept, 2), near)
    kept = in_order(kept, across(kept, 1), core)
    return kept.astype(F32), small, mid.astype(F32)


def mask_columns(known, lengths):
    positions = jnp.arange(known.shape[0], dtype=jnp.int32)
    ends = jnp.cumsum(lengths)
    starts = ends - lengths
    inside = (positions[:, None] >= starts[None, :]) & (positions[:, None] < ends[None, :])
    opening = jnp.any((positions[:, None] == starts[None, :]) & (lengths[None, :] > 0), axis=1)
    dead = ~((known > 0) | opening)
    slots = lengths.shape[0]
    keys = jnp.concatenate([inside, dead[:, None]], axis=1).astype(F32)
    keys = jnp.pad(keys, ((0, 0), (HD, LANES - HD - slots - 1))).astype(BF)
    queries = jnp.where(jnp.pad(inside, ((0, 0), (0, 1))), 0.0, -MASK_BIG)
    queries = jnp.pad(queries, ((0, 0), (0, HD - slots - 1))).T.astype(BF)
    return keys, queries


def local(
    devices, layer_input, gene_known, cell_genes, w_qkv, bias_qv, w_out, b_out, ln1_gain, ln1_bias,
    w_up, b_up, w_down, b_down, ln2_gain, ln2_bias, cotangent,
):
    tokens, width = layer_input.shape
    shard = w_qkv.shape[2]
    side, index = lax.axis_index("tensor"), lax.axis_index("dp")
    core, near = lax.rem(index, 2), lax.rem(index // 2, 2)

    def swapped(values):
        return lax.ppermute(values, "tensor", [(0, 1), (1, 0)])

    def across(values, bit):
        return lax.ppermute(values, "dp", [(i, i ^ bit) for i in range(devices)])

    w_own = w_qkv.reshape(width, 3 * shard)
    quarter = width // 4
    bias_row = jnp.pad(bias_qv.reshape(1, 2 * shard), ((0, 15), (0, shard)))
    sent = jnp.concatenate([lax.dynamic_slice_in_dim(w_own, (2 * core + near) * quarter, quarter, 0), bias_row])
    got = swapped(sent)
    x_oth = swapped(layer_input)
    piece = got[:quarter]
    piece = in_order(piece, across(piece, 2), near)
    w_oth = in_order(piece, across(piece, 1), core)
    bias_oth = got[quarter, : 2 * shard].reshape(2, shard)
    bias = jnp.concatenate([bias_qv, bias_oth], axis=1).astype(F32)

    key_cols, query_rows = mask_columns(gene_known, cell_genes[0])
    key_own = lax.dynamic_slice_in_dim(key_cols, side * tokens, tokens, 0)
    key_oth = lax.dynamic_slice_in_dim(key_cols, (1 - side) * tokens, tokens, 0)
    query_own = lax.dynamic_slice_in_dim(query_rows, side * tokens, tokens, 1)
    b_up_row = jnp.pad(b_up[None], ((0, 15), (0, shard)))
    mid_w = jnp.concatenate([w_out, w_down, jnp.concatenate([w_up[:shard], w_up[shard:]], axis=1), b_up_row])
    vectors = jnp.stack([b_out, ln1_gain, ln1_bias, b_down, ln2_gain, ln2_bias, b_out, b_out])

    k_own, v_own, qt, q = project(layer_input, w_own, w_oth, bias, key_own, query_own)
    x_oth, k_own, mid_w = lax.optimization_barrier((x_oth, k_own, mid_w))
    mid_w_oth = swapped(mid_w)
    probs, ot, linv, k_oth, v_oth = attend(qt, k_own, v_own, x_oth, w_own, w_oth, bias, key_oth)
    activations, res, dot_turned, dnat, mid_own, mid_oth, small = middle(
        layer_input, cotangent, ot, linv, mid_w, mid_w_oth, vectors
    )
    mid_got = swapped(mid_oth)
    dq, dx_oth, sums = attend_backward(1, probs, dot_turned, dnat, q, k_oth, v_oth, x_oth, w_own, w_oth)
    mid_got, dq = lax.optimization_barrier((mid_got, dq))
    mid = (mid_own + mid_got.astype(F32)).reshape(2, 3 * shard // 2, width)
    mid_got = across(take(mid, 1 - near).astype(BF), 2)
    dx_got = swapped(dx_oth)
    packed, bias_grad, dq, dk, dv = attend_backward(
        0, probs, dot_turned, dnat, q, k_own, v_own, layer_input, dq, sums
    )
    mid_got, dx_got, packed = lax.optimization_barrier((mid_got, dx_got, packed))
    mid = take(mid, near) + mid_got.astype(F32)
    input_grad = input_gradient(res, dx_got, dq, dk, dv, w_own, w_oth)
    values_grad = bias_grad[1:2] + sums[2, 0:1]

    def small_rows(mine):
        b_up_row = jnp.pad(small[6:7, mine], ((0, 0), (0, shard)))
        bias_row = jnp.concatenate([bias_grad[0:1, mine], values_grad[:, mine]], axis=1)
        return jnp.concatenate([small[:6], b_up_row, bias_row])

    qkv, small, mid = sum_gradients(
        packed, small_rows(slice(0, shard)), small_rows(slice(shard, width)), mid, devices
    )
    qkv_g = qkv.reshape(3, shard, 2, shard).transpose(2, 1, 0, 3).reshape(width, 3, shard)
    up_g = jnp.concatenate([mid[width:, :shard], mid[width:, shard:]])
    return (
        activations, input_grad, qkv_g, small[7].reshape(2, shard), mid[:shard], small[0], small[1], small[2],
        up_g, small[6, :shard], mid[shard:width], small[3], small[4], small[5],
    )


def solution(mesh):
    placed = (
        P(("dp", "tensor"), None),
        P("dp"),
        P("dp", None),
        P(None, None, "tensor"),
        P(None, "tensor"),
        P("tensor", None),
        P(),
        P(),
        P(),
        P(None, "tensor"),
        P("tensor"),
        P("tensor", None),
        P(),
        P(),
        P(),
        P(("dp", "tensor"), None),
    )
    return jax.shard_map(
        functools.partial(local, mesh.shape["dp"]),
        mesh=mesh,
        in_specs=placed,
        out_specs=(
            P(("dp", "tensor"), None),
            P(("dp", "tensor"), None),
            P(None, None, "tensor"),
            P(None, "tensor"),
            P("tensor", None),
            P(),
            P(),
            P(),
            P(None, "tensor"),
            P("tensor"),
            P("tensor", None),
            P(),
            P(),
            P(),
        ),
        check_vma=False,
    )
```

```python
import functools

import jax
import jax.numpy as jnp
from jax import lax
from jax.experimental import pallas as pl
from jax.experimental.pallas import tpu as pltpu
from jax.sharding import PartitionSpec as P

HD = 64
LANES = 128
NORM_EPS = 1e-05
MASK_BIG = 2.0**100
LOG2E = 1.4426950408889634
VMEM_BYTES = 58 * 2**20
BF = jnp.bfloat16
F32 = jnp.float32
VMEM = pl.BlockSpec(memory_space=pltpu.VMEM)
HBM = pl.BlockSpec(memory_space=pl.ANY)


def dot(left, right, left_dim, right_dim):
    return lax.dot_general(
        left, right, (((left_dim,), (right_dim,)), ((), ())), preferred_element_type=F32
    )


def params():
    return pltpu.CompilerParams(vmem_limit_bytes=VMEM_BYTES)


def cost(macs, moved):
    return pl.CostEstimate(flops=2 * macs, bytes_accessed=moved, transcendentals=0)


def values_columns(rows):
    lane = lax.broadcasted_iota(jnp.int32, (rows, LANES), 1)
    return jnp.where((lane == HD) | (lane == HD + 1), 1.0, 0.0)


def key_value_block(x, w_refs, bias_ref, extra_k, k_ref, v_ref, rows):
    shard = w_refs[0].shape[2]
    extra_k = extra_k.astype(F32)
    extra_v = values_columns(x.shape[0])
    low = lax.broadcasted_iota(jnp.int32, extra_k.shape, 1) < HD
    for side, w_ref in enumerate(w_refs):
        mine = slice(side * shard, (side + 1) * shard)
        keys = dot(x, w_ref[1], 1, 0)
        values = dot(x, w_ref[2], 1, 0) + bias_ref[1:2, mine]
        for i in range(shard // HD):
            pair = slice((i // 2) * LANES, (i // 2 + 1) * LANES)
            k_pair, v_pair = keys[:, pair], values[:, pair]
            if i % 2:
                k_pair, v_pair = pltpu.roll(k_pair, HD, 1), pltpu.roll(v_pair, HD, 1)
            h = side * (shard // HD) + i
            k_ref[h, rows, :] = jnp.where(low, k_pair, extra_k).astype(BF)
            v_ref[h, rows, :] = jnp.where(low, v_pair, extra_v).astype(BF)


def project_kernel(x_ref, own_ref, oth_ref, bias_ref, extra_k_ref, extra_q_ref, k_ref, v_ref, qt_ref, q_ref):
    x = x_ref[...]
    shard = own_ref.shape[2]
    key_value_block(x, (own_ref, oth_ref), bias_ref, extra_k_ref[...], k_ref, v_ref, slice(None))
    for side, w_ref in enumerate((own_ref, oth_ref)):
        mine = slice(side * shard, (side + 1) * shard)
        q = (dot(x, w_ref[0], 1, 0) + bias_ref[0:1, mine]).astype(BF)
        q_ref[:, mine] = q
        turned = q.T
        for i in range(shard // HD):
            h = side * (shard // HD) + i
            qt_ref[h, :HD, :] = turned[i * HD : (i + 1) * HD, :]
            qt_ref[h, HD:, :] = extra_q_ref[...]


def project(x, w_own, w_oth, bias, extra_k, extra_q):
    tokens, width = x.shape
    heads = width // HD
    block = 256
    whole = lambda *shape: pl.BlockSpec(shape, lambda i: (0,) * len(shape))
    per_head = pl.BlockSpec((heads, block, LANES), lambda i: (0, i, 0))
    return pl.pallas_call(
        project_kernel,
        grid=(tokens // block,),
        out_shape=(
            jax.ShapeDtypeStruct((heads, tokens, LANES), BF),
            jax.ShapeDtypeStruct((heads, tokens, LANES), BF),
            jax.ShapeDtypeStruct((heads, LANES, tokens), BF),
            jax.ShapeDtypeStruct((tokens, width), BF),
        ),
        in_specs=[
            pl.BlockSpec((block, width), lambda i: (i, 0)),
            whole(*w_own.shape),
            whole(*w_oth.shape),
            whole(*bias.shape),
            pl.BlockSpec((block, LANES), lambda i: (i, 0)),
            pl.BlockSpec((HD, block), lambda i: (0, i)),
        ],
        out_specs=(
            per_head,
            per_head,
            pl.BlockSpec((heads, LANES, block), lambda i: (0, 0, i)),
            pl.BlockSpec((block, width), lambda i: (i, 0)),
        ),
        compiler_params=params(),
        cost_estimate=cost(3 * tokens * width * width, 12 * tokens * width),
        name="project",
    )(x, w_own, w_oth, bias, extra_k, extra_q)


def attend_kernel(
    sub, chunk, qt_hbm, k_hbm, v_hbm, x_ref, own_ref, oth_ref, bias_ref, extra_ref,
    p_hbm, ot_ref, linv_ref, k_oth_hbm, v_oth_hbm,
    qt_ref, k0_ref, k1_ref, v0_ref, v1_ref,
    s0_scr, s1_scr, peak0_scr, peak1_scr, row_scr, acc_scr, p_scr, sem, in_sem, out_sem,
):
    heads, _, queries = qt_ref.shape
    half = k0_ref.shape[1]
    parts = queries // chunk
    steps = heads * parts
    slots = p_scr.shape[0]

    def copies_in(h):
        return [
            pltpu.make_async_copy(src.at[h], dst.at[h], in_sem.at[h, n])
            for n, (src, dst) in enumerate(((qt_hbm, qt_ref), (k_hbm, k0_ref), (v_hbm, v0_ref)))
        ]

    for h in range(heads):
        for copy in copies_in(h):
            copy.start()

    @pl.loop(0, half // sub)
    def _(i):
        rows = pl.ds(pl.multiple_of(i * sub, sub), sub)
        key_value_block(x_ref[rows, :], (own_ref, oth_ref), bias_ref, extra_ref[rows, :], k1_ref, v1_ref, rows)

    copies_kv = [
        pltpu.make_async_copy(k1_ref, k_oth_hbm, out_sem.at[0]),
        pltpu.make_async_copy(v1_ref, v_oth_hbm, out_sem.at[1]),
    ]
    for copy in copies_kv:
        copy.start()

    def columns(step):
        return pl.ds(pl.multiple_of(lax.rem(step, parts) * chunk, chunk), chunk)

    def copy_out(step):
        slot = lax.rem(step, slots)
        return pltpu.make_async_copy(p_scr.at[slot], p_hbm.at[step // parts, :, columns(step)], sem.at[slot])

    def blocks(first, second):
        for part, ref in enumerate((first, second)):
            for u in range(half // sub):
                yield ref, slice(u * sub, (u + 1) * sub), slice(part * half + u * sub, part * half + (u + 1) * sub)

    def scores(step, s_ref, peak, keys, rows, to):
        s = dot(keys[step // parts, rows, :], qt_ref[step // parts, :, columns(step)], 1, 0)
        s_ref[to, :] = s
        return jnp.maximum(peak, jnp.max(s.reshape(sub // 8, 8, chunk), axis=0))

    def mix(step, s_ref, values, rows, to):
        p = jnp.exp2((s_ref[to, :] - row_scr[...]) * (LOG2E * HD**-0.5)).astype(BF)
        p_scr[lax.rem(step, slots), to, :] = p
        return dot(values[step // parts, rows, :], p, 0, 0)

    def run(step, s_ref, peak_ref, after, s_after, peak_after):
        row_scr[...] = jnp.max(peak_ref[...], axis=0, keepdims=True)

        @pl.when(step >= slots)
        def _():
            copy_out(step - slots).wait()

        peak = jnp.full((8, chunk), -jnp.inf, F32)
        acc = jnp.zeros((LANES, chunk), F32)
        for (k_ref, rows, to), (v_ref, _, _) in zip(blocks(k0_ref, k1_ref), blocks(v0_ref, v1_ref)):
            peak = scores(after, s_after, peak, k_ref, rows, to)
            acc = acc + mix(step, s_ref, v_ref, rows, to)
        peak_after[...] = peak
        acc_scr[...] = acc
        copy_out(step).start()
        inverse = 1.0 / acc_scr[HD : HD + 1, :]
        linv_ref[step // parts, :, columns(step)] = inverse
        ot_ref[step // parts, :, columns(step)] = acc_scr[:HD, :] * inverse

    for copy in copies_in(0):
        copy.wait()
    peak = jnp.full((8, chunk), -jnp.inf, F32)
    for k_ref, rows, to in blocks(k0_ref, k1_ref):
        peak = scores(0, s0_scr, peak, k_ref, rows, to)
    peak0_scr[...] = peak

    @pl.loop(0, steps // 2)
    def _(i):
        run(2 * i, s0_scr, peak0_scr, 2 * i + 1, s1_scr, peak1_scr)
        after = 2 * i + 2

        @pl.when((after < steps) & (lax.rem(after, parts) == 0))
        def _():
            for copy in copies_in(after // parts):
                copy.wait()

        run(2 * i + 1, s1_scr, peak1_scr, jnp.minimum(after, steps - 1), s0_scr, peak0_scr)

    for slot in range(slots):
        copy_out(steps - slots + slot).wait()
    for copy in copies_kv:
        copy.wait()


def attend(qt, k_own, v_own, x_oth, w_own, w_oth, bias, extra):
    heads, _, queries = qt.shape
    keys = 2 * queries
    sub, chunk, slots = 256, 512, 4
    per_head = jax.ShapeDtypeStruct(k_own.shape, BF)
    return pl.pallas_call(
        functools.partial(attend_kernel, sub, chunk),
        out_shape=(
            jax.ShapeDtypeStruct((heads, keys, queries), BF),
            jax.ShapeDtypeStruct((heads, HD, queries), F32),
            jax.ShapeDtypeStruct((heads, 1, queries), F32),
            per_head,
            per_head,
        ),
        in_specs=[HBM] * 3 + [VMEM] * 5,
        out_specs=(HBM, VMEM, VMEM, HBM, HBM),
        scratch_shapes=[
            pltpu.VMEM(qt.shape, BF),
            pltpu.VMEM(k_own.shape, BF),
            pltpu.VMEM(k_own.shape, BF),
            pltpu.VMEM(k_own.shape, BF),
            pltpu.VMEM(k_own.shape, BF),
            pltpu.VMEM((keys, chunk), F32),
            pltpu.VMEM((keys, chunk), F32),
            pltpu.VMEM((8, chunk), F32),
            pltpu.VMEM((8, chunk), F32),
            pltpu.VMEM((1, chunk), F32),
            pltpu.VMEM((LANES, chunk), F32),
            pltpu.VMEM((slots, keys, chunk), BF),
            pltpu.SemaphoreType.DMA((slots,)),
            pltpu.SemaphoreType.DMA((heads, 3)),
            pltpu.SemaphoreType.DMA((2,)),
        ],
        compiler_params=params(),
        cost_estimate=cost(heads * keys * queries * 512, 2 * heads * keys * queries),
        name="attend",
    )(qt, k_own, v_own, x_oth, w_own, w_oth, bias, extra)


def normalize(values):
    mean = jnp.mean(values, axis=-1, keepdims=True)
    centered = values - mean
    inverse = lax.rsqrt(jnp.mean(centered * centered, axis=-1, keepdims=True) + NORM_EPS)
    return centered * inverse, inverse


def norm_back(e, normed, inverse):
    return inverse * (
        e - jnp.mean(e, axis=-1, keepdims=True) - normed * jnp.mean(e * normed, axis=-1, keepdims=True)
    )


def middle_kernel(
    sub, x_ref, cot_ref, ot_ref, linv_ref, w_own_ref, w_oth_ref, vec_ref,
    act_ref, res_ref, dot_ref, dnat_ref, own_ref, oth_ref, small_ref,
    att_scr, w_out_ref, w_up_ref, w_down_ref, b_up_ref, gw_ref,
):
    block, width = x_ref.shape
    heads = width // HD
    shard = width // 2
    b_out, gain1, bias1, b_down, gain2, bias2 = (vec_ref[i : i + 1, :] for i in range(6))

    @pl.when(pl.program_id(0) == 0)
    def _():
        gw_ref[...] = jnp.zeros_like(gw_ref)
        small_ref[...] = jnp.zeros_like(small_ref)
        for side, ref in enumerate((w_own_ref, w_oth_ref)):
            mine = slice(side * shard, (side + 1) * shard)
            w_out_ref[mine, :] = ref[:shard, :]
            w_down_ref[mine, :] = ref[shard : 2 * shard, :]
            w_up_ref[:shard, mine] = ref[2 * shard : 3 * shard, :shard]
            w_up_ref[shard:, mine] = ref[2 * shard : 3 * shard, shard:]
            b_up_ref[:, mine] = ref[3 * shard : 3 * shard + 1, :shard].astype(F32)

    def col_sum(row, values):
        small_ref[row : row + 1, :] += jnp.sum(values, axis=0, keepdims=True)

    def chain(u):
        rows = slice(u * sub, (u + 1) * sub)
        for h in range(heads):
            att_scr[u, h * HD : (h + 1) * HD, :] = ot_ref[h, :, rows].astype(BF)
        branch = dot(att_scr[u], w_out_ref[...], 0, 0)
        yield
        n1, inv1 = normalize(x_ref[rows, :].astype(F32) + branch + b_out)
        first = n1 * gain1 + bias1
        first_low = first.astype(BF)
        yield
        pre = dot(first_low, w_up_ref[...], 1, 0) + b_up_ref[...]
        yield
        cdf = 0.5 * (1.0 + lax.erf(pre * 0.5**0.5))
        hidden = (pre * cdf).astype(BF)
        slope = cdf + pre * (0.3989422804014327 * jnp.exp(-0.5 * pre * pre))
        yield
        branch = dot(hidden, w_down_ref[...], 1, 0)
        yield
        n2, inv2 = normalize(first + branch + b_down)
        act_ref[rows, :] = (n2 * gain2 + bias2).astype(BF)
        cot = cot_ref[rows, :].astype(F32)
        two = norm_back(cot * gain2, n2, inv2)
        two_low = two.astype(BF)
        yield
        back = dot(two_low, w_down_ref[...], 1, 1)
        gw_ref[2] += dot(hidden, two_low, 0, 0)
        col_sum(3, two)
        col_sum(4, cot * n2)
        col_sum(5, cot)
        yield
        pre_grad = (back * slope).astype(BF)
        yield
        back = dot(pre_grad, w_up_ref[...], 1, 1)
        gw_ref[1] += dot(first_low, pre_grad, 0, 0)
        col_sum(6, pre_grad.astype(F32))
        yield
        one = two + back
        res = norm_back(one * gain1, n1, inv1)
        res_ref[rows, :] = res
        res_low = res.astype(BF)
        yield
        turned = dot(w_out_ref[...], res_low, 1, 1)
        gw_ref[0] += dot(att_scr[u], res_low, 1, 0)
        col_sum(1, one * n1)
        col_sum(2, one)
        col_sum(0, res)
        yield
        pick = lax.broadcasted_iota(jnp.int32, (HD, sub), 0)
        for h in range(heads):
            head = slice(h * HD, (h + 1) * HD)
            grad = (turned[head].astype(BF).astype(F32) * linv_ref[h, :, rows]).astype(BF)
            inner = -jnp.sum(grad.astype(F32) * ot_ref[h, :, rows], axis=0, keepdims=True)
            high = inner.astype(BF).astype(F32)
            dot_ref[h, :HD, rows] = grad
            dot_ref[h, HD:, rows] = jnp.where(pick == 0, high, jnp.where(pick == 1, inner - high, 0.0)).astype(BF)
            att_scr[u, head, :] = grad
        dnat_ref[rows, :] = att_scr[u].T
        yield

    for _ in zip(*(chain(u) for u in range(block // sub))):
        pass

    @pl.when(pl.program_id(0) == pl.num_programs(0) - 1)
    def _():
        for ref, mine in ((own_ref, slice(0, shard)), (oth_ref, slice(shard, width))):
            ref[:shard, :] = gw_ref[0, mine, :].astype(ref.dtype)
            ref[shard:width, :] = gw_ref[2, mine, :].astype(ref.dtype)
            ref[width:, :shard] = gw_ref[1, :shard, mine].astype(ref.dtype)
            ref[width:, shard:] = gw_ref[1, shard:, mine].astype(ref.dtype)


def middle(x, cot, ot, linv, w_own, w_oth, vectors):
    tokens, width = x.shape
    heads = width // HD
    block, sub = 512, 256
    whole = lambda *shape: pl.BlockSpec(shape, lambda i: (0,) * len(shape))
    rows = pl.BlockSpec((block, width), lambda i: (i, 0))
    columns = lambda n: pl.BlockSpec((heads, n, block), lambda i: (0, 0, i))
    square = pltpu.VMEM((width, width), BF)
    return pl.pallas_call(
        functools.partial(middle_kernel, sub),
        grid=(tokens // block,),
        out_shape=(
            jax.ShapeDtypeStruct((tokens, width), BF),
            jax.ShapeDtypeStruct((tokens, width), F32),
            jax.ShapeDtypeStruct((heads, LANES, tokens), BF),
            jax.ShapeDtypeStruct((tokens, width), BF),
            jax.ShapeDtypeStruct((3 * width // 2, width), F32),
            jax.ShapeDtypeStruct((3 * width // 2, width), BF),
            jax.ShapeDtypeStruct((8, width), F32),
        ),
        in_specs=[rows, rows, columns(HD), columns(1), whole(*w_own.shape), whole(*w_oth.shape), whole(*vectors.shape)],
        out_specs=(
            rows, rows, columns(LANES), rows,
            whole(3 * width // 2, width), whole(3 * width // 2, width), whole(8, width),
        ),
        scratch_shapes=[
            pltpu.VMEM((block // sub, width, sub), BF), square, square, square,
            pltpu.VMEM((1, width), F32), pltpu.VMEM((3, width, width), F32),
        ],
        compiler_params=params(),
        cost_estimate=cost(9 * tokens * width * width, 20 * tokens * width),
        name="middle",
    )(x, cot, ot, linv, w_own, w_oth, vectors)


def times_weights(grad, own_ref, oth_ref, third):
    shard = own_ref.shape[2]
    return dot(grad[:, :shard], own_ref[third], 1, 1) + dot(grad[:, shard:], oth_ref[third], 1, 1)


def backward_kernel(sub, count, part, *refs):
    if part:
        (p_hbm, dot_hbm, dnat_hbm, q_hbm, k_hbm, v_hbm, x_hbm, own_hbm, oth_hbm,
         dq_hbm, dx_ref, gw_ref, bias_ref,
         dot_ref, dnat_ref, q_ref, k_ref, v_ref, x_ref, own_ref, oth_ref,
         dq_ref, dk_ref, dv_ref, acc_scr, p_scr, sem, pair_sem, last_sem, out_sem) = refs
        more = ((own_hbm, own_ref), (oth_hbm, oth_ref))
    else:
        (core_ref, small_ref, value_ref,
         p_hbm, dot_hbm, dnat_hbm, q_hbm, k_hbm, v_hbm, x_hbm, dq_hbm, gw_hbm,
         sent_ref, kept_ref, dq_out, dk_hbm, dv_hbm,
         dot_ref, dnat_ref, q_ref, k_ref, v_ref, x_ref, before_ref, gw_ref,
         dq_ref, dk_ref, dv_ref, gq_ref, bias_ref, acc_scr, p_scr, sem, pair_sem, last_sem, out_sem) = refs
        more = ((dq_hbm, before_ref), (gw_hbm, gw_ref))
    heads, _, queries = dot_ref.shape
    keys = k_ref.shape[1]
    width = heads * HD
    shard = width // 2
    block = sub * count
    blocks = keys // block
    slots = p_scr.shape[0]
    total = heads // 2 * blocks
    low = lax.broadcasted_iota(jnp.int32, (sub, LANES), 1) < HD

    def copy_in(step):
        rows = pl.ds(pl.multiple_of(part * keys + lax.rem(step, blocks) * block, block), block)
        pair = pl.ds(step // blocks * 2, 2)
        slot = lax.rem(step, slots)
        return pltpu.make_async_copy(p_hbm.at[pair, rows, :], p_scr.at[slot], sem.at[slot])

    def pair_copies(p):
        pair = pl.ds(2 * p, 2)
        lanes = pl.ds(pl.multiple_of(p * LANES, LANES), LANES)
        by_head = ((dot_hbm, dot_ref), (k_hbm, k_ref), (v_hbm, v_ref))
        by_lane = ((dnat_hbm, dnat_ref), (q_hbm, q_ref))
        return [
            pltpu.make_async_copy(src.at[pair], dst.at[pair], pair_sem.at[p, n]) for n, (src, dst) in enumerate(by_head)
        ] + [
            pltpu.make_async_copy(src.at[:, lanes], dst.at[:, lanes], pair_sem.at[p, 3 + n])
            for n, (src, dst) in enumerate(by_lane)
        ]

    last = ((x_hbm, x_ref),) + more

    def rows_out(p):
        rows = pl.ds(pl.multiple_of(p * 2 * HD, 2 * HD), 2 * HD)
        return pltpu.make_async_copy(dq_ref.at[rows, :], dq_hbm.at[rows, :], out_sem.at[p])

    last_copies = [pltpu.make_async_copy(src, dst, last_sem.at[n]) for n, (src, dst) in enumerate(last)]

    for copy in pair_copies(0):
        copy.start()
    for step in range(slots - 1):
        copy_in(step).start()

    @pl.loop(0, heads // 2)
    def _(p):
        lanes = pl.ds(pl.multiple_of(p * LANES, LANES), LANES)
        for copy in pair_copies(p):
            copy.wait()

        @pl.when(p + 1 < heads // 2)
        def _():
            for copy in pair_copies(p + 1):
                copy.start()

        @pl.when(p == 1)
        def _():
            for copy in last_copies:
                copy.start()

        acc_scr[...] = jnp.zeros_like(acc_scr)

        @pl.loop(0, blocks)
        def _(j):
            step = p * blocks + j
            slot = lax.rem(step, slots)
            copy_in(step).wait()

            @pl.when(step + slots - 1 < total)
            def _():
                copy_in(step + slots - 1).start()

            acc = [0.0, 0.0]
            for u in range(count):
                here = pl.ds(pl.multiple_of(j * block + u * sub, sub), sub)
                dks, dvs = [], []
                for side in range(2):
                    h = 2 * p + side
                    prob = p_scr[slot, side, u * sub : (u + 1) * sub, :]
                    slope = dot(v_ref[h, here, :], dot_ref[h], 1, 0)
                    dvs.append(dot(prob, dnat_ref[:, lanes], 1, 0))
                    ds = (prob.astype(F32) * slope).astype(BF)
                    dks.append(dot(ds, q_ref[:, lanes], 1, 0))
                    acc[side] = acc[side] + dot(k_ref[h, here, :], ds, 0, 0)
                dk_ref[here, lanes] = (jnp.where(low, dks[0], dks[1]) * HD**-0.5).astype(BF)
                dv_ref[here, lanes] = jnp.where(low, dvs[0], dvs[1]).astype(BF)
            for side in range(2):
                acc_scr[side] += acc[side]

        for side in range(2):
            dq_ref[pl.ds(pl.multiple_of((2 * p + side) * HD, HD), HD), :] = acc_scr[side, :HD, :]
        if part:
            rows_out(p).start()

    for copy in last_copies:
        copy.wait()
    bias_ref[...] = jnp.zeros_like(bias_ref)
    if part:
        gw_ref[...] = jnp.zeros_like(gw_ref)
        copies_out = [rows_out(p) for p in range(heads // 2)]
    else:
        gq_ref[...] = jnp.zeros_like(gq_ref)
        copies_out = [
            pltpu.make_async_copy(dk_ref, dk_hbm, out_sem.at[0]),
            pltpu.make_async_copy(dv_ref, dv_hbm, out_sem.at[1]),
        ]
        for copy in copies_out:
            copy.start()

    @pl.loop(0, keys // sub)
    def _(i):
        rows = pl.ds(pl.multiple_of(i * sub, sub), sub)
        x, dk, dv = x_ref[rows, :], dk_ref[rows, :], dv_ref[rows, :]
        gw_ref[0] += dot(x, dk, 0, 0)
        gw_ref[1] += dot(x, dv, 0, 0)
        bias_ref[1:2, :] += jnp.sum(dv.astype(F32), axis=0, keepdims=True)
        if part:
            dx_ref[rows, :] = (times_weights(dk, own_ref, oth_ref, 1) + times_weights(dv, own_ref, oth_ref, 2)).astype(BF)
        else:
            dq = ((before_ref[:, rows] + dq_ref[:, rows]) * HD**-0.5).astype(BF).T
            dq_out[rows, :] = dq
            gq_ref[...] += dot(x, dq, 0, 0)
            bias_ref[0:1, :] += jnp.sum(dq.astype(F32), axis=0, keepdims=True)

    if not part:
        first = core_ref[0] == 0
        bias_ref[1:2, :] += value_ref[1:2, :]
        cut = 3 * width // 2
        for side in range(2):
            mine = slice(side * shard, (side + 1) * shard)
            pieces = [gq_ref[:, mine], gw_ref[0, :, mine], gw_ref[1, :, mine]]
            blocks = [piece[at : at + shard, :].astype(BF) for piece in pieces for at in (0, shard)]
            for n in range(3):
                to = slice(side * cut + n * shard, side * cut + (n + 1) * shard)
                kept_ref[to, :] = jnp.where(first, blocks[n], blocks[3 + n])
                sent_ref[to, :] = jnp.where(first, blocks[3 + n], blocks[n])
            rows16 = [small_ref[:6, :shard], small_ref[6:7, mine], bias_ref[0:1, mine]]
            rows16 += [small_ref[:6, shard:], jnp.zeros((1, shard), F32), bias_ref[1:2, mine]]
            value = jnp.concatenate(rows16, axis=0)
            high = value.astype(BF)
            for n, half in enumerate((high, (value - high.astype(F32)).astype(BF))):
                to = slice(2 * cut + (2 * side + n) * 16, 2 * cut + (2 * side + n + 1) * 16)
                kept_ref[to, :] = half
                sent_ref[to, :] = half

    for copy in copies_out:
        copy.wait()


def attend_backward(part, first, probs, dot_turned, dnat, q, k, v, x, *more):
    heads, keys, queries = probs.shape
    width = heads * HD
    sub, count, slots = 256, 2, 4
    sums = jax.ShapeDtypeStruct((2, width, width), F32)
    turned = jax.ShapeDtypeStruct((width, queries), F32)
    grad = jax.ShapeDtypeStruct((queries, width), BF)
    inputs = (dot_turned, dnat, q, k, v, x) + more
    held = [pltpu.VMEM(a.shape, a.dtype) for a in inputs]
    held += [pltpu.VMEM(turned.shape, F32), pltpu.VMEM(grad.shape, BF), pltpu.VMEM(grad.shape, BF)]
    if part:
        out_shape = (turned, grad, sums, jax.ShapeDtypeStruct((2, width), F32))
        out_specs = (HBM, VMEM, VMEM, VMEM)
    else:
        payload = jax.ShapeDtypeStruct((3 * width + 64, width // 2), BF)
        out_shape = (payload, payload, grad, grad, grad)
        out_specs = (VMEM, VMEM, VMEM, HBM, HBM)
        held += [pltpu.VMEM((width, width), F32), pltpu.VMEM((2, width), F32)]
    first_specs = [pl.BlockSpec(memory_space=pltpu.SMEM), VMEM, VMEM][: len(first)]
    return pl.pallas_call(
        functools.partial(backward_kernel, sub, count, part),
        out_shape=out_shape,
        in_specs=first_specs + [HBM] * (1 + len(inputs)),
        out_specs=out_specs,
        scratch_shapes=held
        + [
            pltpu.VMEM((2, LANES, queries), F32),
            pltpu.VMEM((slots, 2, sub * count, queries), BF),
            pltpu.SemaphoreType.DMA((slots,)),
            pltpu.SemaphoreType.DMA((heads // 2, 5)),
            pltpu.SemaphoreType.DMA((1 + len(more),)),
            pltpu.SemaphoreType.DMA((heads // 2,)),
        ],
        compiler_params=params(),
        cost_estimate=cost(heads * keys * queries * 512, heads * keys * queries),
        name="attend_back_own" if not part else "attend_back_other",
    )(*first, probs, *inputs)


def input_kernel(res_ref, got_ref, dq_ref, dk_ref, dv_ref, own_ref, oth_ref, dx_ref):
    dx = res_ref[...] + got_ref[...].astype(F32)
    for third, ref in enumerate((dq_ref, dk_ref, dv_ref)):
        dx = dx + times_weights(ref[...], own_ref, oth_ref, third)
    dx_ref[...] = dx


def input_gradient(res, got, dq, dk, dv, w_own, w_oth):
    tokens, width = res.shape
    rows = pl.BlockSpec((256, width), lambda i: (i, 0))
    whole = pl.BlockSpec(w_own.shape, lambda i: (0, 0, 0))
    return pl.pallas_call(
        input_kernel,
        grid=(tokens // 256,),
        out_shape=jax.ShapeDtypeStruct((tokens, width), F32),
        in_specs=[rows] * 5 + [whole] * 2,
        out_specs=rows,
        compiler_params=params(),
        cost_estimate=cost(3 * tokens * width * width, 16 * tokens * width),
        name="input_gradient",
    )(res, got, dq, dk, dv, w_own, w_oth)


def after(values, *others):
    return lax.optimization_barrier((values,) + others)[0]


def two_halves(values):
    high = values.astype(BF)
    return jnp.concatenate([high, (values - high.astype(F32)).astype(BF)], axis=0)


def one_value(halves):
    rows = halves.shape[0] // 2
    return halves[:rows].astype(F32) + halves[rows:].astype(F32)


def take(values, which):
    return lax.dynamic_index_in_dim(values, which, 0, False)


def in_order(mine, theirs, which):
    return jnp.concatenate([jnp.where(which == 0, mine, theirs), jnp.where(which == 0, theirs, mine)])


def sum_gradients(sent, kept, mid, input_grad, devices):
    index = lax.axis_index("dp")
    core, near = lax.rem(index, 2), lax.rem(index // 2, 2)
    rows = (sent.shape[0] - 64) // 2

    def across(values, bit):
        return lax.ppermute(values, "dp", [(i, i ^ bit) for i in range(devices)])

    got = across(sent, 1)
    halves = mid.reshape(2, mid.shape[0] // 2, -1)
    mid_got = across(take(halves, 1 - core).astype(BF), 1)
    total = kept[: 2 * rows].astype(F32) + got[: 2 * rows].astype(F32)
    small_own = one_value(kept[2 * rows : 2 * rows + 32]) + one_value(got[2 * rows : 2 * rows + 32])
    small_oth = one_value(kept[2 * rows + 32 :]) + one_value(got[2 * rows + 32 :])
    mid = (take(halves, core) + mid_got.astype(F32)).astype(BF)
    oth_two = two_halves(small_oth)
    mid_got = across(after(mid, oth_two), 4)
    result = input_grad(got)

    own_two = two_halves(small_own)
    got = lax.ppermute(jnp.concatenate([total[rows:].astype(BF), oth_two]), "tensor", [(0, 1), (1, 0)])
    total = total[:rows] + got[:rows].astype(F32)
    small = one_value(own_two) + one_value(got[rows:])

    halves = total.reshape(2, rows // 2, -1)
    two = two_halves(small)
    got = across(jnp.concatenate([take(halves, 1 - near).astype(BF), two]), 2)
    total = take(halves, near) + got[: rows // 2].astype(F32)
    small = one_value(two) + one_value(got[rows // 2 :])

    bit = 4
    while bit < devices:
        sent = jnp.concatenate([total.astype(BF), two_halves(small)])
        mid = (mid.astype(F32) + mid_got.astype(F32)).astype(BF)
        if 2 * bit < devices:
            mid_got = across(mid, 2 * bit)
        got = across(sent, bit)
        total = sent[: rows // 2].astype(F32) + got[: rows // 2].astype(F32)
        small = one_value(sent[rows // 2 :]) + one_value(got[rows // 2 :])
        bit *= 2
    mid = in_order(mid, across(mid, 1), core)
    mid = in_order(after(mid, got), after(across(mid, 2), got), near)

    total = total.astype(BF)
    total = in_order(total, across(total, 2), near)
    total = in_order(total, across(total, 1), core)
    return total.astype(F32), small, mid.astype(F32), result


def mask_columns(known, lengths):
    positions = jnp.arange(known.shape[0], dtype=jnp.int32)
    ends = jnp.cumsum(lengths)
    starts = ends - lengths
    inside = (positions[:, None] >= starts[None, :]) & (positions[:, None] < ends[None, :])
    opening = jnp.any((positions[:, None] == starts[None, :]) & (lengths[None, :] > 0), axis=1)
    dead = ~((known > 0) | opening)
    slots = lengths.shape[0]
    keys = jnp.concatenate([inside, dead[:, None]], axis=1).astype(F32)
    keys = jnp.pad(keys, ((0, 0), (HD, LANES - HD - slots - 1))).astype(BF)
    queries = jnp.where(jnp.pad(inside, ((0, 0), (0, 1))), 0.0, -MASK_BIG)
    queries = jnp.pad(queries, ((0, 0), (0, HD - slots - 1))).T.astype(BF)
    return keys, queries


def local(
    devices, layer_input, gene_known, cell_genes, w_qkv, bias_qv, w_out, b_out, ln1_gain, ln1_bias,
    w_up, b_up, w_down, b_down, ln2_gain, ln2_bias, cotangent,
):
    tokens, width = layer_input.shape
    shard = w_qkv.shape[2]
    side, index = lax.axis_index("tensor"), lax.axis_index("dp")
    core, near = lax.rem(index, 2), lax.rem(index // 2, 2)

    def swapped(values):
        return lax.ppermute(values, "tensor", [(0, 1), (1, 0)])

    def across(values, bit):
        return lax.ppermute(values, "dp", [(i, i ^ bit) for i in range(devices)])

    w_own = w_qkv.transpose(1, 0, 2)
    quarter = 3 * width // 4
    mine = lax.dynamic_slice_in_dim(w_own.reshape(3 * width, shard), (2 * core + near) * quarter, quarter, 0)
    got = swapped(jnp.concatenate([mine, jnp.pad(bias_qv, ((0, 14), (0, 0)))]))
    x_oth = swapped(layer_input)
    piece = got[:quarter]
    piece = in_order(piece, across(piece, 2), near)
    w_oth = in_order(piece, across(piece, 1), core).reshape(3, width, shard)
    bias = jnp.concatenate([bias_qv, got[quarter : quarter + 2]], axis=1).astype(F32)

    key_cols, query_rows = mask_columns(gene_known, cell_genes[0])
    key_own = lax.dynamic_slice_in_dim(key_cols, side * tokens, tokens, 0)
    key_oth = lax.dynamic_slice_in_dim(key_cols, (1 - side) * tokens, tokens, 0)
    query_own = lax.dynamic_slice_in_dim(query_rows, side * tokens, tokens, 1)
    b_up_row = jnp.pad(b_up[None], ((0, 15), (0, shard)))
    mid_w = jnp.concatenate([w_out, w_down, jnp.concatenate([w_up[:shard], w_up[shard:]], axis=1), b_up_row])
    vectors = jnp.stack([b_out, ln1_gain, ln1_bias, b_down, ln2_gain, ln2_bias, b_out, b_out])

    k_own, v_own, qt, q = project(layer_input, w_own, w_oth, bias, key_own, query_own)
    x_oth, k_own, mid_w = lax.optimization_barrier((x_oth, k_own, mid_w))
    mid_w_oth = swapped(mid_w)
    probs, ot, linv, k_oth, v_oth = attend(qt, k_own, v_own, x_oth, w_own, w_oth, bias, key_oth)
    activations, res, dot_turned, dnat, mid_own, mid_oth, small = middle(
        layer_input, cotangent, ot, linv, mid_w, mid_w_oth, vectors
    )
    mid_got = swapped(mid_oth)
    dq, dx_oth, sums, value_grad = attend_backward(
        1, (), probs, dot_turned, dnat, q, k_oth, v_oth, x_oth, w_own, w_oth
    )
    mid_got, dq = lax.optimization_barrier((mid_got, dq))
    mid = (mid_own + mid_got.astype(F32)).reshape(2, 3 * shard // 2, width)
    mid_got = across(take(mid, 1 - near).astype(BF), 2)
    dx_got = swapped(dx_oth)
    sent, kept, dq, dk, dv = attend_backward(
        0, (core[None], small, value_grad), probs, dot_turned, dnat, q, k_own, v_own, layer_input, dq, sums
    )
    mid_got, dx_got, sent = lax.optimization_barrier((mid_got, dx_got, sent))
    mid = take(mid, near) + mid_got.astype(F32)

    def input_grad(token):
        return input_gradient(res, dx_got, after(dq, token), dk, dv, w_own, w_oth)

    qkv, small, mid, input_grad = sum_gradients(sent, kept, mid, input_grad, devices)
    qkv_g = qkv.reshape(3, width, shard).transpose(1, 0, 2)
    wide = jnp.concatenate([small[:6], small[8:14]], axis=1)
    up_g = jnp.concatenate([mid[width:, :shard], mid[width:, shard:]])
    return (
        activations, input_grad, qkv_g, jnp.stack([small[7], small[15]]), mid[:shard], wide[0], wide[1], wide[2],
        up_g, small[6], mid[shard:width], wide[3], wide[4], wide[5],
    )


def solution(mesh):
    placed = (
        P(("dp", "tensor"), None),
        P("dp"),
        P("dp", None),
        P(None, None, "tensor"),
        P(None, "tensor"),
        P("tensor", None),
        P(),
        P(),
        P(),
        P(None, "tensor"),
        P("tensor"),
        P("tensor", None),
        P(),
        P(),
        P(),
        P(("dp", "tensor"), None),
    )
    return jax.shard_map(
        functools.partial(local, mesh.shape["dp"]),
        mesh=mesh,
        in_specs=placed,
        out_specs=(
            P(("dp", "tensor"), None),
            P(("dp", "tensor"), None),
            P(None, None, "tensor"),
            P(None, "tensor"),
            P("tensor", None),
            P(),
            P(),
            P(),
            P(None, "tensor"),
            P("tensor"),
            P("tensor", None),
            P(),
            P(),
            P(),
        ),
        check_vma=False,
    )
```

```python
import functools

import jax
import jax.numpy as jnp
from jax import lax
from jax.experimental import pallas as pl
from jax.experimental.pallas import tpu as pltpu
from jax.sharding import PartitionSpec as P

HD = 64
LANES = 128
NORM_EPS = 1e-05
MASK_BIG = 2.0**100
LOG2E = 1.4426950408889634
VMEM_BYTES = 58 * 2**20
BF = jnp.bfloat16
F32 = jnp.float32
VMEM = pl.BlockSpec(memory_space=pltpu.VMEM)
HBM = pl.BlockSpec(memory_space=pl.ANY)


def dot(left, right, left_dim, right_dim):
    return lax.dot_general(
        left, right, (((left_dim,), (right_dim,)), ((), ())), preferred_element_type=F32
    )


def params():
    return pltpu.CompilerParams(vmem_limit_bytes=VMEM_BYTES)


def cost(macs, moved):
    return pl.CostEstimate(flops=2 * macs, bytes_accessed=moved, transcendentals=0)


def values_columns(rows):
    lane = lax.broadcasted_iota(jnp.int32, (rows, LANES), 1)
    return jnp.where((lane == HD) | (lane == HD + 1), 1.0, 0.0)


def live_rows(place_ref, first, rows, columns=slice(None)):
    place = place_ref[:, columns]
    row = lax.broadcasted_iota(jnp.int32, (rows, place.shape[1]), 0) + first
    return jnp.where(row == place, 1.0, 0.0).astype(BF)


def key_value_block(x_ref, place_ref, bounds_ref, w_refs, bias_ref, x_out, k_ref, v_ref, first, rows):
    at = pl.ds(first, rows)
    later = slice(first, None) if isinstance(first, int) else slice(None)
    x = dot(live_rows(place_ref, first, rows, later), x_ref[later, :], 1, 0).astype(BF)
    x_out[at, :] = x
    shard = w_refs[0].shape[2]
    row = lax.broadcasted_iota(jnp.int32, (rows, LANES), 0) + first
    extra_k = jnp.where((row >= bounds_ref[0:1, :]) & (row < bounds_ref[1:2, :]), 1.0, 0.0)
    extra_v = values_columns(rows)
    low = lax.broadcasted_iota(jnp.int32, (rows, LANES), 1) < HD
    for side, w_ref in enumerate(w_refs):
        mine = slice(side * shard, (side + 1) * shard)
        keys = dot(x, w_ref[1], 1, 0)
        values = dot(x, w_ref[2], 1, 0) + bias_ref[1:2, mine]
        for i in range(shard // HD):
            pair = slice((i // 2) * LANES, (i // 2 + 1) * LANES)
            k_pair, v_pair = keys[:, pair], values[:, pair]
            if i % 2:
                k_pair, v_pair = pltpu.roll(k_pair, HD, 1), pltpu.roll(v_pair, HD, 1)
            h = side * (shard // HD) + i
            k_ref[h, at, :] = jnp.where(low, k_pair, extra_k).astype(BF)
            v_ref[h, at, :] = jnp.where(low, v_pair, extra_v).astype(BF)


def project_kernel(x_ref, own_ref, oth_ref, bias_ref, place_ref, bounds_ref, extra_q_ref, k_ref, v_ref, x_out, qt_ref, q_ref):
    block = q_ref.shape[0]
    first = pl.multiple_of(pl.program_id(0) * block, block)
    shard = own_ref.shape[2]
    key_value_block(
        x_ref, place_ref, bounds_ref, (own_ref, oth_ref), bias_ref, x_out, k_ref, v_ref, first, block
    )
    x = x_ref[pl.ds(first, block), :]
    for side, w_ref in enumerate((own_ref, oth_ref)):
        mine = slice(side * shard, (side + 1) * shard)
        q = (dot(x, w_ref[0], 1, 0) + bias_ref[0:1, mine]).astype(BF)
        q_ref[:, mine] = q
        turned = q.T
        for i in range(shard // HD):
            h = side * (shard // HD) + i
            qt_ref[h, :HD, :] = turned[i * HD : (i + 1) * HD, :]
            qt_ref[h, HD:, :] = extra_q_ref[...]


def project(x, w_own, w_oth, bias, place, bounds, extra_q):
    tokens, width = x.shape
    heads = width // HD
    block = 256
    whole = lambda *shape: pl.BlockSpec(shape, lambda i: (0,) * len(shape))
    per_head = whole(heads, tokens, LANES)
    return pl.pallas_call(
        project_kernel,
        grid=(tokens // block,),
        out_shape=(
            jax.ShapeDtypeStruct((heads, tokens, LANES), BF),
            jax.ShapeDtypeStruct((heads, tokens, LANES), BF),
            jax.ShapeDtypeStruct((tokens, width), BF),
            jax.ShapeDtypeStruct((heads, LANES, tokens), BF),
            jax.ShapeDtypeStruct((tokens, width), BF),
        ),
        in_specs=[
            whole(*x.shape),
            whole(*w_own.shape),
            whole(*w_oth.shape),
            whole(*bias.shape),
            whole(*place.shape),
            whole(*bounds.shape),
            pl.BlockSpec((HD, block), lambda i: (0, i)),
        ],
        out_specs=(
            per_head,
            per_head,
            whole(tokens, width),
            pl.BlockSpec((heads, LANES, block), lambda i: (0, 0, i)),
            pl.BlockSpec((block, width), lambda i: (i, 0)),
        ),
        compiler_params=params(),
        cost_estimate=cost(5 * tokens * width * width, 12 * tokens * width),
        name="project",
    )(x, w_own, w_oth, bias, place, bounds, extra_q)


def key_sizes(keys):
    return (keys * 13 // 16, keys)


def for_size(live, keys, work):
    below = 0
    for size in key_sizes(keys):

        @pl.when((live > below) & (live <= size) if below else live <= size)
        def _():
            work(size)

        below = size


def attend_kernel(
    count, chunk, live_ref, qt_hbm, k_hbm, v_hbm, x_ref, own_ref, oth_ref, bias_ref, place_ref, bounds_ref,
    p_hbm, ot_ref, linv_ref, k_oth_hbm, v_oth_hbm, x_oth_hbm,
    qt_ref, k0_ref, k1_ref, v0_ref, v1_ref, x1_ref,
    s0_scr, s1_scr, peak0_scr, peak1_scr, row_scr, acc_scr, p_scr, sem, in_sem, out_sem,
):
    heads, _, queries = qt_ref.shape
    half = k0_ref.shape[1]
    parts = queries // chunk
    steps = heads * parts
    slots = p_scr.shape[0]

    def copies_in(h):
        return [
            pltpu.make_async_copy(src.at[h], dst.at[h], in_sem.at[h, n])
            for n, (src, dst) in enumerate(((qt_hbm, qt_ref), (k_hbm, k0_ref), (v_hbm, v0_ref)))
        ]

    for h in range(heads):
        for copy in copies_in(h):
            copy.start()

    def project_live(size):
        for first in range(0, size, size // count):
            key_value_block(
                x_ref, place_ref, bounds_ref, (own_ref, oth_ref), bias_ref, x1_ref, k1_ref, v1_ref, first, size // count
            )
        if size < half:
            x1_ref[size:, :] = jnp.zeros((half - size, x1_ref.shape[1]), BF)

    for_size(live_ref[1], half, project_live)

    copies_kv = [
        pltpu.make_async_copy(k1_ref, k_oth_hbm, out_sem.at[0]),
        pltpu.make_async_copy(v1_ref, v_oth_hbm, out_sem.at[1]),
        pltpu.make_async_copy(x1_ref, x_oth_hbm, out_sem.at[2]),
    ]
    for copy in copies_kv:
        copy.start()

    def columns(step):
        return pl.ds(pl.multiple_of(lax.rem(step, parts) * chunk, chunk), chunk)

    def copies_out(step, size):
        slot = lax.rem(step, slots)
        copies = []
        for part in range(2):
            rows = slice(part * half, part * half + size)
            to = p_hbm.at[step // parts, rows, columns(step)]
            copies.append(pltpu.make_async_copy(p_scr.at[slot, rows, :], to, sem.at[slot, part]))
        return copies

    def blocks(first, second, size):
        for part, ref in enumerate((first, second)):
            for at in range(0, size, size // count):
                end = at + size // count
                yield ref, slice(at, end), slice(part * half + at, part * half + end)

    def scores(step, s_ref, peak, keys, rows, to):
        s = dot(keys[step // parts, rows, :], qt_ref[step // parts, :, columns(step)], 1, 0)
        s_ref[to, :] = s
        return jnp.maximum(peak, jnp.max(s.reshape(-1, 8, chunk), axis=0))

    def mix(step, s_ref, values, rows, to):
        p = jnp.exp2((s_ref[to, :] - row_scr[...]) * (LOG2E * HD**-0.5)).astype(BF)
        p_scr[lax.rem(step, slots), to, :] = p
        return dot(values[step // parts, rows, :], p, 0, 0)

    def run(size, step, s_ref, peak_ref, after, s_after, peak_after):
        row_scr[...] = jnp.max(peak_ref[...], axis=0, keepdims=True)

        @pl.when(step >= slots)
        def _():
            for copy in copies_out(step - slots, size):
                copy.wait()

        peak = jnp.full((8, chunk), -jnp.inf, F32)
        acc = jnp.zeros((LANES, chunk), F32)
        for (k_ref, rows, to), (v_ref, _, _) in zip(blocks(k0_ref, k1_ref, size), blocks(v0_ref, v1_ref, size)):
            peak = scores(after, s_after, peak, k_ref, rows, to)
            acc = acc + mix(step, s_ref, v_ref, rows, to)
        peak_after[...] = peak
        acc_scr[...] = acc
        for copy in copies_out(step, size):
            copy.start()
        inverse = 1.0 / acc_scr[HD : HD + 1, :]
        linv_ref[step // parts, :, columns(step)] = inverse
        ot_ref[step // parts, :, columns(step)] = acc_scr[:HD, :] * inverse

    for copy in copies_in(0):
        copy.wait()

    def work(size):
        peak = jnp.full((8, chunk), -jnp.inf, F32)
        for k_ref, rows, to in blocks(k0_ref, k1_ref, size):
            peak = scores(0, s0_scr, peak, k_ref, rows, to)
        peak0_scr[...] = peak

        @pl.loop(0, steps // 2)
        def _(i):
            run(size, 2 * i, s0_scr, peak0_scr, 2 * i + 1, s1_scr, peak1_scr)
            after = 2 * i + 2

            @pl.when((after < steps) & (lax.rem(after, parts) == 0))
            def _():
                for copy in copies_in(after // parts):
                    copy.wait()

            run(size, 2 * i + 1, s1_scr, peak1_scr, jnp.minimum(after, steps - 1), s0_scr, peak0_scr)

        for slot in range(slots):
            for copy in copies_out(steps - slots + slot, size):
                copy.wait()

    for_size(live_ref[1], half, work)
    for copy in copies_kv:
        copy.wait()


def attend(live, qt, k_own, v_own, x_oth, w_own, w_oth, bias, place, bounds):
    heads, _, queries = qt.shape
    keys = 2 * queries
    count, chunk, slots = 4, 512, 4
    per_head = jax.ShapeDtypeStruct(k_own.shape, BF)
    return pl.pallas_call(
        functools.partial(attend_kernel, count, chunk),
        out_shape=(
            jax.ShapeDtypeStruct((heads, keys, queries), BF),
            jax.ShapeDtypeStruct((heads, HD, queries), F32),
            jax.ShapeDtypeStruct((heads, 1, queries), F32),
            per_head,
            per_head,
            jax.ShapeDtypeStruct(x_oth.shape, BF),
        ),
        in_specs=[pl.BlockSpec(memory_space=pltpu.SMEM)] + [HBM] * 3 + [VMEM] * 6,
        out_specs=(HBM, VMEM, VMEM, HBM, HBM, HBM),
        scratch_shapes=[
            pltpu.VMEM(qt.shape, BF),
            pltpu.VMEM(k_own.shape, BF),
            pltpu.VMEM(k_own.shape, BF),
            pltpu.VMEM(k_own.shape, BF),
            pltpu.VMEM(k_own.shape, BF),
            pltpu.VMEM(x_oth.shape, BF),
            pltpu.VMEM((keys, chunk), F32),
            pltpu.VMEM((keys, chunk), F32),
            pltpu.VMEM((8, chunk), F32),
            pltpu.VMEM((8, chunk), F32),
            pltpu.VMEM((1, chunk), F32),
            pltpu.VMEM((LANES, chunk), F32),
            pltpu.VMEM((slots, keys, chunk), BF),
            pltpu.SemaphoreType.DMA((slots, 2)),
            pltpu.SemaphoreType.DMA((heads, 3)),
            pltpu.SemaphoreType.DMA((3,)),
        ],
        compiler_params=params(),
        cost_estimate=cost(heads * keys * queries * 512, 2 * heads * keys * queries),
        name="attend",
    )(live, qt, k_own, v_own, x_oth, w_own, w_oth, bias, place, bounds)


def normalize(values):
    mean = jnp.mean(values, axis=-1, keepdims=True)
    centered = values - mean
    inverse = lax.rsqrt(jnp.mean(centered * centered, axis=-1, keepdims=True) + NORM_EPS)
    return centered * inverse, inverse


def norm_back(e, normed, inverse):
    return inverse * (
        e - jnp.mean(e, axis=-1, keepdims=True) - normed * jnp.mean(e * normed, axis=-1, keepdims=True)
    )


def middle_kernel(
    sub, x_ref, cot_ref, ot_ref, linv_ref, w_own_ref, w_oth_ref, vec_ref,
    act_ref, res_ref, dot_ref, dnat_ref, own_ref, oth_ref, small_ref,
    att_scr, w_out_ref, w_up_ref, w_down_ref, b_up_ref, gw_ref,
):
    block, width = x_ref.shape
    heads = width // HD
    shard = width // 2
    b_out, gain1, bias1, b_down, gain2, bias2 = (vec_ref[i : i + 1, :] for i in range(6))

    @pl.when(pl.program_id(0) == 0)
    def _():
        gw_ref[...] = jnp.zeros_like(gw_ref)
        small_ref[...] = jnp.zeros_like(small_ref)
        for side, ref in enumerate((w_own_ref, w_oth_ref)):
            mine = slice(side * shard, (side + 1) * shard)
            w_out_ref[mine, :] = ref[:shard, :]
            w_down_ref[mine, :] = ref[shard : 2 * shard, :]
            w_up_ref[:shard, mine] = ref[2 * shard : 3 * shard, :shard]
            w_up_ref[shard:, mine] = ref[2 * shard : 3 * shard, shard:]
            b_up_ref[:, mine] = ref[3 * shard : 3 * shard + 1, :shard].astype(F32)

    def col_sum(row, values):
        small_ref[row : row + 1, :] += jnp.sum(values, axis=0, keepdims=True)

    def chain(u):
        rows = slice(u * sub, (u + 1) * sub)
        for h in range(heads):
            att_scr[u, h * HD : (h + 1) * HD, :] = ot_ref[h, :, rows].astype(BF)
        branch = dot(att_scr[u], w_out_ref[...], 0, 0)
        yield
        n1, inv1 = normalize(x_ref[rows, :].astype(F32) + branch + b_out)
        first = n1 * gain1 + bias1
        first_low = first.astype(BF)
        yield
        pre = dot(first_low, w_up_ref[...], 1, 0) + b_up_ref[...]
        yield
        cdf = 0.5 * (1.0 + lax.erf(pre * 0.5**0.5))
        hidden = (pre * cdf).astype(BF)
        slope = cdf + pre * (0.3989422804014327 * jnp.exp(-0.5 * pre * pre))
        yield
        branch = dot(hidden, w_down_ref[...], 1, 0)
        yield
        n2, inv2 = normalize(first + branch + b_down)
        act_ref[rows, :] = (n2 * gain2 + bias2).astype(BF)
        cot = cot_ref[rows, :].astype(F32)
        two = norm_back(cot * gain2, n2, inv2)
        two_low = two.astype(BF)
        yield
        back = dot(two_low, w_down_ref[...], 1, 1)
        gw_ref[2] += dot(hidden, two_low, 0, 0)
        col_sum(3, two)
        col_sum(4, cot * n2)
        col_sum(5, cot)
        yield
        pre_grad = (back * slope).astype(BF)
        yield
        back = dot(pre_grad, w_up_ref[...], 1, 1)
        gw_ref[1] += dot(first_low, pre_grad, 0, 0)
        col_sum(6, pre_grad.astype(F32))
        yield
        one = two + back
        res = norm_back(one * gain1, n1, inv1)
        res_ref[rows, :] = res
        res_low = res.astype(BF)
        yield
        turned = dot(w_out_ref[...], res_low, 1, 1)
        gw_ref[0] += dot(att_scr[u], res_low, 1, 0)
        col_sum(1, one * n1)
        col_sum(2, one)
        col_sum(0, res)
        yield
        pick = lax.broadcasted_iota(jnp.int32, (HD, sub), 0)
        for h in range(heads):
            head = slice(h * HD, (h + 1) * HD)
            grad = (turned[head].astype(BF).astype(F32) * linv_ref[h, :, rows]).astype(BF)
            inner = -jnp.sum(grad.astype(F32) * ot_ref[h, :, rows], axis=0, keepdims=True)
            high = inner.astype(BF).astype(F32)
            dot_ref[h, :HD, rows] = grad
            dot_ref[h, HD:, rows] = jnp.where(pick == 0, high, jnp.where(pick == 1, inner - high, 0.0)).astype(BF)
            att_scr[u, head, :] = grad
        dnat_ref[rows, :] = att_scr[u].T
        yield

    for _ in zip(*(chain(u) for u in range(block // sub))):
        pass

    @pl.when(pl.program_id(0) == pl.num_programs(0) - 1)
    def _():
        for ref, mine in ((own_ref, slice(0, shard)), (oth_ref, slice(shard, width))):
            ref[:shard, :] = gw_ref[0, mine, :].astype(ref.dtype)
            ref[shard:width, :] = gw_ref[2, mine, :].astype(ref.dtype)
            ref[width:, :shard] = gw_ref[1, :shard, mine].astype(ref.dtype)
            ref[width:, shard:] = gw_ref[1, shard:, mine].astype(ref.dtype)


def middle(x, cot, ot, linv, w_own, w_oth, vectors):
    tokens, width = x.shape
    heads = width // HD
    block, sub = 512, 256
    whole = lambda *shape: pl.BlockSpec(shape, lambda i: (0,) * len(shape))
    rows = pl.BlockSpec((block, width), lambda i: (i, 0))
    columns = lambda n: pl.BlockSpec((heads, n, block), lambda i: (0, 0, i))
    square = pltpu.VMEM((width, width), BF)
    return pl.pallas_call(
        functools.partial(middle_kernel, sub),
        grid=(tokens // block,),
        out_shape=(
            jax.ShapeDtypeStruct((tokens, width), BF),
            jax.ShapeDtypeStruct((tokens, width), F32),
            jax.ShapeDtypeStruct((heads, LANES, tokens), BF),
            jax.ShapeDtypeStruct((tokens, width), BF),
            jax.ShapeDtypeStruct((3 * width // 2, width), F32),
            jax.ShapeDtypeStruct((3 * width // 2, width), BF),
            jax.ShapeDtypeStruct((8, width), F32),
        ),
        in_specs=[rows, rows, columns(HD), columns(1), whole(*w_own.shape), whole(*w_oth.shape), whole(*vectors.shape)],
        out_specs=(
            rows, rows, columns(LANES), rows,
            whole(3 * width // 2, width), whole(3 * width // 2, width), whole(8, width),
        ),
        scratch_shapes=[
            pltpu.VMEM((block // sub, width, sub), BF), square, square, square,
            pltpu.VMEM((1, width), F32), pltpu.VMEM((3, width, width), F32),
        ],
        compiler_params=params(),
        cost_estimate=cost(9 * tokens * width * width, 20 * tokens * width),
        name="middle",
    )(x, cot, ot, linv, w_own, w_oth, vectors)


def times_weights(grad, own_ref, oth_ref, third):
    shard = own_ref.shape[2]
    return dot(grad[:, :shard], own_ref[third], 1, 1) + dot(grad[:, shard:], oth_ref[third], 1, 1)


def backward_kernel(sub, part, *refs):
    if part:
        (live_ref, place_ref, p_hbm, dot_hbm, dnat_hbm, q_hbm, k_hbm, v_hbm, x_hbm, own_hbm, oth_hbm,
         dq_hbm, dx_ref, gw_ref, bias_ref,
         dot_ref, dnat_ref, q_ref, k_ref, v_ref, x_ref, own_ref, oth_ref,
         dq_ref, dk_ref, dv_ref, dx_scr, acc_scr, p_scr, sem, pair_sem, last_sem, out_sem) = refs
        more = ((own_hbm, own_ref), (oth_hbm, oth_ref))
    else:
        (live_ref, small_ref, value_ref,
         p_hbm, dot_hbm, dnat_hbm, q_hbm, k_hbm, v_hbm, x_hbm, dq_hbm, gw_hbm, whole_hbm,
         sent_ref, kept_ref, dq_out, dk_hbm, dv_hbm,
         dot_ref, dnat_ref, q_ref, k_ref, v_ref, x_ref, before_ref, gw_ref, whole_ref,
         dq_ref, dk_ref, dv_ref, gq_ref, bias_ref, acc_scr, p_scr, sem, pair_sem, last_sem, out_sem) = refs
        more = ((dq_hbm, before_ref), (gw_hbm, gw_ref), (whole_hbm, whole_ref))
    heads, _, queries = dot_ref.shape
    keys = k_ref.shape[1]
    width = heads * HD
    shard = width // 2
    slots = p_scr.shape[0]
    pairs = heads // 2

    def parts_of(size):
        return [(at, at + size // 2) for at in range(0, size, size // 2)]

    def copy_in(p, j, size):
        first, end = parts_of(size)[j]
        slot = lax.rem(p * len(parts_of(size)) + j, slots)
        src = p_hbm.at[pl.ds(2 * p, 2), part * keys + first : part * keys + end, :]
        return pltpu.make_async_copy(src, p_scr.at[slot, :, : end - first, :], sem.at[slot])

    def pair_copies(p):
        pair = pl.ds(2 * p, 2)
        lanes = pl.ds(pl.multiple_of(p * LANES, LANES), LANES)
        by_head = ((dot_hbm, dot_ref), (k_hbm, k_ref), (v_hbm, v_ref))
        by_lane = ((dnat_hbm, dnat_ref), (q_hbm, q_ref))
        return [
            pltpu.make_async_copy(src.at[pair], dst.at[pair], pair_sem.at[p, n]) for n, (src, dst) in enumerate(by_head)
        ] + [
            pltpu.make_async_copy(src.at[:, lanes], dst.at[:, lanes], pair_sem.at[p, 3 + n])
            for n, (src, dst) in enumerate(by_lane)
        ]

    last = ((x_hbm, x_ref),) + more

    def rows_out(p):
        rows = pl.ds(pl.multiple_of(p * 2 * HD, 2 * HD), 2 * HD)
        return pltpu.make_async_copy(dq_ref.at[rows, :], dq_hbm.at[rows, :], out_sem.at[p])

    last_copies = [pltpu.make_async_copy(src, dst, last_sem.at[n]) for n, (src, dst) in enumerate(last)]

    for copy in pair_copies(0):
        copy.start()

    def work(size):
        if size < keys:
            dk_ref[size:, :] = jnp.zeros((keys - size, width), BF)
            dv_ref[size:, :] = jnp.zeros((keys - size, width), BF)
        cuts = parts_of(size)
        count = len(cuts)
        for step in range(slots - 1):
            copy_in(step // count, step % count, size).start()

        @pl.loop(0, pairs)
        def _(p):
            lanes = pl.ds(pl.multiple_of(p * LANES, LANES), LANES)
            for copy in pair_copies(p):
                copy.wait()

            @pl.when(p + 1 < pairs)
            def _():
                for copy in pair_copies(p + 1):
                    copy.start()

            @pl.when(p == 1)
            def _():
                for copy in last_copies:
                    copy.start()

            total = [0.0, 0.0]
            for j, (first, end) in enumerate(cuts):
                slot = lax.rem(p * count + j, slots)
                copy_in(p, j, size).wait()
                ahead = j + slots - 1

                @pl.when(p + ahead // count < pairs)
                def _():
                    copy_in(p + ahead // count, ahead % count, size).start()

                for at in range(first, end, size // 4):
                    rows = size // 4
                    here = slice(at, at + rows)
                    low = lax.broadcasted_iota(jnp.int32, (rows, LANES), 1) < HD
                    dks, dvs = [], []
                    for side in range(2):
                        h = 2 * p + side
                        prob = p_scr[slot, side, at - first : at - first + rows, :]
                        slope = dot(v_ref[h, here, :], dot_ref[h], 1, 0)
                        dvs.append(dot(prob, dnat_ref[:, lanes], 1, 0))
                        ds = (prob.astype(F32) * slope).astype(BF)
                        dks.append(dot(ds, q_ref[:, lanes], 1, 0))
                        total[side] = total[side] + dot(k_ref[h, here, :], ds, 0, 0)
                    dk_ref[here, lanes] = (jnp.where(low, dks[0], dks[1]) * HD**-0.5).astype(BF)
                    dv_ref[here, lanes] = jnp.where(low, dvs[0], dvs[1]).astype(BF)
                for side in range(2):
                    if j == 0:
                        acc_scr[side] = total[side]
                    else:
                        acc_scr[side] += total[side]
                total = [0.0, 0.0]

            for side in range(2):
                dq_ref[pl.ds(pl.multiple_of((2 * p + side) * HD, HD), HD), :] = acc_scr[side, :HD, :]
            if part:
                rows_out(p).start()

    for_size(live_ref[1], keys, work)
    for copy in last_copies:
        copy.wait()
    bias_ref[...] = jnp.zeros_like(bias_ref)
    if part:
        gw_ref[...] = jnp.zeros_like(gw_ref)
        copies_out = [rows_out(p) for p in range(heads // 2)]
    else:
        gq_ref[...] = jnp.zeros_like(gq_ref)
        copies_out = [
            pltpu.make_async_copy(dk_ref, dk_hbm, out_sem.at[0]),
            pltpu.make_async_copy(dv_ref, dv_hbm, out_sem.at[1]),
        ]
        for copy in copies_out:
            copy.start()

    def weight_sums(size):
        for at in range(0, size, size // 4):
            rows = slice(at, at + size // 4)
            x, dk, dv = x_ref[rows, :], dk_ref[rows, :], dv_ref[rows, :]
            gw_ref[0] += dot(x, dk, 0, 0)
            gw_ref[1] += dot(x, dv, 0, 0)
            bias_ref[1:2, :] += jnp.sum(dv.astype(F32), axis=0, keepdims=True)
            if part:
                dx = times_weights(dk, own_ref, oth_ref, 1) + times_weights(dv, own_ref, oth_ref, 2)
                dx_scr[rows, :] = dx.astype(BF)
        if part:
            for at in range(0, keys, sub):
                rows, earlier = slice(at, at + sub), min(at + sub, size)
                dx_ref[rows, :] = dot(live_rows(place_ref, 0, earlier, rows), dx_scr[:earlier, :], 0, 0).astype(BF)

    for_size(live_ref[1], keys, weight_sums)
    if not part:

        @pl.loop(0, queries // sub)
        def _(i):
            rows = pl.ds(pl.multiple_of(i * sub, sub), sub)
            dq = ((before_ref[:, rows] + dq_ref[:, rows]) * HD**-0.5).astype(BF).T
            dq_out[rows, :] = dq
            gq_ref[...] += dot(whole_ref[rows, :], dq, 0, 0)
            bias_ref[0:1, :] += jnp.sum(dq.astype(F32), axis=0, keepdims=True)

    if not part:
        first = live_ref[0] == 0
        bias_ref[1:2, :] += value_ref[1:2, :]
        cut = 3 * width // 2
        for side in range(2):
            mine = slice(side * shard, (side + 1) * shard)
            pieces = [gq_ref[:, mine], gw_ref[0, :, mine], gw_ref[1, :, mine]]
            blocks = [piece[at : at + shard, :].astype(BF) for piece in pieces for at in (0, shard)]
            for n in range(3):
                to = slice(side * cut + n * shard, side * cut + (n + 1) * shard)
                kept_ref[to, :] = jnp.where(first, blocks[n], blocks[3 + n])
                sent_ref[to, :] = jnp.where(first, blocks[3 + n], blocks[n])
            rows16 = [small_ref[:6, :shard], small_ref[6:7, mine], bias_ref[0:1, mine]]
            rows16 += [small_ref[:6, shard:], jnp.zeros((1, shard), F32), bias_ref[1:2, mine]]
            value = jnp.concatenate(rows16, axis=0)
            high = value.astype(BF)
            for n, half in enumerate((high, (value - high.astype(F32)).astype(BF))):
                to = slice(2 * cut + (2 * side + n) * 16, 2 * cut + (2 * side + n + 1) * 16)
                kept_ref[to, :] = half
                sent_ref[to, :] = half

    for copy in copies_out:
        copy.wait()


def attend_backward(part, first, probs, dot_turned, dnat, q, k, v, x, *more):
    heads, keys, queries = probs.shape
    width = heads * HD
    sub, slots = 256, 4
    sums = jax.ShapeDtypeStruct((2, width, width), F32)
    turned = jax.ShapeDtypeStruct((width, queries), F32)
    grad = jax.ShapeDtypeStruct((queries, width), BF)
    inputs = (dot_turned, dnat, q, k, v, x) + more
    held = [pltpu.VMEM(a.shape, a.dtype) for a in inputs]
    held += [pltpu.VMEM(turned.shape, F32), pltpu.VMEM(grad.shape, BF), pltpu.VMEM(grad.shape, BF)]
    if part:
        out_shape = (turned, grad, sums, jax.ShapeDtypeStruct((2, width), F32))
        out_specs = (HBM, VMEM, VMEM, VMEM)
        held.append(pltpu.VMEM(grad.shape, BF))
    else:
        payload = jax.ShapeDtypeStruct((3 * width + 64, width // 2), BF)
        out_shape = (payload, payload, grad, grad, grad)
        out_specs = (VMEM, VMEM, VMEM, HBM, HBM)
        held += [pltpu.VMEM((width, width), F32), pltpu.VMEM((2, width), F32)]
    first_specs = [pl.BlockSpec(memory_space=pltpu.SMEM), VMEM, VMEM][: len(first)]
    return pl.pallas_call(
        functools.partial(backward_kernel, sub, part),
        out_shape=out_shape,
        in_specs=first_specs + [HBM] * (1 + len(inputs)),
        out_specs=out_specs,
        scratch_shapes=held
        + [
            pltpu.VMEM((2, LANES, queries), F32),
            pltpu.VMEM((slots, 2, keys // 4, queries), BF),
            pltpu.SemaphoreType.DMA((slots,)),
            pltpu.SemaphoreType.DMA((heads // 2, 5)),
            pltpu.SemaphoreType.DMA((1 + len(more),)),
            pltpu.SemaphoreType.DMA((heads // 2,)),
        ],
        compiler_params=params(),
        cost_estimate=cost(heads * keys * queries * 512, heads * keys * queries),
        name="attend_back_own" if not part else "attend_back_other",
    )(*first, probs, *inputs)


def input_kernel(res_ref, got_ref, dq_ref, dk_ref, dv_ref, own_ref, oth_ref, place_ref, dx_ref, live_scr):
    @pl.when(pl.program_id(0) == 0)
    def _():
        @pl.loop(0, live_scr.shape[0] // 256)
        def _(i):
            rows = pl.ds(pl.multiple_of(i * 256, 256), 256)
            live_scr[rows, :] = (
                times_weights(dk_ref[rows, :], own_ref, oth_ref, 1) + times_weights(dv_ref[rows, :], own_ref, oth_ref, 2)
            ).astype(BF)

    dx = res_ref[...] + got_ref[...].astype(F32) + times_weights(dq_ref[...], own_ref, oth_ref, 0)
    dx_ref[...] = dx + dot(live_rows(place_ref, 0, live_scr.shape[0]), live_scr[...], 0, 0)


def input_gradient(res, got, dq, dk, dv, w_own, w_oth, place):
    tokens, width = res.shape
    rows = pl.BlockSpec((256, width), lambda i: (i, 0))
    whole = lambda *shape: pl.BlockSpec(shape, lambda i: (0,) * len(shape))
    return pl.pallas_call(
        input_kernel,
        grid=(tokens // 256,),
        out_shape=jax.ShapeDtypeStruct((tokens, width), F32),
        in_specs=[rows] * 3 + [whole(*dk.shape)] * 2 + [whole(*w_own.shape)] * 2 + [pl.BlockSpec((1, 256), lambda i: (0, i))],
        out_specs=rows,
        scratch_shapes=[pltpu.VMEM(dk.shape, BF)],
        compiler_params=params(),
        cost_estimate=cost(3 * tokens * width * width, 16 * tokens * width),
        name="input_gradient",
    )(res, got, dq, dk, dv, w_own, w_oth, place)


def after(values, *others):
    return lax.optimization_barrier((values,) + others)[0]


def two_halves(values):
    high = values.astype(BF)
    return jnp.concatenate([high, (values - high.astype(F32)).astype(BF)], axis=0)


def one_value(halves):
    rows = halves.shape[0] // 2
    return halves[:rows].astype(F32) + halves[rows:].astype(F32)


def take(values, which):
    return lax.dynamic_index_in_dim(values, which, 0, False)


def in_order(mine, theirs, which):
    return jnp.concatenate([jnp.where(which == 0, mine, theirs), jnp.where(which == 0, theirs, mine)])


def sum_gradients(sent, kept, mid, input_grad, devices):
    index = lax.axis_index("dp")
    core, near = lax.rem(index, 2), lax.rem(index // 2, 2)
    rows = (sent.shape[0] - 64) // 2

    def across(values, bit):
        return lax.ppermute(values, "dp", [(i, i ^ bit) for i in range(devices)])

    got = across(sent, 1)
    halves = mid.reshape(2, mid.shape[0] // 2, -1)
    mid_got = across(take(halves, 1 - core).astype(BF), 1)
    total = kept[: 2 * rows].astype(F32) + got[: 2 * rows].astype(F32)
    small_own = one_value(kept[2 * rows : 2 * rows + 32]) + one_value(got[2 * rows : 2 * rows + 32])
    small_oth = one_value(kept[2 * rows + 32 :]) + one_value(got[2 * rows + 32 :])
    mid = (take(halves, core) + mid_got.astype(F32)).astype(BF)
    oth_two = two_halves(small_oth)
    mid_got = across(after(mid, oth_two), 4)
    result = input_grad(got)

    own_two = two_halves(small_own)
    got = lax.ppermute(jnp.concatenate([total[rows:].astype(BF), oth_two]), "tensor", [(0, 1), (1, 0)])
    total = total[:rows] + got[:rows].astype(F32)
    small = one_value(own_two) + one_value(got[rows:])

    halves = total.reshape(2, rows // 2, -1)
    two = two_halves(small)
    got = across(jnp.concatenate([take(halves, 1 - near).astype(BF), two]), 2)
    total = take(halves, near) + got[: rows // 2].astype(F32)
    small = one_value(two) + one_value(got[rows // 2 :])

    bit = 4
    while bit < devices:
        sent = jnp.concatenate([total.astype(BF), two_halves(small)])
        mid = (mid.astype(F32) + mid_got.astype(F32)).astype(BF)
        if 2 * bit < devices:
            mid_got = across(mid, 2 * bit)
        got = across(sent, bit)
        total = sent[: rows // 2].astype(F32) + got[: rows // 2].astype(F32)
        small = one_value(sent[rows // 2 :]) + one_value(got[rows // 2 :])
        bit *= 2
    mid = in_order(mid, across(mid, 1), core)
    mid = in_order(after(mid, got), after(across(mid, 2), got), near)

    total = total.astype(BF)
    total = in_order(total, across(total, 2), near)
    total = in_order(total, across(total, 1), core)
    return total.astype(F32), small, mid.astype(F32), result


def mask_parts(known, lengths, halves):
    tokens, slots = known.shape[0] // halves, lengths.shape[0]
    positions = jnp.arange(known.shape[0], dtype=jnp.int32)
    ends = jnp.cumsum(lengths)
    starts = ends - lengths
    inside = (positions[:, None] >= starts[None, :]) & (positions[:, None] < ends[None, :])
    opening = jnp.any((positions[:, None] == starts[None, :]) & (lengths[None, :] > 0), axis=1)
    live = ((known > 0) | opening).astype(jnp.int32).reshape(halves, 1, tokens)
    place = jnp.where(live > 0, jnp.cumsum(live, axis=2) - 1, -1)
    counts = jnp.sum(live, axis=2)
    before = lambda ats: jnp.sum(
        jnp.where(positions.reshape(halves, 1, tokens) < ats[None, :, None], live, 0), axis=2
    )
    past = jnp.full((halves, LANES - HD - slots - 1), tokens, jnp.int32)
    none = jnp.full((halves, HD), tokens, jnp.int32)
    low = jnp.concatenate([none, before(starts), counts, past], axis=1)
    high = jnp.concatenate([none, before(ends), jnp.full((halves, 1), tokens, jnp.int32), past], axis=1)
    queries = jnp.where(jnp.pad(inside, ((0, 0), (0, 1))), 0.0, -MASK_BIG)
    queries = jnp.pad(queries, ((0, 0), (0, HD - slots - 1))).T.astype(BF)
    return place, jnp.stack([low, high], axis=1), queries, jnp.max(counts)


def local(
    devices, layer_input, gene_known, cell_genes, w_qkv, bias_qv, w_out, b_out, ln1_gain, ln1_bias,
    w_up, b_up, w_down, b_down, ln2_gain, ln2_bias, cotangent,
):
    tokens, width = layer_input.shape
    shard = w_qkv.shape[2]
    side, index = lax.axis_index("tensor"), lax.axis_index("dp")
    core, near = lax.rem(index, 2), lax.rem(index // 2, 2)

    def swapped(values):
        return lax.ppermute(values, "tensor", [(0, 1), (1, 0)])

    def across(values, bit):
        return lax.ppermute(values, "dp", [(i, i ^ bit) for i in range(devices)])

    w_own = w_qkv.transpose(1, 0, 2)
    quarter = 3 * width // 4
    mine = lax.dynamic_slice_in_dim(w_own.reshape(3 * width, shard), (2 * core + near) * quarter, quarter, 0)
    got = swapped(jnp.concatenate([mine, jnp.pad(bias_qv, ((0, 14), (0, 0)))]))
    x_oth = swapped(layer_input)
    piece = got[:quarter]
    piece = in_order(piece, across(piece, 2), near)
    w_oth = in_order(piece, across(piece, 1), core).reshape(3, width, shard)
    bias = jnp.concatenate([bias_qv, got[quarter : quarter + 2]], axis=1).astype(F32)

    place, bounds, query_rows, most = mask_parts(gene_known, cell_genes[0], 2)
    query_own = lax.dynamic_slice_in_dim(query_rows, side * tokens, tokens, 1)
    place_own, place_oth, bounds_own, bounds_oth = take(place, side), take(place, 1 - side), take(bounds, side), take(bounds, 1 - side)
    live = jnp.stack([core, most])
    b_up_row = jnp.pad(b_up[None], ((0, 15), (0, shard)))
    mid_w = jnp.concatenate([w_out, w_down, jnp.concatenate([w_up[:shard], w_up[shard:]], axis=1), b_up_row])
    vectors = jnp.stack([b_out, ln1_gain, ln1_bias, b_down, ln2_gain, ln2_bias, b_out, b_out])

    k_own, v_own, x_live, qt, q = project(layer_input, w_own, w_oth, bias, place_own, bounds_own, query_own)
    x_oth, k_own, mid_w = lax.optimization_barrier((x_oth, k_own, mid_w))
    mid_w_oth = swapped(mid_w)
    probs, ot, linv, k_oth, v_oth, x_oth = attend(
        live, qt, k_own, v_own, x_oth, w_own, w_oth, bias, place_oth, bounds_oth
    )
    activations, res, dot_turned, dnat, mid_own, mid_oth, small = middle(
        layer_input, cotangent, ot, linv, mid_w, mid_w_oth, vectors
    )
    mid_got = swapped(mid_oth)
    dq, dx_oth, sums, value_grad = attend_backward(
        1, (live, place_oth), probs, dot_turned, dnat, q, k_oth, v_oth, x_oth, w_own, w_oth
    )
    mid_got, dq = lax.optimization_barrier((mid_got, dq))
    mid = (mid_own + mid_got.astype(F32)).reshape(2, 3 * shard // 2, width)
    mid_got = across(take(mid, 1 - near).astype(BF), 2)
    dx_got = swapped(dx_oth)
    sent, kept, dq, dk, dv = attend_backward(
        0, (live, small, value_grad), probs, dot_turned, dnat, q, k_own, v_own, x_live, dq, sums, layer_input
    )
    mid_got, dx_got, sent = lax.optimization_barrier((mid_got, dx_got, sent))
    mid = take(mid, near) + mid_got.astype(F32)

    def input_grad(token):
        return input_gradient(res, dx_got, after(dq, token), dk, dv, w_own, w_oth, place_own)

    qkv, small, mid, input_grad = sum_gradients(sent, kept, mid, input_grad, devices)
    qkv_g = qkv.reshape(3, width, shard).transpose(1, 0, 2)
    wide = jnp.concatenate([small[:6], small[8:14]], axis=1)
    up_g = jnp.concatenate([mid[width:, :shard], mid[width:, shard:]])
    return (
        activations, input_grad, qkv_g, jnp.stack([small[7], small[15]]), mid[:shard], wide[0], wide[1], wide[2],
        up_g, small[6], mid[shard:width], wide[3], wide[4], wide[5],
    )


def solution(mesh):
    placed = (
        P(("dp", "tensor"), None),
        P("dp"),
        P("dp", None),
        P(None, None, "tensor"),
        P(None, "tensor"),
        P("tensor", None),
        P(),
        P(),
        P(),
        P(None, "tensor"),
        P("tensor"),
        P("tensor", None),
        P(),
        P(),
        P(),
        P(("dp", "tensor"), None),
    )
    return jax.shard_map(
        functools.partial(local, mesh.shape["dp"]),
        mesh=mesh,
        in_specs=placed,
        out_specs=(
            P(("dp", "tensor"), None),
            P(("dp", "tensor"), None),
            P(None, None, "tensor"),
            P(None, "tensor"),
            P("tensor", None),
            P(),
            P(),
            P(),
            P(None, "tensor"),
            P("tensor"),
            P("tensor", None),
            P(),
            P(),
            P(),
        ),
        check_vma=False,
    )
```

```python
import functools

import jax
import jax.numpy as jnp
from jax import lax
from jax.experimental import pallas as pl
from jax.experimental.pallas import tpu as pltpu
from jax.sharding import PartitionSpec as P

HD = 64
LANES = 128
NORM_EPS = 1e-05
MASK_BIG = 2.0**100
LOG2E = 1.4426950408889634
VMEM_BYTES = 58 * 2**20
BF = jnp.bfloat16
F32 = jnp.float32
VMEM = pl.BlockSpec(memory_space=pltpu.VMEM)
HBM = pl.BlockSpec(memory_space=pl.ANY)


def dot(left, right, left_dim, right_dim):
    return lax.dot_general(
        left, right, (((left_dim,), (right_dim,)), ((), ())), preferred_element_type=F32
    )


def params():
    return pltpu.CompilerParams(vmem_limit_bytes=VMEM_BYTES)


def cost(macs, moved):
    return pl.CostEstimate(flops=2 * macs, bytes_accessed=moved, transcendentals=0)


def values_columns(rows):
    lane = lax.broadcasted_iota(jnp.int32, (rows, LANES), 1)
    return jnp.where((lane == HD) | (lane == HD + 1), 1.0, 0.0)


def live_rows(place_ref, first, rows, columns=slice(None)):
    place = place_ref[:, columns]
    row = lax.broadcasted_iota(jnp.int32, (rows, place.shape[1]), 0) + first
    return jnp.where(row == place, 1.0, 0.0).astype(BF)


def key_value_block(x_ref, place_ref, bounds_ref, w_refs, bias_ref, x_out, k_ref, v_ref, first, rows, base=0):
    at, to = pl.ds(first, rows), pl.ds(base + first, rows)
    later = slice(first, None) if isinstance(first, int) else slice(None)
    x = dot(live_rows(place_ref, first, rows, later), x_ref[later, :], 1, 0).astype(BF)
    x_out[at, :] = x
    shard = w_refs[0].shape[2]
    row = lax.broadcasted_iota(jnp.int32, (rows, LANES), 0) + first
    extra_k = jnp.where((row >= bounds_ref[0:1, :]) & (row < bounds_ref[1:2, :]), 1.0, 0.0)
    extra_v = values_columns(rows)
    low = lax.broadcasted_iota(jnp.int32, (rows, LANES), 1) < HD
    for side, w_ref in enumerate(w_refs):
        mine = slice(side * shard, (side + 1) * shard)
        keys = dot(x, w_ref[1], 1, 0)
        values = dot(x, w_ref[2], 1, 0) + bias_ref[1:2, mine]
        for i in range(shard // HD):
            pair = slice((i // 2) * LANES, (i // 2 + 1) * LANES)
            k_pair, v_pair = keys[:, pair], values[:, pair]
            if i % 2:
                k_pair, v_pair = pltpu.roll(k_pair, HD, 1), pltpu.roll(v_pair, HD, 1)
            h = side * (shard // HD) + i
            k_ref[h, to, :] = jnp.where(low, k_pair, extra_k).astype(BF)
            v_ref[h, to, :] = jnp.where(low, v_pair, extra_v).astype(BF)


def project_kernel(x_ref, own_ref, oth_ref, bias_ref, place_ref, bounds_ref, extra_q_ref, k_ref, v_ref, x_out, qt_ref, q_ref):
    block = q_ref.shape[0]
    first = pl.multiple_of(pl.program_id(0) * block, block)
    shard = own_ref.shape[2]
    key_value_block(
        x_ref, place_ref, bounds_ref, (own_ref, oth_ref), bias_ref, x_out, k_ref, v_ref, first, block
    )
    x = x_ref[pl.ds(first, block), :]
    for side, w_ref in enumerate((own_ref, oth_ref)):
        mine = slice(side * shard, (side + 1) * shard)
        q = (dot(x, w_ref[0], 1, 0) + bias_ref[0:1, mine]).astype(BF)
        q_ref[:, mine] = q
        turned = q.T
        for i in range(shard // HD):
            h = side * (shard // HD) + i
            qt_ref[h, :HD, :] = turned[i * HD : (i + 1) * HD, :]
            qt_ref[h, HD:, :] = extra_q_ref[...]


def project(x, w_own, w_oth, bias, place, bounds, extra_q):
    tokens, width = x.shape
    heads = width // HD
    block = 256
    whole = lambda *shape: pl.BlockSpec(shape, lambda i: (0,) * len(shape))
    per_head = whole(heads, tokens, LANES)
    return pl.pallas_call(
        project_kernel,
        grid=(tokens // block,),
        out_shape=(
            jax.ShapeDtypeStruct((heads, tokens, LANES), BF),
            jax.ShapeDtypeStruct((heads, tokens, LANES), BF),
            jax.ShapeDtypeStruct((tokens, width), BF),
            jax.ShapeDtypeStruct((heads, LANES, tokens), BF),
            jax.ShapeDtypeStruct((tokens, width), BF),
        ),
        in_specs=[
            whole(*x.shape),
            whole(*w_own.shape),
            whole(*w_oth.shape),
            whole(*bias.shape),
            whole(*place.shape),
            whole(*bounds.shape),
            pl.BlockSpec((HD, block), lambda i: (0, i)),
        ],
        out_specs=(
            per_head,
            per_head,
            whole(tokens, width),
            pl.BlockSpec((heads, LANES, block), lambda i: (0, 0, i)),
            pl.BlockSpec((block, width), lambda i: (i, 0)),
        ),
        compiler_params=params(),
        cost_estimate=cost(5 * tokens * width * width, 12 * tokens * width),
        name="project",
    )(x, w_own, w_oth, bias, place, bounds, extra_q)


def key_sizes(keys):
    return (keys * 13 // 16, keys)


def for_size(live, keys, work):
    below = 0
    for n, size in enumerate(key_sizes(keys)):

        @pl.when((live > below) & (live <= size) if below else live <= size)
        def _():
            work(size, n > 0)

        below = size


def sweep(rolled, size, count, body, carry=0):
    rows = size // count
    if rolled:
        return lax.fori_loop(0, count, lambda i, held: body(pl.multiple_of(i * rows, rows), held), carry)
    for i in range(count):
        carry = body(i * rows, carry)
    return carry


def attend_kernel(
    count, chunk, live_ref, qt_hbm, k_hbm, v_hbm, x_ref, own_ref, oth_ref, bias_ref, place_ref, bounds_ref,
    p_hbm, ot_ref, linv_ref, k_oth_hbm, v_oth_hbm, x_oth_hbm,
    qt_ref, k_ref, v_ref, x1_ref,
    s0_scr, s1_scr, peak0_scr, peak1_scr, row_scr, acc_scr, p_scr, sem, in_sem, out_sem,
):
    heads, _, queries = qt_ref.shape
    half = x_ref.shape[0]
    parts = queries // chunk
    steps = heads * parts
    slots = p_scr.shape[0]

    def copies_in(h):
        return [
            pltpu.make_async_copy(src.at[h], dst, in_sem.at[h, n])
            for n, (src, dst) in enumerate(
                ((qt_hbm, qt_ref.at[h]), (k_hbm, k_ref.at[h, :half]), (v_hbm, v_ref.at[h, :half]))
            )
        ]

    for h in range(heads):
        for copy in copies_in(h):
            copy.start()

    def project_live(size, rolled):
        def block(first, carry):
            key_value_block(
                x_ref, place_ref, bounds_ref, (own_ref, oth_ref), bias_ref, x1_ref, k_ref, v_ref, first, size // count, half
            )
            return carry

        sweep(rolled, size, count, block)
        if size < half:
            x1_ref[size:, :] = jnp.zeros((half - size, x1_ref.shape[1]), BF)

    for_size(live_ref[1], half, project_live)

    copies_kv = [
        pltpu.make_async_copy(k_ref.at[:, half:, :], k_oth_hbm, out_sem.at[0]),
        pltpu.make_async_copy(v_ref.at[:, half:, :], v_oth_hbm, out_sem.at[1]),
        pltpu.make_async_copy(x1_ref, x_oth_hbm, out_sem.at[2]),
    ]
    for copy in copies_kv:
        copy.start()

    def columns(step):
        return pl.ds(pl.multiple_of(lax.rem(step, parts) * chunk, chunk), chunk)

    def copies_out(step, size):
        slot = lax.rem(step, slots)
        copies = []
        for part in range(2):
            rows = slice(part * half, part * half + size)
            to = p_hbm.at[step // parts, rows, columns(step)]
            copies.append(pltpu.make_async_copy(p_scr.at[slot, rows, :], to, sem.at[slot, part]))
        return copies

    def scores(step, s_ref, peak, rows):
        s = dot(k_ref[step // parts, rows, :], qt_ref[step // parts, :, columns(step)], 1, 0)
        s_ref[rows, :] = s
        return jnp.maximum(peak, jnp.max(s.reshape(-1, 8, chunk), axis=0))

    def mix(step, s_ref, rows):
        p = jnp.exp2((s_ref[rows, :] - row_scr[...]) * (LOG2E * HD**-0.5)).astype(BF)
        p_scr[lax.rem(step, slots), rows, :] = p
        return dot(v_ref[step // parts, rows, :], p, 0, 0)

    def over_keys(size, rolled, block, carry):
        if size == half:
            return sweep(rolled, 2 * half, 2 * count, lambda at, held: block(pl.ds(at, size // count), held), carry)
        for part in range(2):
            rows = lambda at, held: block(pl.ds(part * half + at, size // count), held)
            carry = sweep(rolled, size, count, rows, carry)
        return carry

    def run(size, rolled, step, s_ref, peak_ref, after, s_after, peak_after):
        row_scr[...] = jnp.max(peak_ref[...], axis=0, keepdims=True)

        @pl.when(step >= slots)
        def _():
            for copy in copies_out(step - slots, size):
                copy.wait()

        def block(rows, held):
            peak = scores(after, s_after, held[0], rows)
            return peak, held[1] + mix(step, s_ref, rows)

        start = (jnp.full((8, chunk), -jnp.inf, F32), jnp.zeros((LANES, chunk), F32))
        peak_after[...], acc_scr[...] = over_keys(size, rolled, block, start)
        for copy in copies_out(step, size):
            copy.start()
        inverse = 1.0 / acc_scr[HD : HD + 1, :]
        linv_ref[step // parts, :, columns(step)] = inverse
        ot_ref[step // parts, :, columns(step)] = acc_scr[:HD, :] * inverse

    for copy in copies_in(0):
        copy.wait()

    def work(size, rolled):
        def first_block(rows, peak):
            return scores(0, s0_scr, peak, rows)

        peak0_scr[...] = over_keys(size, rolled, first_block, jnp.full((8, chunk), -jnp.inf, F32))

        @pl.loop(0, steps // 2)
        def _(i):
            run(size, rolled, 2 * i, s0_scr, peak0_scr, 2 * i + 1, s1_scr, peak1_scr)
            after = 2 * i + 2

            @pl.when((after < steps) & (lax.rem(after, parts) == 0))
            def _():
                for copy in copies_in(after // parts):
                    copy.wait()

            run(size, rolled, 2 * i + 1, s1_scr, peak1_scr, jnp.minimum(after, steps - 1), s0_scr, peak0_scr)

        for slot in range(slots):
            for copy in copies_out(steps - slots + slot, size):
                copy.wait()

    for_size(live_ref[1], half, work)
    for copy in copies_kv:
        copy.wait()


def attend(live, qt, k_own, v_own, x_oth, w_own, w_oth, bias, place, bounds):
    heads, _, queries = qt.shape
    keys = 2 * queries
    count, chunk, slots = 4, 512, 4
    per_head = jax.ShapeDtypeStruct(k_own.shape, BF)
    return pl.pallas_call(
        functools.partial(attend_kernel, count, chunk),
        out_shape=(
            jax.ShapeDtypeStruct((heads, keys, queries), BF),
            jax.ShapeDtypeStruct((heads, HD, queries), F32),
            jax.ShapeDtypeStruct((heads, 1, queries), F32),
            per_head,
            per_head,
            jax.ShapeDtypeStruct(x_oth.shape, BF),
        ),
        in_specs=[pl.BlockSpec(memory_space=pltpu.SMEM)] + [HBM] * 3 + [VMEM] * 6,
        out_specs=(HBM, VMEM, VMEM, HBM, HBM, HBM),
        scratch_shapes=[
            pltpu.VMEM(qt.shape, BF),
            pltpu.VMEM((heads, keys, LANES), BF),
            pltpu.VMEM((heads, keys, LANES), BF),
            pltpu.VMEM(x_oth.shape, BF),
            pltpu.VMEM((keys, chunk), F32),
            pltpu.VMEM((keys, chunk), F32),
            pltpu.VMEM((8, chunk), F32),
            pltpu.VMEM((8, chunk), F32),
            pltpu.VMEM((1, chunk), F32),
            pltpu.VMEM((LANES, chunk), F32),
            pltpu.VMEM((slots, keys, chunk), BF),
            pltpu.SemaphoreType.DMA((slots, 2)),
            pltpu.SemaphoreType.DMA((heads, 3)),
            pltpu.SemaphoreType.DMA((3,)),
        ],
        compiler_params=params(),
        cost_estimate=cost(heads * keys * queries * 512, 2 * heads * keys * queries),
        name="attend",
    )(live, qt, k_own, v_own, x_oth, w_own, w_oth, bias, place, bounds)


def normalize(values):
    mean = jnp.mean(values, axis=-1, keepdims=True)
    centered = values - mean
    inverse = lax.rsqrt(jnp.mean(centered * centered, axis=-1, keepdims=True) + NORM_EPS)
    return centered * inverse, inverse


def norm_back(e, normed, inverse):
    return inverse * (
        e - jnp.mean(e, axis=-1, keepdims=True) - normed * jnp.mean(e * normed, axis=-1, keepdims=True)
    )


def middle_kernel(
    sub, x_ref, cot_ref, ot_ref, linv_ref, w_own_ref, w_oth_ref, vec_ref,
    act_ref, res_ref, dot_ref, dnat_ref, own_ref, oth_ref, small_ref,
    att_scr, w_out_ref, w_up_ref, w_down_ref, b_up_ref, gw_ref,
):
    block, width = x_ref.shape
    heads = width // HD
    shard = width // 2
    b_out, gain1, bias1, b_down, gain2, bias2 = (vec_ref[i : i + 1, :] for i in range(6))

    @pl.when(pl.program_id(0) == 0)
    def _():
        gw_ref[...] = jnp.zeros_like(gw_ref)
        small_ref[...] = jnp.zeros_like(small_ref)
        for side, ref in enumerate((w_own_ref, w_oth_ref)):
            mine = slice(side * shard, (side + 1) * shard)
            w_out_ref[mine, :] = ref[:shard, :]
            w_down_ref[mine, :] = ref[shard : 2 * shard, :]
            w_up_ref[:shard, mine] = ref[2 * shard : 3 * shard, :shard]
            w_up_ref[shard:, mine] = ref[2 * shard : 3 * shard, shard:]
            b_up_ref[:, mine] = ref[3 * shard : 3 * shard + 1, :shard].astype(F32)

    def col_sum(row, values):
        small_ref[row : row + 1, :] += jnp.sum(values, axis=0, keepdims=True)

    def chain(u):
        rows = slice(u * sub, (u + 1) * sub)
        for h in range(heads):
            att_scr[u, h * HD : (h + 1) * HD, :] = ot_ref[h, :, rows].astype(BF)
        branch = dot(att_scr[u], w_out_ref[...], 0, 0)
        yield
        n1, inv1 = normalize(x_ref[rows, :].astype(F32) + branch + b_out)
        first = n1 * gain1 + bias1
        first_low = first.astype(BF)
        yield
        pre = dot(first_low, w_up_ref[...], 1, 0) + b_up_ref[...]
        yield
        cdf = 0.5 * (1.0 + lax.erf(pre * 0.5**0.5))
        hidden = (pre * cdf).astype(BF)
        slope = cdf + pre * (0.3989422804014327 * jnp.exp(-0.5 * pre * pre))
        yield
        branch = dot(hidden, w_down_ref[...], 1, 0)
        yield
        n2, inv2 = normalize(first + branch + b_down)
        act_ref[rows, :] = (n2 * gain2 + bias2).astype(BF)
        cot = cot_ref[rows, :].astype(F32)
        two = norm_back(cot * gain2, n2, inv2)
        two_low = two.astype(BF)
        yield
        back = dot(two_low, w_down_ref[...], 1, 1)
        gw_ref[2] += dot(hidden, two_low, 0, 0)
        col_sum(3, two)
        col_sum(4, cot * n2)
        col_sum(5, cot)
        yield
        pre_grad = (back * slope).astype(BF)
        yield
        back = dot(pre_grad, w_up_ref[...], 1, 1)
        gw_ref[1] += dot(first_low, pre_grad, 0, 0)
        col_sum(6, pre_grad.astype(F32))
        yield
        one = two + back
        res = norm_back(one * gain1, n1, inv1)
        res_ref[rows, :] = res
        res_low = res.astype(BF)
        yield
        turned = dot(w_out_ref[...], res_low, 1, 1)
        gw_ref[0] += dot(att_scr[u], res_low, 1, 0)
        col_sum(1, one * n1)
        col_sum(2, one)
        col_sum(0, res)
        yield
        pick = lax.broadcasted_iota(jnp.int32, (HD, sub), 0)
        for h in range(heads):
            head = slice(h * HD, (h + 1) * HD)
            grad = (turned[head].astype(BF).astype(F32) * linv_ref[h, :, rows]).astype(BF)
            inner = -jnp.sum(grad.astype(F32) * ot_ref[h, :, rows], axis=0, keepdims=True)
            high = inner.astype(BF).astype(F32)
            dot_ref[h, :HD, rows] = grad
            dot_ref[h, HD:, rows] = jnp.where(pick == 0, high, jnp.where(pick == 1, inner - high, 0.0)).astype(BF)
            att_scr[u, head, :] = grad
        dnat_ref[rows, :] = att_scr[u].T
        yield

    for _ in zip(*(chain(u) for u in range(block // sub))):
        pass

    @pl.when(pl.program_id(0) == pl.num_programs(0) - 1)
    def _():
        for ref, mine in ((own_ref, slice(0, shard)), (oth_ref, slice(shard, width))):
            ref[:shard, :] = gw_ref[0, mine, :].astype(ref.dtype)
            ref[shard:width, :] = gw_ref[2, mine, :].astype(ref.dtype)
            ref[width:, :shard] = gw_ref[1, :shard, mine].astype(ref.dtype)
            ref[width:, shard:] = gw_ref[1, shard:, mine].astype(ref.dtype)


def middle(x, cot, ot, linv, w_own, w_oth, vectors):
    tokens, width = x.shape
    heads = width // HD
    block, sub = 512, 256
    whole = lambda *shape: pl.BlockSpec(shape, lambda i: (0,) * len(shape))
    rows = pl.BlockSpec((block, width), lambda i: (i, 0))
    columns = lambda n: pl.BlockSpec((heads, n, block), lambda i: (0, 0, i))
    square = pltpu.VMEM((width, width), BF)
    return pl.pallas_call(
        functools.partial(middle_kernel, sub),
        grid=(tokens // block,),
        out_shape=(
            jax.ShapeDtypeStruct((tokens, width), BF),
            jax.ShapeDtypeStruct((tokens, width), F32),
            jax.ShapeDtypeStruct((heads, LANES, tokens), BF),
            jax.ShapeDtypeStruct((tokens, width), BF),
            jax.ShapeDtypeStruct((3 * width // 2, width), F32),
            jax.ShapeDtypeStruct((3 * width // 2, width), BF),
            jax.ShapeDtypeStruct((8, width), F32),
        ),
        in_specs=[rows, rows, columns(HD), columns(1), whole(*w_own.shape), whole(*w_oth.shape), whole(*vectors.shape)],
        out_specs=(
            rows, rows, columns(LANES), rows,
            whole(3 * width // 2, width), whole(3 * width // 2, width), whole(8, width),
        ),
        scratch_shapes=[
            pltpu.VMEM((block // sub, width, sub), BF), square, square, square,
            pltpu.VMEM((1, width), F32), pltpu.VMEM((3, width, width), F32),
        ],
        compiler_params=params(),
        cost_estimate=cost(9 * tokens * width * width, 20 * tokens * width),
        name="middle",
    )(x, cot, ot, linv, w_own, w_oth, vectors)


def times_weights(grad, own_ref, oth_ref, third):
    shard = own_ref.shape[2]
    return dot(grad[:, :shard], own_ref[third], 1, 1) + dot(grad[:, shard:], oth_ref[third], 1, 1)


def backward_kernel(sub, part, *refs):
    if part:
        (live_ref, place_ref, p_hbm, dot_hbm, dnat_hbm, q_hbm, k_hbm, v_hbm, x_hbm, own_hbm, oth_hbm,
         dq_hbm, dx_ref, gw_ref, bias_ref,
         dot_ref, dnat_ref, q_ref, k_ref, v_ref, x_ref, own_ref, oth_ref,
         dq_ref, dk_ref, dv_ref, dx_scr, acc_scr, p_scr, sem, pair_sem, last_sem, out_sem) = refs
        more = ((own_hbm, own_ref), (oth_hbm, oth_ref))
    else:
        (live_ref, small_ref, value_ref,
         p_hbm, dot_hbm, dnat_hbm, q_hbm, k_hbm, v_hbm, x_hbm, dq_hbm, gw_hbm, whole_hbm,
         sent_ref, kept_ref, dq_out, dk_hbm, dv_hbm,
         dot_ref, dnat_ref, q_ref, k_ref, v_ref, x_ref, before_ref, gw_ref, whole_ref,
         dq_ref, dk_ref, dv_ref, gq_ref, bias_ref, acc_scr, p_scr, sem, pair_sem, last_sem, out_sem) = refs
        more = ((dq_hbm, before_ref), (gw_hbm, gw_ref), (whole_hbm, whole_ref))
    heads, _, queries = dot_ref.shape
    keys = k_ref.shape[1]
    width = heads * HD
    shard = width // 2
    slots = p_scr.shape[0]
    pairs = heads // 2

    def copy_in(p, j, size):
        block = size // 2
        slot = lax.rem(p * 2 + j, slots)
        first = part * keys + j * block
        if not isinstance(j, int):
            first = pl.multiple_of(first, 16)
        src = p_hbm.at[pl.ds(2 * p, 2), pl.ds(first, block), :]
        return pltpu.make_async_copy(src, p_scr.at[slot, :, :block, :], sem.at[slot])

    def pair_copies(p):
        pair = pl.ds(2 * p, 2)
        lanes = pl.ds(pl.multiple_of(p * LANES, LANES), LANES)
        by_head = ((dot_hbm, dot_ref), (k_hbm, k_ref), (v_hbm, v_ref))
        by_lane = ((dnat_hbm, dnat_ref), (q_hbm, q_ref))
        return [
            pltpu.make_async_copy(src.at[pair], dst.at[pair], pair_sem.at[p, n]) for n, (src, dst) in enumerate(by_head)
        ] + [
            pltpu.make_async_copy(src.at[:, lanes], dst.at[:, lanes], pair_sem.at[p, 3 + n])
            for n, (src, dst) in enumerate(by_lane)
        ]

    last = ((x_hbm, x_ref),) + more

    def rows_out(p):
        rows = pl.ds(pl.multiple_of(p * 2 * HD, 2 * HD), 2 * HD)
        return pltpu.make_async_copy(dq_ref.at[rows, :], dq_hbm.at[rows, :], out_sem.at[p])

    last_copies = [pltpu.make_async_copy(src, dst, last_sem.at[n]) for n, (src, dst) in enumerate(last)]

    for copy in pair_copies(0):
        copy.start()

    def work(size, rolled):
        block, rows = size // 2, size // 4
        low = lax.broadcasted_iota(jnp.int32, (rows, LANES), 1) < HD
        if size < keys:
            dk_ref[size:, :] = jnp.zeros((keys - size, width), BF)
            dv_ref[size:, :] = jnp.zeros((keys - size, width), BF)
        for step in range(slots - 1):
            copy_in(step // 2, step % 2, size).start()

        @pl.loop(0, pairs)
        def _(p):
            lanes = pl.ds(pl.multiple_of(p * LANES, LANES), LANES)
            for copy in pair_copies(p):
                copy.wait()

            @pl.when(p + 1 < pairs)
            def _():
                for copy in pair_copies(p + 1):
                    copy.start()

            @pl.when(p == 1)
            def _():
                for copy in last_copies:
                    copy.start()

            acc_scr[...] = jnp.zeros_like(acc_scr)

            def one_block(j):
                slot = lax.rem(p * 2 + j, slots)
                copy_in(p, j, size).wait()
                ahead = 2 * p + j + slots - 1

                @pl.when(ahead < 2 * pairs)
                def _():
                    copy_in(ahead // 2, lax.rem(ahead, 2), size).start()

                def at_rows(at, total):
                    here = pl.ds(pl.multiple_of(j * block + at, 16), rows)
                    total, dks, dvs = list(total), [], []
                    for side in range(2):
                        h = 2 * p + side
                        prob = p_scr[slot, side, pl.ds(at, rows), :]
                        slope = dot(v_ref[h, here, :], dot_ref[h], 1, 0)
                        dvs.append(dot(prob, dnat_ref[:, lanes], 1, 0))
                        ds = (prob.astype(F32) * slope).astype(BF)
                        dks.append(dot(ds, q_ref[:, lanes], 1, 0))
                        total[side] = total[side] + dot(k_ref[h, here, :], ds, 0, 0)
                    dk_ref[here, lanes] = (jnp.where(low, dks[0], dks[1]) * HD**-0.5).astype(BF)
                    dv_ref[here, lanes] = jnp.where(low, dvs[0], dvs[1]).astype(BF)
                    return tuple(total)

                zero = jnp.zeros((LANES, queries), F32)
                for side, total in enumerate(sweep(rolled, block, 2, at_rows, (zero, zero))):
                    acc_scr[side] += total

            pl.loop(0, 2)(one_block)

            for side in range(2):
                dq_ref[pl.ds(pl.multiple_of((2 * p + side) * HD, HD), HD), :] = acc_scr[side, :HD, :]
            if part:
                rows_out(p).start()

    for_size(live_ref[1], keys, work)
    for copy in last_copies:
        copy.wait()
    bias_ref[...] = jnp.zeros_like(bias_ref)
    if part:
        gw_ref[...] = jnp.zeros_like(gw_ref)
        copies_out = [rows_out(p) for p in range(heads // 2)]
    else:
        gq_ref[...] = jnp.zeros_like(gq_ref)
        copies_out = [
            pltpu.make_async_copy(dk_ref, dk_hbm, out_sem.at[0]),
            pltpu.make_async_copy(dv_ref, dv_hbm, out_sem.at[1]),
        ]
        for copy in copies_out:
            copy.start()

    def weight_sums(size, rolled):
        def at_rows(at, carry):
            rows = pl.ds(at, size // 4)
            x, dk, dv = x_ref[rows, :], dk_ref[rows, :], dv_ref[rows, :]
            gw_ref[0] += dot(x, dk, 0, 0)
            gw_ref[1] += dot(x, dv, 0, 0)
            bias_ref[1:2, :] += jnp.sum(dv.astype(F32), axis=0, keepdims=True)
            if part:
                dx = times_weights(dk, own_ref, oth_ref, 1) + times_weights(dv, own_ref, oth_ref, 2)
                dx_scr[rows, :] = dx.astype(BF)
            return carry

        def back_in_place(at, carry):
            rows = pl.ds(at, sub)
            earlier = size if rolled else min(at + sub, size)
            dx_ref[rows, :] = dot(live_rows(place_ref, 0, earlier, rows), dx_scr[:earlier, :], 0, 0).astype(BF)
            return carry

        sweep(True, size, 4, at_rows)
        if part:
            sweep(rolled, keys, keys // sub, back_in_place)

    for_size(live_ref[1], keys, weight_sums)
    if not part:

        @pl.loop(0, queries // sub)
        def _(i):
            rows = pl.ds(pl.multiple_of(i * sub, sub), sub)
            dq = ((before_ref[:, rows] + dq_ref[:, rows]) * HD**-0.5).astype(BF).T
            dq_out[rows, :] = dq
            gq_ref[...] += dot(whole_ref[rows, :], dq, 0, 0)
            bias_ref[0:1, :] += jnp.sum(dq.astype(F32), axis=0, keepdims=True)

    if not part:
        first = live_ref[0] == 0
        bias_ref[1:2, :] += value_ref[1:2, :]
        cut = 3 * width // 2
        for side in range(2):
            mine = slice(side * shard, (side + 1) * shard)
            pieces = [gq_ref[:, mine], gw_ref[0, :, mine], gw_ref[1, :, mine]]
            blocks = [piece[at : at + shard, :].astype(BF) for piece in pieces for at in (0, shard)]
            for n in range(3):
                to = slice(side * cut + n * shard, side * cut + (n + 1) * shard)
                kept_ref[to, :] = jnp.where(first, blocks[n], blocks[3 + n])
                sent_ref[to, :] = jnp.where(first, blocks[3 + n], blocks[n])
            rows16 = [small_ref[:6, :shard], small_ref[6:7, mine], bias_ref[0:1, mine]]
            rows16 += [small_ref[:6, shard:], jnp.zeros((1, shard), F32), bias_ref[1:2, mine]]
            value = jnp.concatenate(rows16, axis=0)
            high = value.astype(BF)
            for n, half in enumerate((high, (value - high.astype(F32)).astype(BF))):
                to = slice(2 * cut + (2 * side + n) * 16, 2 * cut + (2 * side + n + 1) * 16)
                kept_ref[to, :] = half
                sent_ref[to, :] = half

    for copy in copies_out:
        copy.wait()


def attend_backward(part, first, probs, dot_turned, dnat, q, k, v, x, *more):
    heads, keys, queries = probs.shape
    width = heads * HD
    sub, slots = 256, 4
    sums = jax.ShapeDtypeStruct((2, width, width), F32)
    turned = jax.ShapeDtypeStruct((width, queries), F32)
    grad = jax.ShapeDtypeStruct((queries, width), BF)
    inputs = (dot_turned, dnat, q, k, v, x) + more
    held = [pltpu.VMEM(a.shape, a.dtype) for a in inputs]
    held += [pltpu.VMEM(turned.shape, F32), pltpu.VMEM(grad.shape, BF), pltpu.VMEM(grad.shape, BF)]
    if part:
        out_shape = (turned, grad, sums, jax.ShapeDtypeStruct((2, width), F32))
        out_specs = (HBM, VMEM, VMEM, VMEM)
        held.append(pltpu.VMEM(grad.shape, BF))
    else:
        payload = jax.ShapeDtypeStruct((3 * width + 64, width // 2), BF)
        out_shape = (payload, payload, grad, grad, grad)
        out_specs = (VMEM, VMEM, VMEM, HBM, HBM)
        held += [pltpu.VMEM((width, width), F32), pltpu.VMEM((2, width), F32)]
    first_specs = [pl.BlockSpec(memory_space=pltpu.SMEM), VMEM, VMEM][: len(first)]
    return pl.pallas_call(
        functools.partial(backward_kernel, sub, part),
        out_shape=out_shape,
        in_specs=first_specs + [HBM] * (1 + len(inputs)),
        out_specs=out_specs,
        scratch_shapes=held
        + [
            pltpu.VMEM((2, LANES, queries), F32),
            pltpu.VMEM((slots, 2, keys // 4, queries), BF),
            pltpu.SemaphoreType.DMA((slots,)),
            pltpu.SemaphoreType.DMA((heads // 2, 5)),
            pltpu.SemaphoreType.DMA((1 + len(more),)),
            pltpu.SemaphoreType.DMA((heads // 2,)),
        ],
        compiler_params=params(),
        cost_estimate=cost(heads * keys * queries * 512, heads * keys * queries),
        name="attend_back_own" if not part else "attend_back_other",
    )(*first, probs, *inputs)


def input_kernel(res_ref, got_ref, dq_ref, dk_ref, dv_ref, own_ref, oth_ref, place_ref, dx_ref, live_scr):
    @pl.when(pl.program_id(0) == 0)
    def _():
        @pl.loop(0, live_scr.shape[0] // 256)
        def _(i):
            rows = pl.ds(pl.multiple_of(i * 256, 256), 256)
            live_scr[rows, :] = (
                times_weights(dk_ref[rows, :], own_ref, oth_ref, 1) + times_weights(dv_ref[rows, :], own_ref, oth_ref, 2)
            ).astype(BF)

    dx = res_ref[...] + got_ref[...].astype(F32) + times_weights(dq_ref[...], own_ref, oth_ref, 0)
    dx_ref[...] = dx + dot(live_rows(place_ref, 0, live_scr.shape[0]), live_scr[...], 0, 0)


def input_gradient(res, got, dq, dk, dv, w_own, w_oth, place):
    tokens, width = res.shape
    rows = pl.BlockSpec((256, width), lambda i: (i, 0))
    whole = lambda *shape: pl.BlockSpec(shape, lambda i: (0,) * len(shape))
    return pl.pallas_call(
        input_kernel,
        grid=(tokens // 256,),
        out_shape=jax.ShapeDtypeStruct((tokens, width), F32),
        in_specs=[rows] * 3 + [whole(*dk.shape)] * 2 + [whole(*w_own.shape)] * 2 + [pl.BlockSpec((1, 256), lambda i: (0, i))],
        out_specs=rows,
        scratch_shapes=[pltpu.VMEM(dk.shape, BF)],
        compiler_params=params(),
        cost_estimate=cost(3 * tokens * width * width, 16 * tokens * width),
        name="input_gradient",
    )(res, got, dq, dk, dv, w_own, w_oth, place)


def after(values, *others):
    return lax.optimization_barrier((values,) + others)[0]


def two_halves(values):
    high = values.astype(BF)
    return jnp.concatenate([high, (values - high.astype(F32)).astype(BF)], axis=0)


def one_value(halves):
    rows = halves.shape[0] // 2
    return halves[:rows].astype(F32) + halves[rows:].astype(F32)


def take(values, which):
    return lax.dynamic_index_in_dim(values, which, 0, False)


def in_order(mine, theirs, which):
    return jnp.concatenate([jnp.where(which == 0, mine, theirs), jnp.where(which == 0, theirs, mine)])


def sum_gradients(sent, kept, mid, input_grad, devices):
    index = lax.axis_index("dp")
    core, near = lax.rem(index, 2), lax.rem(index // 2, 2)
    rows = (sent.shape[0] - 64) // 2

    def across(values, bit):
        return lax.ppermute(values, "dp", [(i, i ^ bit) for i in range(devices)])

    got = across(sent, 1)
    halves = mid.reshape(2, mid.shape[0] // 2, -1)
    mid_got = across(take(halves, 1 - core).astype(BF), 1)
    total = kept[: 2 * rows].astype(F32) + got[: 2 * rows].astype(F32)
    small_own = one_value(kept[2 * rows : 2 * rows + 32]) + one_value(got[2 * rows : 2 * rows + 32])
    small_oth = one_value(kept[2 * rows + 32 :]) + one_value(got[2 * rows + 32 :])
    mid = (take(halves, core) + mid_got.astype(F32)).astype(BF)
    oth_two = two_halves(small_oth)
    mid_got = across(after(mid, oth_two), 4)
    result = input_grad(got)

    own_two = two_halves(small_own)
    got = lax.ppermute(jnp.concatenate([total[rows:].astype(BF), oth_two]), "tensor", [(0, 1), (1, 0)])
    total = total[:rows] + got[:rows].astype(F32)
    small = one_value(own_two) + one_value(got[rows:])

    halves = total.reshape(2, rows // 2, -1)
    two = two_halves(small)
    got = across(jnp.concatenate([take(halves, 1 - near).astype(BF), two]), 2)
    total = take(halves, near) + got[: rows // 2].astype(F32)
    small = one_value(two) + one_value(got[rows // 2 :])

    bit = 4
    while bit < devices:
        sent = jnp.concatenate([total.astype(BF), two_halves(small)])
        mid = (mid.astype(F32) + mid_got.astype(F32)).astype(BF)
        if 2 * bit < devices:
            mid_got = across(mid, 2 * bit)
        got = across(sent, bit)
        total = sent[: rows // 2].astype(F32) + got[: rows // 2].astype(F32)
        small = one_value(sent[rows // 2 :]) + one_value(got[rows // 2 :])
        bit *= 2
    mid = in_order(mid, across(mid, 1), core)
    mid = in_order(after(mid, got), after(across(mid, 2), got), near)

    total = total.astype(BF)
    total = in_order(total, across(total, 2), near)
    total = in_order(total, across(total, 1), core)
    return total.astype(F32), small, mid.astype(F32), result


def mask_parts(known, lengths, halves):
    tokens, slots = known.shape[0] // halves, lengths.shape[0]
    positions = jnp.arange(known.shape[0], dtype=jnp.int32)
    ends = jnp.cumsum(lengths)
    starts = ends - lengths
    inside = (positions[:, None] >= starts[None, :]) & (positions[:, None] < ends[None, :])
    opening = jnp.any((positions[:, None] == starts[None, :]) & (lengths[None, :] > 0), axis=1)
    live = ((known > 0) | opening).astype(jnp.int32).reshape(halves, 1, tokens)
    place = jnp.where(live > 0, jnp.cumsum(live, axis=2) - 1, -1)
    counts = jnp.sum(live, axis=2)
    before = lambda ats: jnp.sum(
        jnp.where(positions.reshape(halves, 1, tokens) < ats[None, :, None], live, 0), axis=2
    )
    past = jnp.full((halves, LANES - HD - slots - 1), tokens, jnp.int32)
    none = jnp.full((halves, HD), tokens, jnp.int32)
    low = jnp.concatenate([none, before(starts), counts, past], axis=1)
    high = jnp.concatenate([none, before(ends), jnp.full((halves, 1), tokens, jnp.int32), past], axis=1)
    queries = jnp.where(jnp.pad(inside, ((0, 0), (0, 1))), 0.0, -MASK_BIG)
    queries = jnp.pad(queries, ((0, 0), (0, HD - slots - 1))).T.astype(BF)
    return place, jnp.stack([low, high], axis=1), queries, jnp.max(counts)


def local(
    devices, layer_input, gene_known, cell_genes, w_qkv, bias_qv, w_out, b_out, ln1_gain, ln1_bias,
    w_up, b_up, w_down, b_down, ln2_gain, ln2_bias, cotangent,
):
    tokens, width = layer_input.shape
    shard = w_qkv.shape[2]
    side, index = lax.axis_index("tensor"), lax.axis_index("dp")
    core, near = lax.rem(index, 2), lax.rem(index // 2, 2)

    def swapped(values):
        return lax.ppermute(values, "tensor", [(0, 1), (1, 0)])

    def across(values, bit):
        return lax.ppermute(values, "dp", [(i, i ^ bit) for i in range(devices)])

    w_own = w_qkv.transpose(1, 0, 2)
    quarter = 3 * width // 4
    mine = lax.dynamic_slice_in_dim(w_own.reshape(3 * width, shard), (2 * core + near) * quarter, quarter, 0)
    got = swapped(jnp.concatenate([mine, jnp.pad(bias_qv, ((0, 14), (0, 0)))]))
    x_oth = swapped(layer_input)
    piece = got[:quarter]
    piece = in_order(piece, across(piece, 2), near)
    w_oth = in_order(piece, across(piece, 1), core).reshape(3, width, shard)
    bias = jnp.concatenate([bias_qv, got[quarter : quarter + 2]], axis=1).astype(F32)

    place, bounds, query_rows, most = mask_parts(gene_known, cell_genes[0], 2)
    query_own = lax.dynamic_slice_in_dim(query_rows, side * tokens, tokens, 1)
    place_own, place_oth, bounds_own, bounds_oth = take(place, side), take(place, 1 - side), take(bounds, side), take(bounds, 1 - side)
    live = jnp.stack([core, most])
    b_up_row = jnp.pad(b_up[None], ((0, 15), (0, shard)))
    mid_w = jnp.concatenate([w_out, w_down, jnp.concatenate([w_up[:shard], w_up[shard:]], axis=1), b_up_row])
    vectors = jnp.stack([b_out, ln1_gain, ln1_bias, b_down, ln2_gain, ln2_bias, b_out, b_out])

    k_own, v_own, x_live, qt, q = project(layer_input, w_own, w_oth, bias, place_own, bounds_own, query_own)
    x_oth, k_own, mid_w = lax.optimization_barrier((x_oth, k_own, mid_w))
    mid_w_oth = swapped(mid_w)
    probs, ot, linv, k_oth, v_oth, x_oth = attend(
        live, qt, k_own, v_own, x_oth, w_own, w_oth, bias, place_oth, bounds_oth
    )
    activations, res, dot_turned, dnat, mid_own, mid_oth, small = middle(
        layer_input, cotangent, ot, linv, mid_w, mid_w_oth, vectors
    )
    mid_got = swapped(mid_oth)
    dq, dx_oth, sums, value_grad = attend_backward(
        1, (live, place_oth), probs, dot_turned, dnat, q, k_oth, v_oth, x_oth, w_own, w_oth
    )
    mid_got, dq = lax.optimization_barrier((mid_got, dq))
    mid = (mid_own + mid_got.astype(F32)).reshape(2, 3 * shard // 2, width)
    mid_got = across(take(mid, 1 - near).astype(BF), 2)
    dx_got = swapped(dx_oth)
    sent, kept, dq, dk, dv = attend_backward(
        0, (live, small, value_grad), probs, dot_turned, dnat, q, k_own, v_own, x_live, dq, sums, layer_input
    )
    mid_got, dx_got, sent = lax.optimization_barrier((mid_got, dx_got, sent))
    mid = take(mid, near) + mid_got.astype(F32)

    def input_grad(token):
        return input_gradient(res, dx_got, after(dq, token), dk, dv, w_own, w_oth, place_own)

    qkv, small, mid, input_grad = sum_gradients(sent, kept, mid, input_grad, devices)
    qkv_g = qkv.reshape(3, width, shard).transpose(1, 0, 2)
    wide = jnp.concatenate([small[:6], small[8:14]], axis=1)
    up_g = jnp.concatenate([mid[width:, :shard], mid[width:, shard:]])
    return (
        activations, input_grad, qkv_g, jnp.stack([small[7], small[15]]), mid[:shard], wide[0], wide[1], wide[2],
        up_g, small[6], mid[shard:width], wide[3], wide[4], wide[5],
    )


def solution(mesh):
    placed = (
        P(("dp", "tensor"), None),
        P("dp"),
        P("dp", None),
        P(None, None, "tensor"),
        P(None, "tensor"),
        P("tensor", None),
        P(),
        P(),
        P(),
        P(None, "tensor"),
        P("tensor"),
        P("tensor", None),
        P(),
        P(),
        P(),
        P(("dp", "tensor"), None),
    )
    return jax.shard_map(
        functools.partial(local, mesh.shape["dp"]),
        mesh=mesh,
        in_specs=placed,
        out_specs=(
            P(("dp", "tensor"), None),
            P(("dp", "tensor"), None),
            P(None, None, "tensor"),
            P(None, "tensor"),
            P("tensor", None),
            P(),
            P(),
            P(),
            P(None, "tensor"),
            P("tensor"),
            P("tensor", None),
            P(),
            P(),
            P(),
        ),
        check_vma=False,
    )
```

```python
import functools

import jax
import jax.numpy as jnp
from jax import lax
from jax.experimental import pallas as pl
from jax.experimental.pallas import tpu as pltpu
from jax.sharding import PartitionSpec as P

HD = 64
LANES = 128
NORM_EPS = 1e-05
MASK_BIG = 2.0**100
LOG2E = 1.4426950408889634
VMEM_BYTES = 58 * 2**20
BF = jnp.bfloat16
F32 = jnp.float32
VMEM = pl.BlockSpec(memory_space=pltpu.VMEM)
HBM = pl.BlockSpec(memory_space=pl.ANY)


def dot(left, right, left_dim, right_dim):
    return lax.dot_general(
        left, right, (((left_dim,), (right_dim,)), ((), ())), preferred_element_type=F32
    )


def params():
    return pltpu.CompilerParams(vmem_limit_bytes=VMEM_BYTES)


def cost(macs, moved):
    return pl.CostEstimate(flops=2 * macs, bytes_accessed=moved, transcendentals=0)


def values_columns(rows):
    lane = lax.broadcasted_iota(jnp.int32, (rows, LANES), 1)
    return jnp.where((lane == HD) | (lane == HD + 1), 1.0, 0.0)


def live_rows(place_ref, first, rows, columns=slice(None)):
    place = place_ref[:, columns]
    row = lax.broadcasted_iota(jnp.int32, (rows, place.shape[1]), 0) + first
    return jnp.where(row == place, 1.0, 0.0).astype(BF)


def key_value_block(x_ref, place_ref, bounds_ref, w_refs, bias_ref, x_out, k_ref, v_ref, first, rows, base=0):
    at, to = pl.ds(first, rows), pl.ds(base + first, rows)
    later = slice(first, None) if isinstance(first, int) else slice(None)
    x = dot(live_rows(place_ref, first, rows, later), x_ref[later, :], 1, 0).astype(BF)
    x_out[at, :] = x
    shard = w_refs[0].shape[2]
    row = lax.broadcasted_iota(jnp.int32, (rows, LANES), 0) + first
    extra_k = jnp.where((row >= bounds_ref[0:1, :]) & (row < bounds_ref[1:2, :]), 1.0, 0.0)
    extra_v = values_columns(rows)
    low = lax.broadcasted_iota(jnp.int32, (rows, LANES), 1) < HD
    for side, w_ref in enumerate(w_refs):
        mine = slice(side * shard, (side + 1) * shard)
        keys = dot(x, w_ref[1], 1, 0)
        values = dot(x, w_ref[2], 1, 0) + bias_ref[1:2, mine]
        for i in range(shard // HD):
            pair = slice((i // 2) * LANES, (i // 2 + 1) * LANES)
            k_pair, v_pair = keys[:, pair], values[:, pair]
            if i % 2:
                k_pair, v_pair = pltpu.roll(k_pair, HD, 1), pltpu.roll(v_pair, HD, 1)
            h = side * (shard // HD) + i
            k_ref[h, to, :] = jnp.where(low, k_pair, extra_k).astype(BF)
            v_ref[h, to, :] = jnp.where(low, v_pair, extra_v).astype(BF)


def project_kernel(x_ref, own_ref, oth_ref, bias_ref, place_ref, bounds_ref, extra_q_ref, k_ref, v_ref, x_out, qt_ref, q_ref):
    block = q_ref.shape[0]
    first = pl.multiple_of(pl.program_id(0) * block, block)
    shard = own_ref.shape[2]
    key_value_block(
        x_ref, place_ref, bounds_ref, (own_ref, oth_ref), bias_ref, x_out, k_ref, v_ref, first, block
    )
    x = x_ref[pl.ds(first, block), :]
    for side, w_ref in enumerate((own_ref, oth_ref)):
        mine = slice(side * shard, (side + 1) * shard)
        q = (dot(x, w_ref[0], 1, 0) + bias_ref[0:1, mine]).astype(BF)
        q_ref[:, mine] = q
        turned = q.T
        for i in range(shard // HD):
            h = side * (shard // HD) + i
            qt_ref[h, :HD, :] = turned[i * HD : (i + 1) * HD, :]
            qt_ref[h, HD:, :] = extra_q_ref[...]


def project(x, w_own, w_oth, bias, place, bounds, extra_q):
    tokens, width = x.shape
    heads = width // HD
    block = 256
    whole = lambda *shape: pl.BlockSpec(shape, lambda i: (0,) * len(shape))
    per_head = whole(heads, tokens, LANES)
    return pl.pallas_call(
        project_kernel,
        grid=(tokens // block,),
        out_shape=(
            jax.ShapeDtypeStruct((heads, tokens, LANES), BF),
            jax.ShapeDtypeStruct((heads, tokens, LANES), BF),
            jax.ShapeDtypeStruct((tokens, width), BF),
            jax.ShapeDtypeStruct((heads, LANES, tokens), BF),
            jax.ShapeDtypeStruct((tokens, width), BF),
        ),
        in_specs=[
            whole(*x.shape),
            whole(*w_own.shape),
            whole(*w_oth.shape),
            whole(*bias.shape),
            whole(*place.shape),
            whole(*bounds.shape),
            pl.BlockSpec((HD, block), lambda i: (0, i)),
        ],
        out_specs=(
            per_head,
            per_head,
            whole(tokens, width),
            pl.BlockSpec((heads, LANES, block), lambda i: (0, 0, i)),
            pl.BlockSpec((block, width), lambda i: (i, 0)),
        ),
        compiler_params=params(),
        cost_estimate=cost(5 * tokens * width * width, 12 * tokens * width),
        name="project",
    )(x, w_own, w_oth, bias, place, bounds, extra_q)


def key_sizes(keys):
    return (keys * 13 // 16, keys)


def for_size(live, keys, work):
    below = 0
    for n, size in enumerate(key_sizes(keys)):

        @pl.when((live > below) & (live <= size) if below else live <= size)
        def _():
            work(size, n > 0)

        below = size


def sweep(rolled, size, count, body, carry=0):
    rows = size // count
    if rolled:
        return lax.fori_loop(0, count, lambda i, held: body(pl.multiple_of(i * rows, rows), held), carry)
    for i in range(count):
        carry = body(i * rows, carry)
    return carry


def attend_kernel(
    count, chunk, live_ref, qt_hbm, k_hbm, v_hbm, x_ref, own_ref, oth_ref, bias_ref, place_ref, bounds_ref,
    p_hbm, ot_ref, linv_ref, k_oth_hbm, v_oth_hbm, x_oth_hbm,
    qt_ref, k_ref, v_ref, x1_ref,
    s0_scr, s1_scr, peak0_scr, peak1_scr, row_scr, acc_scr, p_scr, sem, in_sem, out_sem,
):
    heads, _, queries = qt_ref.shape
    half = x_ref.shape[0]
    parts = queries // chunk
    steps = heads * parts
    slots = p_scr.shape[0]

    def copies_in(h):
        return [
            pltpu.make_async_copy(src.at[h], dst, in_sem.at[h, n])
            for n, (src, dst) in enumerate(
                ((qt_hbm, qt_ref.at[h]), (k_hbm, k_ref.at[h, :half]), (v_hbm, v_ref.at[h, :half]))
            )
        ]

    for h in range(heads):
        for copy in copies_in(h):
            copy.start()

    def project_live(size, rolled):
        def block(first, carry):
            key_value_block(
                x_ref, place_ref, bounds_ref, (own_ref, oth_ref), bias_ref, x1_ref, k_ref, v_ref, first, size // count, half
            )
            return carry

        sweep(rolled, size, count, block)
        if size < half:
            x1_ref[size:, :] = jnp.zeros((half - size, x1_ref.shape[1]), BF)

    for_size(live_ref[1], half, project_live)

    copies_kv = [
        pltpu.make_async_copy(k_ref.at[:, half:, :], k_oth_hbm, out_sem.at[0]),
        pltpu.make_async_copy(v_ref.at[:, half:, :], v_oth_hbm, out_sem.at[1]),
        pltpu.make_async_copy(x1_ref, x_oth_hbm, out_sem.at[2]),
    ]
    for copy in copies_kv:
        copy.start()

    def columns(step):
        return pl.ds(pl.multiple_of(lax.rem(step, parts) * chunk, chunk), chunk)

    def copies_out(step, size):
        slot = lax.rem(step, slots)
        copies = []
        for part in range(2):
            rows = slice(part * half, part * half + size)
            to = p_hbm.at[step // parts, rows, columns(step)]
            copies.append(pltpu.make_async_copy(p_scr.at[slot, rows, :], to, sem.at[slot, part]))
        return copies

    def scores(step, s_ref, peak, rows):
        s = dot(k_ref[step // parts, rows, :], qt_ref[step // parts, :, columns(step)], 1, 0)
        s_ref[rows, :] = s
        return jnp.maximum(peak, jnp.max(s.reshape(-1, 8, chunk), axis=0))

    def mix(step, s_ref, rows):
        p = jnp.exp2((s_ref[rows, :] - row_scr[...]) * (LOG2E * HD**-0.5)).astype(BF)
        p_scr[lax.rem(step, slots), rows, :] = p
        return dot(v_ref[step // parts, rows, :], p, 0, 0)

    def over_keys(size, rolled, block, carry):
        if size == half:
            return sweep(rolled, 2 * half, 2 * count, lambda at, held: block(pl.ds(at, size // count), held), carry)
        for part in range(2):
            rows = lambda at, held: block(pl.ds(part * half + at, size // count), held)
            carry = sweep(rolled, size, count, rows, carry)
        return carry

    def run(size, rolled, step, s_ref, peak_ref, after, s_after, peak_after):
        row_scr[...] = jnp.max(peak_ref[...], axis=0, keepdims=True)

        @pl.when(step >= slots)
        def _():
            for copy in copies_out(step - slots, size):
                copy.wait()

        def block(rows, held):
            peak = scores(after, s_after, held[0], rows)
            return peak, held[1] + mix(step, s_ref, rows)

        start = (jnp.full((8, chunk), -jnp.inf, F32), jnp.zeros((LANES, chunk), F32))
        peak_after[...], acc_scr[...] = over_keys(size, rolled, block, start)
        for copy in copies_out(step, size):
            copy.start()
        inverse = 1.0 / acc_scr[HD : HD + 1, :]
        linv_ref[step // parts, :, columns(step)] = inverse
        ot_ref[step // parts, :, columns(step)] = acc_scr[:HD, :] * inverse

    for copy in copies_in(0):
        copy.wait()

    def work(size, rolled):
        def first_block(rows, peak):
            return scores(0, s0_scr, peak, rows)

        peak0_scr[...] = over_keys(size, rolled, first_block, jnp.full((8, chunk), -jnp.inf, F32))

        @pl.loop(0, steps // 2)
        def _(i):
            run(size, rolled, 2 * i, s0_scr, peak0_scr, 2 * i + 1, s1_scr, peak1_scr)
            after = 2 * i + 2

            @pl.when((after < steps) & (lax.rem(after, parts) == 0))
            def _():
                for copy in copies_in(after // parts):
                    copy.wait()

            run(size, rolled, 2 * i + 1, s1_scr, peak1_scr, jnp.minimum(after, steps - 1), s0_scr, peak0_scr)

        for slot in range(slots):
            for copy in copies_out(steps - slots + slot, size):
                copy.wait()

    for_size(live_ref[1], half, work)
    for copy in copies_kv:
        copy.wait()


def attend(live, qt, k_own, v_own, x_oth, w_own, w_oth, bias, place, bounds):
    heads, _, queries = qt.shape
    keys = 2 * queries
    count, chunk, slots = 4, 512, 4
    per_head = jax.ShapeDtypeStruct(k_own.shape, BF)
    return pl.pallas_call(
        functools.partial(attend_kernel, count, chunk),
        out_shape=(
            jax.ShapeDtypeStruct((heads, keys, queries), BF),
            jax.ShapeDtypeStruct((heads, HD, queries), F32),
            jax.ShapeDtypeStruct((heads, 1, queries), F32),
            per_head,
            per_head,
            jax.ShapeDtypeStruct(x_oth.shape, BF),
        ),
        in_specs=[pl.BlockSpec(memory_space=pltpu.SMEM)] + [HBM] * 3 + [VMEM] * 6,
        out_specs=(HBM, VMEM, VMEM, HBM, HBM, HBM),
        scratch_shapes=[
            pltpu.VMEM(qt.shape, BF),
            pltpu.VMEM((heads, keys, LANES), BF),
            pltpu.VMEM((heads, keys, LANES), BF),
            pltpu.VMEM(x_oth.shape, BF),
            pltpu.VMEM((keys, chunk), F32),
            pltpu.VMEM((keys, chunk), F32),
            pltpu.VMEM((8, chunk), F32),
            pltpu.VMEM((8, chunk), F32),
            pltpu.VMEM((1, chunk), F32),
            pltpu.VMEM((LANES, chunk), F32),
            pltpu.VMEM((slots, keys, chunk), BF),
            pltpu.SemaphoreType.DMA((slots, 2)),
            pltpu.SemaphoreType.DMA((heads, 3)),
            pltpu.SemaphoreType.DMA((3,)),
        ],
        compiler_params=params(),
        cost_estimate=cost(heads * keys * queries * 512, 2 * heads * keys * queries),
        name="attend",
    )(live, qt, k_own, v_own, x_oth, w_own, w_oth, bias, place, bounds)


def normalize(values):
    mean = jnp.mean(values, axis=-1, keepdims=True)
    centered = values - mean
    inverse = lax.rsqrt(jnp.mean(centered * centered, axis=-1, keepdims=True) + NORM_EPS)
    return centered * inverse, inverse


def norm_back(e, normed, inverse):
    return inverse * (
        e - jnp.mean(e, axis=-1, keepdims=True) - normed * jnp.mean(e * normed, axis=-1, keepdims=True)
    )


def middle_kernel(
    sub, x_ref, cot_ref, ot_ref, linv_ref, w_own_ref, w_oth_ref, vec_ref,
    act_ref, res_ref, dot_ref, dnat_ref, own_ref, oth_ref, small_ref,
    att_scr, w_out_ref, w_up_ref, w_down_ref, b_up_ref, gw_ref,
):
    block, width = x_ref.shape
    heads = width // HD
    shard = width // 2
    b_out, gain1, bias1, b_down, gain2, bias2 = (vec_ref[i : i + 1, :] for i in range(6))

    @pl.when(pl.program_id(0) == 0)
    def _():
        gw_ref[...] = jnp.zeros_like(gw_ref)
        small_ref[...] = jnp.zeros_like(small_ref)
        for side, ref in enumerate((w_own_ref, w_oth_ref)):
            mine = slice(side * shard, (side + 1) * shard)
            w_out_ref[mine, :] = ref[:shard, :]
            w_down_ref[mine, :] = ref[shard : 2 * shard, :]
            w_up_ref[:shard, mine] = ref[2 * shard : 3 * shard, :shard]
            w_up_ref[shard:, mine] = ref[2 * shard : 3 * shard, shard:]
            b_up_ref[:, mine] = ref[3 * shard : 3 * shard + 1, :shard].astype(F32)

    def col_sum(row, values):
        small_ref[row : row + 1, :] += jnp.sum(values, axis=0, keepdims=True)

    def chain(u):
        rows = slice(u * sub, (u + 1) * sub)
        for h in range(heads):
            att_scr[u, h * HD : (h + 1) * HD, :] = ot_ref[h, :, rows].astype(BF)
        branch = dot(att_scr[u], w_out_ref[...], 0, 0)
        yield
        n1, inv1 = normalize(x_ref[rows, :].astype(F32) + branch + b_out)
        first = n1 * gain1 + bias1
        first_low = first.astype(BF)
        yield
        pre = dot(first_low, w_up_ref[...], 1, 0) + b_up_ref[...]
        yield
        cdf = 0.5 * (1.0 + lax.erf(pre * 0.5**0.5))
        hidden = (pre * cdf).astype(BF)
        slope = cdf + pre * (0.3989422804014327 * jnp.exp(-0.5 * pre * pre))
        yield
        branch = dot(hidden, w_down_ref[...], 1, 0)
        yield
        n2, inv2 = normalize(first + branch + b_down)
        act_ref[rows, :] = (n2 * gain2 + bias2).astype(BF)
        cot = cot_ref[rows, :].astype(F32)
        two = norm_back(cot * gain2, n2, inv2)
        two_low = two.astype(BF)
        yield
        back = dot(two_low, w_down_ref[...], 1, 1)
        gw_ref[2] += dot(hidden, two_low, 0, 0)
        col_sum(3, two)
        col_sum(4, cot * n2)
        col_sum(5, cot)
        yield
        pre_grad = (back * slope).astype(BF)
        yield
        back = dot(pre_grad, w_up_ref[...], 1, 1)
        gw_ref[1] += dot(first_low, pre_grad, 0, 0)
        col_sum(6, pre_grad.astype(F32))
        yield
        one = two + back
        res = norm_back(one * gain1, n1, inv1)
        res_ref[rows, :] = res
        res_low = res.astype(BF)
        yield
        turned = dot(w_out_ref[...], res_low, 1, 1)
        gw_ref[0] += dot(att_scr[u], res_low, 1, 0)
        col_sum(1, one * n1)
        col_sum(2, one)
        col_sum(0, res)
        yield
        pick = lax.broadcasted_iota(jnp.int32, (HD, sub), 0)
        for h in range(heads):
            head = slice(h * HD, (h + 1) * HD)
            grad = (turned[head].astype(BF).astype(F32) * linv_ref[h, :, rows]).astype(BF)
            inner = -jnp.sum(grad.astype(F32) * ot_ref[h, :, rows], axis=0, keepdims=True)
            high = inner.astype(BF).astype(F32)
            dot_ref[h, :HD, rows] = grad
            dot_ref[h, HD:, rows] = jnp.where(pick == 0, high, jnp.where(pick == 1, inner - high, 0.0)).astype(BF)
            att_scr[u, head, :] = grad
        dnat_ref[rows, :] = att_scr[u].T
        yield

    for _ in zip(*(chain(u) for u in range(block // sub))):
        pass

    @pl.when(pl.program_id(0) == pl.num_programs(0) - 1)
    def _():
        for ref, mine in ((own_ref, slice(0, shard)), (oth_ref, slice(shard, width))):
            ref[:shard, :] = gw_ref[0, mine, :].astype(ref.dtype)
            ref[shard:width, :] = gw_ref[2, mine, :].astype(ref.dtype)
            ref[width:, :shard] = gw_ref[1, :shard, mine].astype(ref.dtype)
            ref[width:, shard:] = gw_ref[1, shard:, mine].astype(ref.dtype)


def middle(x, cot, ot, linv, w_own, w_oth, vectors):
    tokens, width = x.shape
    heads = width // HD
    block, sub = 512, 256
    whole = lambda *shape: pl.BlockSpec(shape, lambda i: (0,) * len(shape))
    rows = pl.BlockSpec((block, width), lambda i: (i, 0))
    columns = lambda n: pl.BlockSpec((heads, n, block), lambda i: (0, 0, i))
    square = pltpu.VMEM((width, width), BF)
    return pl.pallas_call(
        functools.partial(middle_kernel, sub),
        grid=(tokens // block,),
        out_shape=(
            jax.ShapeDtypeStruct((tokens, width), BF),
            jax.ShapeDtypeStruct((tokens, width), F32),
            jax.ShapeDtypeStruct((heads, LANES, tokens), BF),
            jax.ShapeDtypeStruct((tokens, width), BF),
            jax.ShapeDtypeStruct((3 * width // 2, width), F32),
            jax.ShapeDtypeStruct((3 * width // 2, width), BF),
            jax.ShapeDtypeStruct((8, width), F32),
        ),
        in_specs=[rows, rows, columns(HD), columns(1), whole(*w_own.shape), whole(*w_oth.shape), whole(*vectors.shape)],
        out_specs=(
            rows, rows, columns(LANES), rows,
            whole(3 * width // 2, width), whole(3 * width // 2, width), whole(8, width),
        ),
        scratch_shapes=[
            pltpu.VMEM((block // sub, width, sub), BF), square, square, square,
            pltpu.VMEM((1, width), F32), pltpu.VMEM((3, width, width), F32),
        ],
        compiler_params=params(),
        cost_estimate=cost(9 * tokens * width * width, 20 * tokens * width),
        name="middle",
    )(x, cot, ot, linv, w_own, w_oth, vectors)


def times_weights(grad, own_ref, oth_ref, third):
    shard = own_ref.shape[2]
    return dot(grad[:, :shard], own_ref[third], 1, 1) + dot(grad[:, shard:], oth_ref[third], 1, 1)


def backward_kernel(sub, part, *refs):
    if part:
        (live_ref, place_ref, p_hbm, dot_hbm, dnat_hbm, q_hbm, k_hbm, v_hbm, x_hbm, own_hbm, oth_hbm,
         dq_hbm, dx_ref, gw_ref, bias_ref,
         dot_ref, dnat_ref, q_ref, k_ref, v_ref, x_ref, own_ref, oth_ref,
         dq_ref, dk_ref, dv_ref, dx_scr, acc_scr, p_scr, sem, pair_sem, last_sem, out_sem) = refs
        more = ((own_hbm, own_ref), (oth_hbm, oth_ref))
    else:
        (live_ref, small_ref, value_ref,
         p_hbm, dot_hbm, dnat_hbm, q_hbm, k_hbm, v_hbm, x_hbm, dq_hbm, gw_hbm, whole_hbm,
         sent_ref, kept_ref, dq_out, dk_hbm, dv_hbm,
         dot_ref, dnat_ref, q_ref, k_ref, v_ref, x_ref, before_ref, gw_ref, whole_ref,
         dq_ref, dk_ref, dv_ref, gq_ref, bias_ref, acc_scr, p_scr, sem, pair_sem, last_sem, out_sem) = refs
        more = ((dq_hbm, before_ref), (gw_hbm, gw_ref), (whole_hbm, whole_ref))
    heads, _, queries = dot_ref.shape
    keys = k_ref.shape[1]
    width = heads * HD
    shard = width // 2
    slots = p_scr.shape[0]
    pairs = heads // 2

    def copy_in(p, j, size):
        block = size // 2
        slot = lax.rem(p * 2 + j, slots)
        first = part * keys + j * block
        if not isinstance(j, int):
            first = pl.multiple_of(first, 16)
        src = p_hbm.at[pl.ds(2 * p, 2), pl.ds(first, block), :]
        return pltpu.make_async_copy(src, p_scr.at[slot, :, :block, :], sem.at[slot])

    def pair_copies(p):
        pair = pl.ds(2 * p, 2)
        lanes = pl.ds(pl.multiple_of(p * LANES, LANES), LANES)
        by_head = ((dot_hbm, dot_ref), (k_hbm, k_ref), (v_hbm, v_ref))
        by_lane = ((dnat_hbm, dnat_ref), (q_hbm, q_ref))
        return [
            pltpu.make_async_copy(src.at[pair], dst.at[pair], pair_sem.at[p, n]) for n, (src, dst) in enumerate(by_head)
        ] + [
            pltpu.make_async_copy(src.at[:, lanes], dst.at[:, lanes], pair_sem.at[p, 3 + n])
            for n, (src, dst) in enumerate(by_lane)
        ]

    last = ((x_hbm, x_ref),) + more

    def rows_out(p):
        rows = pl.ds(pl.multiple_of(p * 2 * HD, 2 * HD), 2 * HD)
        return pltpu.make_async_copy(dq_ref.at[rows, :], dq_hbm.at[rows, :], out_sem.at[p])

    last_copies = [pltpu.make_async_copy(src, dst, last_sem.at[n]) for n, (src, dst) in enumerate(last)]

    for copy in pair_copies(0):
        copy.start()

    def work(size, rolled):
        block, rows = size // 2, size // 4
        low = lax.broadcasted_iota(jnp.int32, (rows, LANES), 1) < HD
        if size < keys:
            dk_ref[size:, :] = jnp.zeros((keys - size, width), BF)
            dv_ref[size:, :] = jnp.zeros((keys - size, width), BF)
        for step in range(slots - 1):
            copy_in(step // 2, step % 2, size).start()

        @pl.loop(0, pairs)
        def _(p):
            lanes = pl.ds(pl.multiple_of(p * LANES, LANES), LANES)
            for copy in pair_copies(p):
                copy.wait()

            @pl.when(p + 1 < pairs)
            def _():
                for copy in pair_copies(p + 1):
                    copy.start()

            @pl.when(p == 1)
            def _():
                for copy in last_copies:
                    copy.start()

            acc_scr[...] = jnp.zeros_like(acc_scr)

            def one_block(j):
                slot = lax.rem(p * 2 + j, slots)
                copy_in(p, j, size).wait()
                ahead = 2 * p + j + slots - 1

                @pl.when(ahead < 2 * pairs)
                def _():
                    copy_in(ahead // 2, lax.rem(ahead, 2), size).start()

                def at_rows(at, total):
                    here = pl.ds(pl.multiple_of(j * block + at, 16), rows)
                    total, dks, dvs = list(total), [], []
                    for side in range(2):
                        h = 2 * p + side
                        prob = p_scr[slot, side, pl.ds(at, rows), :]
                        slope = dot(v_ref[h, here, :], dot_ref[h], 1, 0)
                        dvs.append(dot(prob, dnat_ref[:, lanes], 1, 0))
                        ds = (prob.astype(F32) * slope).astype(BF)
                        dks.append(dot(ds, q_ref[:, lanes], 1, 0))
                        total[side] = total[side] + dot(k_ref[h, here, :], ds, 0, 0)
                    dk_ref[here, lanes] = (jnp.where(low, dks[0], dks[1]) * HD**-0.5).astype(BF)
                    dv_ref[here, lanes] = jnp.where(low, dvs[0], dvs[1]).astype(BF)
                    return tuple(total)

                zero = jnp.zeros((LANES, queries), F32)
                for side, total in enumerate(sweep(rolled, block, 2, at_rows, (zero, zero))):
                    acc_scr[side] += total

            pl.loop(0, 2)(one_block)

            for side in range(2):
                dq_ref[pl.ds(pl.multiple_of((2 * p + side) * HD, HD), HD), :] = acc_scr[side, :HD, :]
            if part:
                rows_out(p).start()

    for_size(live_ref[1], keys, work)
    for copy in last_copies:
        copy.wait()
    if part:
        copies_out = [rows_out(p) for p in range(heads // 2)]
    else:
        copies_out = [
            pltpu.make_async_copy(dk_ref, dk_hbm, out_sem.at[0]),
            pltpu.make_async_copy(dv_ref, dv_hbm, out_sem.at[1]),
        ]
        for copy in copies_out:
            copy.start()

    for n, grad_ref in enumerate((dk_ref, dv_ref)):
        grad = dot(x_ref[...], grad_ref[...], 0, 0)
        gw_ref[n] = grad if part else gw_ref[n] + grad
    bias_ref[1:2, :] = jnp.sum(dv_ref[...].astype(F32), axis=0, keepdims=True)
    if part:
        bias_ref[0:1, :] = jnp.zeros((1, width), F32)

        @pl.loop(0, keys // sub)
        def _(i):
            rows = pl.ds(pl.multiple_of(i * sub, sub), sub)
            dk, dv = dk_ref[rows, :], dv_ref[rows, :]
            dx = times_weights(dk, own_ref, oth_ref, 1) + times_weights(dv, own_ref, oth_ref, 2)
            dx_scr[rows, :] = dx.astype(BF)

        for at in range(0, keys, sub):
            rows, earlier = slice(at, at + sub), at + sub
            dx_ref[rows, :] = dot(live_rows(place_ref, 0, earlier, rows), dx_scr[:earlier, :], 0, 0).astype(BF)
    else:
        dq_out[...] = ((before_ref[...] + dq_ref[...]) * HD**-0.5).astype(BF).T
        gq_ref[...] = dot(whole_ref[...], dq_out[...], 0, 0)
        bias_ref[0:1, :] = jnp.sum(dq_out[...].astype(F32), axis=0, keepdims=True)

    if not part:
        first = live_ref[0] == 0
        bias_ref[1:2, :] += value_ref[1:2, :]
        cut = 3 * width // 2
        for side in range(2):
            mine = slice(side * shard, (side + 1) * shard)
            pieces = [gq_ref[:, mine], gw_ref[0, :, mine], gw_ref[1, :, mine]]
            blocks = [piece[at : at + shard, :].astype(BF) for piece in pieces for at in (0, shard)]
            for n in range(3):
                to = slice(side * cut + n * shard, side * cut + (n + 1) * shard)
                kept_ref[to, :] = jnp.where(first, blocks[n], blocks[3 + n])
                sent_ref[to, :] = jnp.where(first, blocks[3 + n], blocks[n])
            rows16 = [small_ref[:6, :shard], small_ref[6:7, mine], bias_ref[0:1, mine]]
            rows16 += [small_ref[:6, shard:], jnp.zeros((1, shard), F32), bias_ref[1:2, mine]]
            value = jnp.concatenate(rows16, axis=0)
            high = value.astype(BF)
            for n, half in enumerate((high, (value - high.astype(F32)).astype(BF))):
                to = slice(2 * cut + (2 * side + n) * 16, 2 * cut + (2 * side + n + 1) * 16)
                kept_ref[to, :] = half
                sent_ref[to, :] = half

    for copy in copies_out:
        copy.wait()


def attend_backward(part, first, probs, dot_turned, dnat, q, k, v, x, *more):
    heads, keys, queries = probs.shape
    width = heads * HD
    sub, slots = 256, 4
    sums = jax.ShapeDtypeStruct((2, width, width), F32)
    turned = jax.ShapeDtypeStruct((width, queries), F32)
    grad = jax.ShapeDtypeStruct((queries, width), BF)
    inputs = (dot_turned, dnat, q, k, v, x) + more
    held = [pltpu.VMEM(a.shape, a.dtype) for a in inputs]
    held += [pltpu.VMEM(turned.shape, F32), pltpu.VMEM(grad.shape, BF), pltpu.VMEM(grad.shape, BF)]
    if part:
        out_shape = (turned, grad, sums, jax.ShapeDtypeStruct((2, width), F32))
        out_specs = (HBM, VMEM, VMEM, VMEM)
        held.append(pltpu.VMEM(grad.shape, BF))
    else:
        payload = jax.ShapeDtypeStruct((3 * width + 64, width // 2), BF)
        out_shape = (payload, payload, grad, grad, grad)
        out_specs = (VMEM, VMEM, VMEM, HBM, HBM)
        held += [pltpu.VMEM((width, width), F32), pltpu.VMEM((2, width), F32)]
    first_specs = [pl.BlockSpec(memory_space=pltpu.SMEM), VMEM, VMEM][: len(first)]
    return pl.pallas_call(
        functools.partial(backward_kernel, sub, part),
        out_shape=out_shape,
        in_specs=first_specs + [HBM] * (1 + len(inputs)),
        out_specs=out_specs,
        scratch_shapes=held
        + [
            pltpu.VMEM((2, LANES, queries), F32),
            pltpu.VMEM((slots, 2, keys // 4, queries), BF),
            pltpu.SemaphoreType.DMA((slots,)),
            pltpu.SemaphoreType.DMA((heads // 2, 5)),
            pltpu.SemaphoreType.DMA((1 + len(more),)),
            pltpu.SemaphoreType.DMA((heads // 2,)),
        ],
        compiler_params=params(),
        cost_estimate=cost(heads * keys * queries * 512, heads * keys * queries),
        name="attend_back_own" if not part else "attend_back_other",
    )(*first, probs, *inputs)


def input_kernel(res_ref, got_ref, dq_ref, dk_ref, dv_ref, own_ref, oth_ref, place_ref, dx_ref, live_scr):
    block = res_ref.shape[0]
    step = pl.program_id(0)

    @pl.when(step == 0)
    def _():
        live_scr[...] = jnp.zeros_like(live_scr)

    live_scr[pl.ds(pl.multiple_of(step * block, block), block), :] = (
        times_weights(dk_ref[...], own_ref, oth_ref, 1) + times_weights(dv_ref[...], own_ref, oth_ref, 2)
    ).astype(BF)
    dx = res_ref[...] + got_ref[...].astype(F32) + times_weights(dq_ref[...], own_ref, oth_ref, 0)
    dx_ref[...] = dx + dot(live_rows(place_ref, 0, live_scr.shape[0]), live_scr[...], 0, 0)


def input_gradient(res, got, dq, dk, dv, w_own, w_oth, place):
    tokens, width = res.shape
    rows = pl.BlockSpec((256, width), lambda i: (i, 0))
    whole = lambda *shape: pl.BlockSpec(shape, lambda i: (0,) * len(shape))
    return pl.pallas_call(
        input_kernel,
        grid=(tokens // 256,),
        out_shape=jax.ShapeDtypeStruct((tokens, width), F32),
        in_specs=[rows] * 5 + [whole(*w_own.shape)] * 2 + [pl.BlockSpec((1, 256), lambda i: (0, i))],
        out_specs=rows,
        scratch_shapes=[pltpu.VMEM(dk.shape, BF)],
        compiler_params=params(),
        cost_estimate=cost(3 * tokens * width * width, 16 * tokens * width),
        name="input_gradient",
    )(res, got, dq, dk, dv, w_own, w_oth, place)


def after(values, *others):
    return lax.optimization_barrier((values,) + others)[0]


def two_halves(values):
    high = values.astype(BF)
    return jnp.concatenate([high, (values - high.astype(F32)).astype(BF)], axis=0)


def one_value(halves):
    rows = halves.shape[0] // 2
    return halves[:rows].astype(F32) + halves[rows:].astype(F32)


def take(values, which):
    return lax.dynamic_index_in_dim(values, which, 0, False)


def in_order(mine, theirs, which):
    return jnp.concatenate([jnp.where(which == 0, mine, theirs), jnp.where(which == 0, theirs, mine)])


def sum_gradients(sent, kept, mid, input_grad, devices):
    index = lax.axis_index("dp")
    core, near = lax.rem(index, 2), lax.rem(index // 2, 2)
    rows = (sent.shape[0] - 64) // 2

    def across(values, bit):
        return lax.ppermute(values, "dp", [(i, i ^ bit) for i in range(devices)])

    got = across(sent, 1)
    halves = mid.reshape(2, mid.shape[0] // 2, -1)
    mid_got = across(take(halves, 1 - core).astype(BF), 1)
    total = kept[: 2 * rows].astype(F32) + got[: 2 * rows].astype(F32)
    small_own = one_value(kept[2 * rows : 2 * rows + 32]) + one_value(got[2 * rows : 2 * rows + 32])
    small_oth = one_value(kept[2 * rows + 32 :]) + one_value(got[2 * rows + 32 :])
    mid = (take(halves, core) + mid_got.astype(F32)).astype(BF)
    oth_two = two_halves(small_oth)
    mid_got = across(after(mid, oth_two), 4)
    result = input_grad(got)

    own_two = two_halves(small_own)
    got = lax.ppermute(jnp.concatenate([total[rows:].astype(BF), oth_two]), "tensor", [(0, 1), (1, 0)])
    total = total[:rows] + got[:rows].astype(F32)
    small = one_value(own_two) + one_value(got[rows:])

    halves = total.reshape(2, rows // 2, -1)
    two = two_halves(small)
    got = across(jnp.concatenate([take(halves, 1 - near).astype(BF), two]), 2)
    total = take(halves, near) + got[: rows // 2].astype(F32)
    small = one_value(two) + one_value(got[rows // 2 :])

    bit = 4
    while bit < devices:
        sent = jnp.concatenate([total.astype(BF), two_halves(small)])
        mid = (mid.astype(F32) + mid_got.astype(F32)).astype(BF)
        if 2 * bit < devices:
            mid_got = across(mid, 2 * bit)
        got = across(sent, bit)
        total = sent[: rows // 2].astype(F32) + got[: rows // 2].astype(F32)
        small = one_value(sent[rows // 2 :]) + one_value(got[rows // 2 :])
        bit *= 2
    mid = in_order(mid, across(mid, 1), core)
    mid = in_order(after(mid, got), after(across(mid, 2), got), near)

    up = mid.shape[0] * 2 // 3
    mid = mid[:up // 2].astype(F32), mid[up // 2 : up].astype(F32), mid[up:].astype(F32)
    mid = mid[0], mid[1], jnp.concatenate([mid[2][:, : sent.shape[1]], mid[2][:, sent.shape[1] :]])

    total = total.astype(BF)
    total = in_order(total, across(total, 2), near)
    total = in_order(total, across(total, 1), core)
    return total.astype(F32), small, mid, result


def mask_parts(known, lengths, halves):
    tokens, slots = known.shape[0] // halves, lengths.shape[0]
    positions = jnp.arange(known.shape[0], dtype=jnp.int32)
    ends = jnp.cumsum(lengths)
    starts = ends - lengths
    inside = (positions[:, None] >= starts[None, :]) & (positions[:, None] < ends[None, :])
    opening = jnp.any((positions[:, None] == starts[None, :]) & (lengths[None, :] > 0), axis=1)
    live = ((known > 0) | opening).astype(jnp.int32).reshape(halves, 1, tokens)
    place = jnp.where(live > 0, jnp.cumsum(live, axis=2) - 1, -1)
    counts = jnp.sum(live, axis=2)
    before = lambda ats: jnp.sum(
        jnp.where(positions.reshape(halves, 1, tokens) < ats[None, :, None], live, 0), axis=2
    )
    past = jnp.full((halves, LANES - HD - slots - 1), tokens, jnp.int32)
    none = jnp.full((halves, HD), tokens, jnp.int32)
    low = jnp.concatenate([none, before(starts), counts, past], axis=1)
    high = jnp.concatenate([none, before(ends), jnp.full((halves, 1), tokens, jnp.int32), past], axis=1)
    queries = jnp.where(jnp.pad(inside, ((0, 0), (0, 1))), 0.0, -MASK_BIG)
    queries = jnp.pad(queries, ((0, 0), (0, HD - slots - 1))).T.astype(BF)
    return place, jnp.stack([low, high], axis=1), queries, jnp.max(counts)


def local(
    devices, layer_input, gene_known, cell_genes, w_qkv, bias_qv, w_out, b_out, ln1_gain, ln1_bias,
    w_up, b_up, w_down, b_down, ln2_gain, ln2_bias, cotangent,
):
    tokens, width = layer_input.shape
    shard = w_qkv.shape[2]
    side, index = lax.axis_index("tensor"), lax.axis_index("dp")
    core, near = lax.rem(index, 2), lax.rem(index // 2, 2)

    def swapped(values):
        return lax.ppermute(values, "tensor", [(0, 1), (1, 0)])

    def across(values, bit):
        return lax.ppermute(values, "dp", [(i, i ^ bit) for i in range(devices)])

    w_own = w_qkv.transpose(1, 0, 2)
    quarter = 3 * width // 4
    mine = lax.dynamic_slice_in_dim(w_own.reshape(3 * width, shard), (2 * core + near) * quarter, quarter, 0)
    got = swapped(jnp.concatenate([mine, jnp.pad(bias_qv, ((0, 14), (0, 0)))]))
    x_oth = swapped(layer_input)
    piece = got[:quarter]
    piece = in_order(piece, across(piece, 2), near)
    w_oth = in_order(piece, across(piece, 1), core).reshape(3, width, shard)
    bias = jnp.concatenate([bias_qv, got[quarter : quarter + 2]], axis=1).astype(F32)

    place, bounds, query_rows, most = mask_parts(gene_known, cell_genes[0], 2)
    query_own = lax.dynamic_slice_in_dim(query_rows, side * tokens, tokens, 1)
    place_own, place_oth, bounds_own, bounds_oth = take(place, side), take(place, 1 - side), take(bounds, side), take(bounds, 1 - side)
    live = jnp.stack([core, most])
    b_up_row = jnp.pad(b_up[None], ((0, 15), (0, shard)))
    mid_w = jnp.concatenate([w_out, w_down, jnp.concatenate([w_up[:shard], w_up[shard:]], axis=1), b_up_row])
    vectors = jnp.stack([b_out, ln1_gain, ln1_bias, b_down, ln2_gain, ln2_bias, b_out, b_out])

    k_own, v_own, x_live, qt, q = project(layer_input, w_own, w_oth, bias, place_own, bounds_own, query_own)
    x_oth, k_own, mid_w = lax.optimization_barrier((x_oth, k_own, mid_w))
    mid_w_oth = swapped(mid_w)
    probs, ot, linv, k_oth, v_oth, x_oth = attend(
        live, qt, k_own, v_own, x_oth, w_own, w_oth, bias, place_oth, bounds_oth
    )
    activations, res, dot_turned, dnat, mid_own, mid_oth, small = middle(
        layer_input, cotangent, ot, linv, mid_w, mid_w_oth, vectors
    )
    mid_got = swapped(mid_oth)
    dq, dx_oth, sums, value_grad = attend_backward(
        1, (live, place_oth), probs, dot_turned, dnat, q, k_oth, v_oth, x_oth, w_own, w_oth
    )
    mid_got, dq = lax.optimization_barrier((mid_got, dq))
    mid = (mid_own + mid_got.astype(F32)).reshape(2, 3 * shard // 2, width)
    mid_got = across(take(mid, 1 - near).astype(BF), 2)
    dx_got = swapped(dx_oth)
    sent, kept, dq, dk, dv = attend_backward(
        0, (live, small, value_grad), probs, dot_turned, dnat, q, k_own, v_own, x_live, dq, sums, layer_input
    )
    mid_got, dx_got, sent = lax.optimization_barrier((mid_got, dx_got, sent))
    mid = take(mid, near) + mid_got.astype(F32)

    def input_grad(token):
        return input_gradient(res, dx_got, after(dq, token), dk, dv, w_own, w_oth, place_own)

    qkv, small, mid, input_grad = sum_gradients(sent, kept, mid, input_grad, devices)
    qkv_g = qkv.reshape(3, width, shard).transpose(1, 0, 2)
    wide = jnp.concatenate([small[:6], small[8:14]], axis=1)
    out_g, down_g, up_g = mid
    return (
        activations, input_grad, qkv_g, jnp.stack([small[7], small[15]]), out_g, wide[0], wide[1], wide[2],
        up_g, small[6], down_g, wide[3], wide[4], wide[5],
    )


def solution(mesh):
    placed = (
        P(("dp", "tensor"), None),
        P("dp"),
        P("dp", None),
        P(None, None, "tensor"),
        P(None, "tensor"),
        P("tensor", None),
        P(),
        P(),
        P(),
        P(None, "tensor"),
        P("tensor"),
        P("tensor", None),
        P(),
        P(),
        P(),
        P(("dp", "tensor"), None),
    )
    return jax.shard_map(
        functools.partial(local, mesh.shape["dp"]),
        mesh=mesh,
        in_specs=placed,
        out_specs=(
            P(("dp", "tensor"), None),
            P(("dp", "tensor"), None),
            P(None, None, "tensor"),
            P(None, "tensor"),
            P("tensor", None),
            P(),
            P(),
            P(),
            P(None, "tensor"),
            P("tensor"),
            P("tensor", None),
            P(),
            P(),
            P(),
        ),
        check_vma=False,
    )
```

```python
import functools

import jax
import jax.numpy as jnp
from jax import lax
from jax.experimental import pallas as pl
from jax.experimental.pallas import tpu as pltpu
from jax.sharding import PartitionSpec as P

HD = 64
LANES = 128
NORM_EPS = 1e-05
MASK_BIG = 2.0**100
LOG2E = 1.4426950408889634
VMEM_BYTES = 58 * 2**20
BF = jnp.bfloat16
F32 = jnp.float32
VMEM = pl.BlockSpec(memory_space=pltpu.VMEM)
HBM = pl.BlockSpec(memory_space=pl.ANY)


def dot(left, right, left_dim, right_dim):
    return lax.dot_general(
        left, right, (((left_dim,), (right_dim,)), ((), ())), preferred_element_type=F32
    )


def params():
    return pltpu.CompilerParams(vmem_limit_bytes=VMEM_BYTES)


def cost(macs, moved):
    return pl.CostEstimate(flops=2 * macs, bytes_accessed=moved, transcendentals=0)


def values_columns(rows):
    lane = lax.broadcasted_iota(jnp.int32, (rows, LANES), 1)
    return jnp.where((lane == HD) | (lane == HD + 1), 1.0, 0.0)


def live_rows(place_ref, first, rows, columns=slice(None)):
    place = place_ref[:, columns]
    row = lax.broadcasted_iota(jnp.int32, (rows, place.shape[1]), 0) + first
    return jnp.where(row == place, 1.0, 0.0).astype(BF)


def key_value_block(x_ref, place_ref, bounds_ref, w_refs, bias_ref, x_out, k_ref, v_ref, first, rows, base=0):
    at, to = pl.ds(first, rows), pl.ds(base + first, rows)
    later = slice(first, None) if isinstance(first, int) else slice(None)
    x = dot(live_rows(place_ref, first, rows, later), x_ref[later, :], 1, 0).astype(BF)
    x_out[at, :] = x
    shard = w_refs[0].shape[2]
    row = lax.broadcasted_iota(jnp.int32, (rows, LANES), 0) + first
    extra_k = jnp.where((row >= bounds_ref[0:1, :]) & (row < bounds_ref[1:2, :]), 1.0, 0.0)
    extra_v = values_columns(rows)
    low = lax.broadcasted_iota(jnp.int32, (rows, LANES), 1) < HD
    for side, w_ref in enumerate(w_refs):
        mine = slice(side * shard, (side + 1) * shard)
        keys = dot(x, w_ref[1], 1, 0)
        values = dot(x, w_ref[2], 1, 0) + bias_ref[1:2, mine]
        for i in range(shard // HD):
            pair = slice((i // 2) * LANES, (i // 2 + 1) * LANES)
            k_pair, v_pair = keys[:, pair], values[:, pair]
            if i % 2:
                k_pair, v_pair = pltpu.roll(k_pair, HD, 1), pltpu.roll(v_pair, HD, 1)
            h = side * (shard // HD) + i
            k_ref[h, to, :] = jnp.where(low, k_pair, extra_k).astype(BF)
            v_ref[h, to, :] = jnp.where(low, v_pair, extra_v).astype(BF)


def project_kernel(x_ref, own_ref, oth_ref, bias_ref, place_ref, bounds_ref, extra_q_ref, k_ref, v_ref, x_out, qt_ref, q_ref):
    block = q_ref.shape[0]
    first = pl.multiple_of(pl.program_id(0) * block, block)
    shard = own_ref.shape[2]
    key_value_block(
        x_ref, place_ref, bounds_ref, (own_ref, oth_ref), bias_ref, x_out, k_ref, v_ref, first, block
    )
    x = x_ref[pl.ds(first, block), :]
    for side, w_ref in enumerate((own_ref, oth_ref)):
        mine = slice(side * shard, (side + 1) * shard)
        q = (dot(x, w_ref[0], 1, 0) + bias_ref[0:1, mine]).astype(BF)
        q_ref[:, mine] = q
        turned = q.T
        for i in range(shard // HD):
            h = side * (shard // HD) + i
            qt_ref[h, :HD, :] = turned[i * HD : (i + 1) * HD, :]
            qt_ref[h, HD:, :] = extra_q_ref[...]


def project(x, w_own, w_oth, bias, place, bounds, extra_q):
    tokens, width = x.shape
    heads = width // HD
    block = 256
    whole = lambda *shape: pl.BlockSpec(shape, lambda i: (0,) * len(shape))
    per_head = whole(heads, tokens, LANES)
    return pl.pallas_call(
        project_kernel,
        grid=(tokens // block,),
        out_shape=(
            jax.ShapeDtypeStruct((heads, tokens, LANES), BF),
            jax.ShapeDtypeStruct((heads, tokens, LANES), BF),
            jax.ShapeDtypeStruct((tokens, width), BF),
            jax.ShapeDtypeStruct((heads, LANES, tokens), BF),
            jax.ShapeDtypeStruct((tokens, width), BF),
        ),
        in_specs=[
            whole(*x.shape),
            whole(*w_own.shape),
            whole(*w_oth.shape),
            whole(*bias.shape),
            whole(*place.shape),
            whole(*bounds.shape),
            pl.BlockSpec((HD, block), lambda i: (0, i)),
        ],
        out_specs=(
            per_head,
            per_head,
            whole(tokens, width),
            pl.BlockSpec((heads, LANES, block), lambda i: (0, 0, i)),
            pl.BlockSpec((block, width), lambda i: (i, 0)),
        ),
        compiler_params=params(),
        cost_estimate=cost(5 * tokens * width * width, 12 * tokens * width),
        name="project",
    )(x, w_own, w_oth, bias, place, bounds, extra_q)


def key_sizes(keys):
    return (keys * 13 // 16, keys)


def for_size(live, keys, work):
    below = 0
    for n, size in enumerate(key_sizes(keys)):

        @pl.when((live > below) & (live <= size) if below else live <= size)
        def _():
            work(size, n > 0)

        below = size


def sweep(rolled, size, count, body, carry=0):
    rows = size // count
    if rolled:
        return lax.fori_loop(0, count, lambda i, held: body(pl.multiple_of(i * rows, rows), held), carry)
    for i in range(count):
        carry = body(i * rows, carry)
    return carry


def attend_kernel(
    count, chunk, live_ref, qt_hbm, k_hbm, v_hbm, x_ref, own_ref, oth_ref, bias_ref, place_ref, bounds_ref,
    p_hbm, ot_ref, linv_ref, k_oth_hbm, v_oth_hbm, x_oth_hbm,
    qt_ref, k_ref, v_ref, x1_ref,
    s0_scr, s1_scr, peak0_scr, peak1_scr, row_scr, acc_scr, p_scr, sem, in_sem, out_sem,
):
    heads, _, queries = qt_ref.shape
    half = x_ref.shape[0]
    parts = queries // chunk
    steps = heads * parts
    slots = p_scr.shape[0]

    def copies_in(h):
        return [
            pltpu.make_async_copy(src.at[h], dst, in_sem.at[h, n])
            for n, (src, dst) in enumerate(
                ((qt_hbm, qt_ref.at[h]), (k_hbm, k_ref.at[h, :half]), (v_hbm, v_ref.at[h, :half]))
            )
        ]

    for h in range(heads):
        for copy in copies_in(h):
            copy.start()

    def project_live(size, rolled):
        def block(first, carry):
            key_value_block(
                x_ref, place_ref, bounds_ref, (own_ref, oth_ref), bias_ref, x1_ref, k_ref, v_ref, first, size // count, half
            )
            return carry

        sweep(rolled, size, count, block)
        if size < half:
            x1_ref[size:, :] = jnp.zeros((half - size, x1_ref.shape[1]), BF)

    for_size(live_ref[1], half, project_live)

    copies_kv = [
        pltpu.make_async_copy(k_ref.at[:, half:, :], k_oth_hbm, out_sem.at[0]),
        pltpu.make_async_copy(v_ref.at[:, half:, :], v_oth_hbm, out_sem.at[1]),
        pltpu.make_async_copy(x1_ref, x_oth_hbm, out_sem.at[2]),
    ]
    for copy in copies_kv:
        copy.start()

    def columns(step):
        return pl.ds(pl.multiple_of(lax.rem(step, parts) * chunk, chunk), chunk)

    def copies_out(step, size):
        slot = lax.rem(step, slots)
        copies = []
        for part in range(2):
            rows = slice(part * half, part * half + size)
            to = p_hbm.at[step // parts, rows, columns(step)]
            copies.append(pltpu.make_async_copy(p_scr.at[slot, rows, :], to, sem.at[slot, part]))
        return copies

    def scores(step, s_ref, peak, rows):
        s = dot(k_ref[step // parts, rows, :], qt_ref[step // parts, :, columns(step)], 1, 0)
        s_ref[rows, :] = s
        return jnp.maximum(peak, jnp.max(s.reshape(-1, 8, chunk), axis=0))

    def mix(step, s_ref, rows):
        p = jnp.exp2((s_ref[rows, :] - row_scr[...]) * (LOG2E * HD**-0.5)).astype(BF)
        p_scr[lax.rem(step, slots), rows, :] = p
        return dot(v_ref[step // parts, rows, :], p, 0, 0)

    def over_keys(size, rolled, block, carry):
        if size == half:
            return sweep(rolled, 2 * half, 2 * count, lambda at, held: block(pl.ds(at, size // count), held), carry)
        for part in range(2):
            rows = lambda at, held: block(pl.ds(part * half + at, size // count), held)
            carry = sweep(rolled, size, count, rows, carry)
        return carry

    def run(size, rolled, step, s_ref, peak_ref, after, s_after, peak_after):
        row_scr[...] = jnp.max(peak_ref[...], axis=0, keepdims=True)

        @pl.when(step >= slots)
        def _():
            for copy in copies_out(step - slots, size):
                copy.wait()

        def block(rows, held):
            peak = scores(after, s_after, held[0], rows)
            return peak, held[1] + mix(step, s_ref, rows)

        start = (jnp.full((8, chunk), -jnp.inf, F32), jnp.zeros((LANES, chunk), F32))
        peak_after[...], acc_scr[...] = over_keys(size, rolled, block, start)
        for copy in copies_out(step, size):
            copy.start()
        inverse = 1.0 / acc_scr[HD : HD + 1, :]
        linv_ref[step // parts, :, columns(step)] = inverse
        ot_ref[step // parts, :, columns(step)] = acc_scr[:HD, :] * inverse

    for copy in copies_in(0):
        copy.wait()

    def work(size, rolled):
        def first_block(rows, peak):
            return scores(0, s0_scr, peak, rows)

        peak0_scr[...] = over_keys(size, rolled, first_block, jnp.full((8, chunk), -jnp.inf, F32))

        @pl.loop(0, steps // 2)
        def _(i):
            run(size, rolled, 2 * i, s0_scr, peak0_scr, 2 * i + 1, s1_scr, peak1_scr)
            after = 2 * i + 2

            @pl.when((after < steps) & (lax.rem(after, parts) == 0))
            def _():
                for copy in copies_in(after // parts):
                    copy.wait()

            run(size, rolled, 2 * i + 1, s1_scr, peak1_scr, jnp.minimum(after, steps - 1), s0_scr, peak0_scr)

        for slot in range(slots):
            for copy in copies_out(steps - slots + slot, size):
                copy.wait()

    for_size(live_ref[1], half, work)
    for copy in copies_kv:
        copy.wait()


def attend(live, qt, k_own, v_own, x_oth, w_own, w_oth, bias, place, bounds):
    heads, _, queries = qt.shape
    keys = 2 * queries
    count, chunk, slots = 4, 512, 4
    per_head = jax.ShapeDtypeStruct(k_own.shape, BF)
    return pl.pallas_call(
        functools.partial(attend_kernel, count, chunk),
        out_shape=(
            jax.ShapeDtypeStruct((heads, keys, queries), BF),
            jax.ShapeDtypeStruct((heads, HD, queries), F32),
            jax.ShapeDtypeStruct((heads, 1, queries), F32),
            per_head,
            per_head,
            jax.ShapeDtypeStruct(x_oth.shape, BF),
        ),
        in_specs=[pl.BlockSpec(memory_space=pltpu.SMEM)] + [HBM] * 3 + [VMEM] * 6,
        out_specs=(HBM, VMEM, VMEM, HBM, HBM, HBM),
        scratch_shapes=[
            pltpu.VMEM(qt.shape, BF),
            pltpu.VMEM((heads, keys, LANES), BF),
            pltpu.VMEM((heads, keys, LANES), BF),
            pltpu.VMEM(x_oth.shape, BF),
            pltpu.VMEM((keys, chunk), F32),
            pltpu.VMEM((keys, chunk), F32),
            pltpu.VMEM((8, chunk), F32),
            pltpu.VMEM((8, chunk), F32),
            pltpu.VMEM((1, chunk), F32),
            pltpu.VMEM((LANES, chunk), F32),
            pltpu.VMEM((slots, keys, chunk), BF),
            pltpu.SemaphoreType.DMA((slots, 2)),
            pltpu.SemaphoreType.DMA((heads, 3)),
            pltpu.SemaphoreType.DMA((3,)),
        ],
        compiler_params=params(),
        cost_estimate=cost(heads * keys * queries * 512, 2 * heads * keys * queries),
        name="attend",
    )(live, qt, k_own, v_own, x_oth, w_own, w_oth, bias, place, bounds)


def normalize(values):
    mean = jnp.mean(values, axis=-1, keepdims=True)
    centered = values - mean
    inverse = lax.rsqrt(jnp.mean(centered * centered, axis=-1, keepdims=True) + NORM_EPS)
    return centered * inverse, inverse


def norm_back(e, normed, inverse):
    return inverse * (
        e - jnp.mean(e, axis=-1, keepdims=True) - normed * jnp.mean(e * normed, axis=-1, keepdims=True)
    )


def middle_kernel(
    sub, x_ref, cot_ref, ot_ref, linv_ref, w_own_ref, w_oth_ref, vec_ref,
    act_ref, res_ref, dot_ref, dnat_ref, own_ref, oth_ref, small_ref,
    att_scr, w_out_ref, w_up_ref, w_down_ref, b_up_ref, gw_ref,
):
    block, width = x_ref.shape
    heads = width // HD
    shard = width // 2
    b_out, gain1, bias1, b_down, gain2, bias2 = (vec_ref[i : i + 1, :] for i in range(6))

    @pl.when(pl.program_id(0) == 0)
    def _():
        gw_ref[...] = jnp.zeros_like(gw_ref)
        small_ref[...] = jnp.zeros_like(small_ref)
        for side, ref in enumerate((w_own_ref, w_oth_ref)):
            mine = slice(side * shard, (side + 1) * shard)
            w_out_ref[mine, :] = ref[:shard, :]
            w_down_ref[mine, :] = ref[shard : 2 * shard, :]
            w_up_ref[:shard, mine] = ref[2 * shard : 3 * shard, :shard]
            w_up_ref[shard:, mine] = ref[2 * shard : 3 * shard, shard:]
            b_up_ref[:, mine] = ref[3 * shard : 3 * shard + 1, :shard].astype(F32)

    def col_sum(row, values):
        small_ref[row : row + 1, :] += jnp.sum(values, axis=0, keepdims=True)

    def chain(u):
        rows = slice(u * sub, (u + 1) * sub)
        for h in range(heads):
            att_scr[u, h * HD : (h + 1) * HD, :] = ot_ref[h, :, rows].astype(BF)
        branch = dot(att_scr[u], w_out_ref[...], 0, 0)
        yield
        n1, inv1 = normalize(x_ref[rows, :].astype(F32) + branch + b_out)
        first = n1 * gain1 + bias1
        first_low = first.astype(BF)
        yield
        pre = dot(first_low, w_up_ref[...], 1, 0) + b_up_ref[...]
        yield
        cdf = 0.5 * (1.0 + lax.erf(pre * 0.5**0.5))
        hidden = (pre * cdf).astype(BF)
        slope = cdf + pre * (0.3989422804014327 * jnp.exp(-0.5 * pre * pre))
        yield
        branch = dot(hidden, w_down_ref[...], 1, 0)
        yield
        n2, inv2 = normalize(first + branch + b_down)
        act_ref[rows, :] = (n2 * gain2 + bias2).astype(BF)
        cot = cot_ref[rows, :].astype(F32)
        two = norm_back(cot * gain2, n2, inv2)
        two_low = two.astype(BF)
        yield
        back = dot(two_low, w_down_ref[...], 1, 1)
        gw_ref[2] += dot(hidden, two_low, 0, 0)
        col_sum(3, two)
        col_sum(4, cot * n2)
        col_sum(5, cot)
        yield
        pre_grad = (back * slope).astype(BF)
        yield
        back = dot(pre_grad, w_up_ref[...], 1, 1)
        gw_ref[1] += dot(first_low, pre_grad, 0, 0)
        col_sum(6, pre_grad.astype(F32))
        yield
        one = two + back
        res = norm_back(one * gain1, n1, inv1)
        res_ref[rows, :] = res
        res_low = res.astype(BF)
        yield
        turned = dot(w_out_ref[...], res_low, 1, 1)
        gw_ref[0] += dot(att_scr[u], res_low, 1, 0)
        col_sum(1, one * n1)
        col_sum(2, one)
        col_sum(0, res)
        yield
        pick = lax.broadcasted_iota(jnp.int32, (HD, sub), 0)
        for h in range(heads):
            head = slice(h * HD, (h + 1) * HD)
            grad = (turned[head].astype(BF).astype(F32) * linv_ref[h, :, rows]).astype(BF)
            inner = -jnp.sum(grad.astype(F32) * ot_ref[h, :, rows], axis=0, keepdims=True)
            high = inner.astype(BF).astype(F32)
            dot_ref[h, :HD, rows] = grad
            dot_ref[h, HD:, rows] = jnp.where(pick == 0, high, jnp.where(pick == 1, inner - high, 0.0)).astype(BF)
            att_scr[u, head, :] = grad
        dnat_ref[rows, :] = att_scr[u].T
        yield

    for _ in zip(*(chain(u) for u in range(block // sub))):
        pass

    @pl.when(pl.program_id(0) == pl.num_programs(0) - 1)
    def _():
        for ref, mine in ((own_ref, slice(0, shard)), (oth_ref, slice(shard, width))):
            ref[:shard, :] = gw_ref[0, mine, :].astype(ref.dtype)
            ref[shard:width, :] = gw_ref[2, mine, :].astype(ref.dtype)
            ref[width:, :shard] = gw_ref[1, :shard, mine].astype(ref.dtype)
            ref[width:, shard:] = gw_ref[1, shard:, mine].astype(ref.dtype)


def middle(x, cot, ot, linv, w_own, w_oth, vectors):
    tokens, width = x.shape
    heads = width // HD
    block, sub = 512, 256
    whole = lambda *shape: pl.BlockSpec(shape, lambda i: (0,) * len(shape))
    rows = pl.BlockSpec((block, width), lambda i: (i, 0))
    columns = lambda n: pl.BlockSpec((heads, n, block), lambda i: (0, 0, i))
    square = pltpu.VMEM((width, width), BF)
    return pl.pallas_call(
        functools.partial(middle_kernel, sub),
        grid=(tokens // block,),
        out_shape=(
            jax.ShapeDtypeStruct((tokens, width), BF),
            jax.ShapeDtypeStruct((tokens, width), F32),
            jax.ShapeDtypeStruct((heads, LANES, tokens), BF),
            jax.ShapeDtypeStruct((tokens, width), BF),
            jax.ShapeDtypeStruct((3 * width // 2, width), F32),
            jax.ShapeDtypeStruct((3 * width // 2, width), BF),
            jax.ShapeDtypeStruct((8, width), F32),
        ),
        in_specs=[rows, rows, columns(HD), columns(1), whole(*w_own.shape), whole(*w_oth.shape), whole(*vectors.shape)],
        out_specs=(
            rows, rows, columns(LANES), rows,
            whole(3 * width // 2, width), whole(3 * width // 2, width), whole(8, width),
        ),
        scratch_shapes=[
            pltpu.VMEM((block // sub, width, sub), BF), square, square, square,
            pltpu.VMEM((1, width), F32), pltpu.VMEM((3, width, width), F32),
        ],
        compiler_params=params(),
        cost_estimate=cost(9 * tokens * width * width, 20 * tokens * width),
        name="middle",
    )(x, cot, ot, linv, w_own, w_oth, vectors)


def times_weights(grad, own_ref, oth_ref, third):
    shard = own_ref.shape[2]
    return dot(grad[:, :shard], own_ref[third], 1, 1) + dot(grad[:, shard:], oth_ref[third], 1, 1)


def backward_kernel(sub, part, *refs):
    if part:
        (live_ref, p_hbm, dot_hbm, dnat_hbm, q_hbm, k_hbm, v_hbm, x_hbm, own_hbm, oth_hbm,
         dq_hbm, dx_ref, gw_ref, bias_ref,
         dot_ref, dnat_ref, q_ref, k_ref, v_ref, x_ref, own_ref, oth_ref,
         dq_ref, dk_ref, dv_ref, acc_scr, p_scr, sem, pair_sem, last_sem, out_sem) = refs
        more = ((own_hbm, own_ref), (oth_hbm, oth_ref))
    else:
        (live_ref, small_ref, value_ref,
         p_hbm, dot_hbm, dnat_hbm, q_hbm, k_hbm, v_hbm, x_hbm, dq_hbm, gw_hbm, whole_hbm,
         sent_ref, kept_ref, dq_out, dk_hbm, dv_hbm,
         dot_ref, dnat_ref, q_ref, k_ref, v_ref, x_ref, before_ref, gw_ref, whole_ref,
         dq_ref, dk_ref, dv_ref, gq_ref, bias_ref, acc_scr, p_scr, sem, pair_sem, last_sem, out_sem) = refs
        more = ((dq_hbm, before_ref), (gw_hbm, gw_ref), (whole_hbm, whole_ref))
    heads, _, queries = dot_ref.shape
    keys = k_ref.shape[1]
    width = heads * HD
    shard = width // 2
    slots = p_scr.shape[0]
    pairs = heads // 2

    def copy_in(p, j, size):
        block = size // 2
        slot = lax.rem(p * 2 + j, slots)
        first = part * keys + j * block
        if not isinstance(j, int):
            first = pl.multiple_of(first, 16)
        src = p_hbm.at[pl.ds(2 * p, 2), pl.ds(first, block), :]
        return pltpu.make_async_copy(src, p_scr.at[slot, :, :block, :], sem.at[slot])

    def pair_copies(p):
        pair = pl.ds(2 * p, 2)
        lanes = pl.ds(pl.multiple_of(p * LANES, LANES), LANES)
        by_head = ((dot_hbm, dot_ref), (k_hbm, k_ref), (v_hbm, v_ref))
        by_lane = ((dnat_hbm, dnat_ref), (q_hbm, q_ref))
        return [
            pltpu.make_async_copy(src.at[pair], dst.at[pair], pair_sem.at[p, n]) for n, (src, dst) in enumerate(by_head)
        ] + [
            pltpu.make_async_copy(src.at[:, lanes], dst.at[:, lanes], pair_sem.at[p, 3 + n])
            for n, (src, dst) in enumerate(by_lane)
        ]

    last = ((x_hbm, x_ref),) + more

    def rows_out(p):
        rows = pl.ds(pl.multiple_of(p * 2 * HD, 2 * HD), 2 * HD)
        return pltpu.make_async_copy(dq_ref.at[rows, :], dq_hbm.at[rows, :], out_sem.at[p])

    last_copies = [pltpu.make_async_copy(src, dst, last_sem.at[n]) for n, (src, dst) in enumerate(last)]

    for copy in pair_copies(0):
        copy.start()

    def work(size, rolled):
        block, rows = size // 2, size // 4
        low = lax.broadcasted_iota(jnp.int32, (rows, LANES), 1) < HD
        if size < keys:
            dk_ref[size:, :] = jnp.zeros((keys - size, width), BF)
            dv_ref[size:, :] = jnp.zeros((keys - size, width), BF)
        for step in range(slots - 1):
            copy_in(step // 2, step % 2, size).start()

        @pl.loop(0, pairs)
        def _(p):
            lanes = pl.ds(pl.multiple_of(p * LANES, LANES), LANES)
            for copy in pair_copies(p):
                copy.wait()

            @pl.when(p + 1 < pairs)
            def _():
                for copy in pair_copies(p + 1):
                    copy.start()

            @pl.when(p == 1)
            def _():
                for copy in last_copies:
                    copy.start()

            acc_scr[...] = jnp.zeros_like(acc_scr)

            def one_block(j):
                slot = lax.rem(p * 2 + j, slots)
                copy_in(p, j, size).wait()
                ahead = 2 * p + j + slots - 1

                @pl.when(ahead < 2 * pairs)
                def _():
                    copy_in(ahead // 2, lax.rem(ahead, 2), size).start()

                def at_rows(at, total):
                    here = pl.ds(pl.multiple_of(j * block + at, 16), rows)
                    total, dks, dvs = list(total), [], []
                    for side in range(2):
                        h = 2 * p + side
                        prob = p_scr[slot, side, pl.ds(at, rows), :]
                        slope = dot(v_ref[h, here, :], dot_ref[h], 1, 0)
                        dvs.append(dot(prob, dnat_ref[:, lanes], 1, 0))
                        ds = (prob.astype(F32) * slope).astype(BF)
                        dks.append(dot(ds, q_ref[:, lanes], 1, 0))
                        total[side] = total[side] + dot(k_ref[h, here, :], ds, 0, 0)
                    dk_ref[here, lanes] = (jnp.where(low, dks[0], dks[1]) * HD**-0.5).astype(BF)
                    dv_ref[here, lanes] = jnp.where(low, dvs[0], dvs[1]).astype(BF)
                    return tuple(total)

                zero = jnp.zeros((LANES, queries), F32)
                for side, total in enumerate(sweep(rolled, block, 2, at_rows, (zero, zero))):
                    acc_scr[side] += total

            pl.loop(0, 2)(one_block)

            for side in range(2):
                dq_ref[pl.ds(pl.multiple_of((2 * p + side) * HD, HD), HD), :] = acc_scr[side, :HD, :]
            if part:
                rows_out(p).start()

    for_size(live_ref[1], keys, work)
    for copy in last_copies:
        copy.wait()
    if part:
        copies_out = [rows_out(p) for p in range(heads // 2)]
    else:
        copies_out = [
            pltpu.make_async_copy(dk_ref, dk_hbm, out_sem.at[0]),
            pltpu.make_async_copy(dv_ref, dv_hbm, out_sem.at[1]),
        ]
        for copy in copies_out:
            copy.start()

    for n, grad_ref in enumerate((dk_ref, dv_ref)):
        grad = dot(x_ref[...], grad_ref[...], 0, 0)
        gw_ref[n] = grad if part else gw_ref[n] + grad
    bias_ref[1:2, :] = jnp.sum(dv_ref[...].astype(F32), axis=0, keepdims=True)
    if part:
        bias_ref[0:1, :] = jnp.zeros((1, width), F32)

        @pl.loop(0, keys // sub)
        def _(i):
            rows = pl.ds(pl.multiple_of(i * sub, sub), sub)
            dk, dv = dk_ref[rows, :], dv_ref[rows, :]
            dx = times_weights(dk, own_ref, oth_ref, 1) + times_weights(dv, own_ref, oth_ref, 2)
            dx_ref[rows, :] = dx.astype(BF)
    else:
        dq_out[...] = ((before_ref[...] + dq_ref[...]) * HD**-0.5).astype(BF).T
        gq_ref[...] = dot(whole_ref[...], dq_out[...], 0, 0)
        bias_ref[0:1, :] = jnp.sum(dq_out[...].astype(F32), axis=0, keepdims=True)

    if not part:
        first = live_ref[0] == 0
        bias_ref[1:2, :] += value_ref[1:2, :]
        cut = 3 * width // 2
        for side in range(2):
            mine = slice(side * shard, (side + 1) * shard)
            pieces = [gq_ref[:, mine], gw_ref[0, :, mine], gw_ref[1, :, mine]]
            blocks = [piece[at : at + shard, :].astype(BF) for piece in pieces for at in (0, shard)]
            for n in range(3):
                to = slice(side * cut + n * shard, side * cut + (n + 1) * shard)
                kept_ref[to, :] = jnp.where(first, blocks[n], blocks[3 + n])
                sent_ref[to, :] = jnp.where(first, blocks[3 + n], blocks[n])
            rows16 = [small_ref[:6, :shard], small_ref[6:7, mine], bias_ref[0:1, mine]]
            rows16 += [small_ref[:6, shard:], jnp.zeros((1, shard), F32), bias_ref[1:2, mine]]
            value = jnp.concatenate(rows16, axis=0)
            high = value.astype(BF)
            for n, half in enumerate((high, (value - high.astype(F32)).astype(BF))):
                to = slice(2 * cut + (2 * side + n) * 16, 2 * cut + (2 * side + n + 1) * 16)
                kept_ref[to, :] = half
                sent_ref[to, :] = half

    for copy in copies_out:
        copy.wait()


def attend_backward(part, first, probs, dot_turned, dnat, q, k, v, x, *more):
    heads, keys, queries = probs.shape
    width = heads * HD
    sub, slots = 256, 4
    sums = jax.ShapeDtypeStruct((2, width, width), F32)
    turned = jax.ShapeDtypeStruct((width, queries), F32)
    grad = jax.ShapeDtypeStruct((queries, width), BF)
    inputs = (dot_turned, dnat, q, k, v, x) + more
    held = [pltpu.VMEM(a.shape, a.dtype) for a in inputs]
    held += [pltpu.VMEM(turned.shape, F32), pltpu.VMEM(grad.shape, BF), pltpu.VMEM(grad.shape, BF)]
    if part:
        out_shape = (turned, grad, sums, jax.ShapeDtypeStruct((2, width), F32))
        out_specs = (HBM, VMEM, VMEM, VMEM)
    else:
        payload = jax.ShapeDtypeStruct((3 * width + 64, width // 2), BF)
        out_shape = (payload, payload, grad, grad, grad)
        out_specs = (VMEM, VMEM, VMEM, HBM, HBM)
        held += [pltpu.VMEM((width, width), F32), pltpu.VMEM((2, width), F32)]
    first_specs = [pl.BlockSpec(memory_space=pltpu.SMEM), VMEM, VMEM][: len(first)]
    return pl.pallas_call(
        functools.partial(backward_kernel, sub, part),
        out_shape=out_shape,
        in_specs=first_specs + [HBM] * (1 + len(inputs)),
        out_specs=out_specs,
        scratch_shapes=held
        + [
            pltpu.VMEM((2, LANES, queries), F32),
            pltpu.VMEM((slots, 2, keys // 4, queries), BF),
            pltpu.SemaphoreType.DMA((slots,)),
            pltpu.SemaphoreType.DMA((heads // 2, 5)),
            pltpu.SemaphoreType.DMA((1 + len(more),)),
            pltpu.SemaphoreType.DMA((heads // 2,)),
        ],
        compiler_params=params(),
        cost_estimate=cost(heads * keys * queries * 512, heads * keys * queries),
        name="attend_back_own" if not part else "attend_back_other",
    )(*first, probs, *inputs)


def input_kernel(res_ref, got_ref, dq_ref, dk_ref, dv_ref, own_ref, oth_ref, place_ref, dx_ref, live_scr):
    block = res_ref.shape[0]
    step = pl.program_id(0)

    @pl.when(step == 0)
    def _():
        live_scr[...] = jnp.zeros_like(live_scr)

    live_scr[pl.ds(pl.multiple_of(step * block, block), block), :] = (
        times_weights(dk_ref[...], own_ref, oth_ref, 1)
        + times_weights(dv_ref[...], own_ref, oth_ref, 2)
        + got_ref[...].astype(F32)
    ).astype(BF)
    dx = res_ref[...] + times_weights(dq_ref[...], own_ref, oth_ref, 0)
    dx_ref[...] = dx + dot(live_rows(place_ref, 0, live_scr.shape[0]), live_scr[...], 0, 0)


def input_gradient(res, got, dq, dk, dv, w_own, w_oth, place):
    tokens, width = res.shape
    rows = pl.BlockSpec((256, width), lambda i: (i, 0))
    whole = lambda *shape: pl.BlockSpec(shape, lambda i: (0,) * len(shape))
    return pl.pallas_call(
        input_kernel,
        grid=(tokens // 256,),
        out_shape=jax.ShapeDtypeStruct((tokens, width), F32),
        in_specs=[rows] * 5 + [whole(*w_own.shape)] * 2 + [pl.BlockSpec((1, 256), lambda i: (0, i))],
        out_specs=rows,
        scratch_shapes=[pltpu.VMEM(dk.shape, BF)],
        compiler_params=params(),
        cost_estimate=cost(3 * tokens * width * width, 16 * tokens * width),
        name="input_gradient",
    )(res, got, dq, dk, dv, w_own, w_oth, place)


def after(values, *others):
    return lax.optimization_barrier((values,) + others)[0]


def two_halves(values):
    high = values.astype(BF)
    return jnp.concatenate([high, (values - high.astype(F32)).astype(BF)], axis=0)


def one_value(halves):
    rows = halves.shape[0] // 2
    return halves[:rows].astype(F32) + halves[rows:].astype(F32)


def take(values, which):
    return lax.dynamic_index_in_dim(values, which, 0, False)


def in_order(mine, theirs, which):
    return jnp.concatenate([jnp.where(which == 0, mine, theirs), jnp.where(which == 0, theirs, mine)])


def sum_gradients(sent, kept, mid, input_grad, devices):
    index = lax.axis_index("dp")
    core, near = lax.rem(index, 2), lax.rem(index // 2, 2)
    rows = (sent.shape[0] - 64) // 2

    def across(values, bit):
        return lax.ppermute(values, "dp", [(i, i ^ bit) for i in range(devices)])

    got = across(sent, 1)
    halves = mid.reshape(2, mid.shape[0] // 2, -1)
    mid_got = across(take(halves, 1 - core).astype(BF), 1)
    total = kept[: 2 * rows].astype(F32) + got[: 2 * rows].astype(F32)
    small_own = one_value(kept[2 * rows : 2 * rows + 32]) + one_value(got[2 * rows : 2 * rows + 32])
    small_oth = one_value(kept[2 * rows + 32 :]) + one_value(got[2 * rows + 32 :])
    mid = (take(halves, core) + mid_got.astype(F32)).astype(BF)
    oth_two = two_halves(small_oth)
    mid_got = across(after(mid, oth_two), 4)
    result = input_grad(got)

    own_two = two_halves(small_own)
    got = lax.ppermute(jnp.concatenate([total[rows:].astype(BF), oth_two]), "tensor", [(0, 1), (1, 0)])
    total = total[:rows] + got[:rows].astype(F32)
    small = one_value(own_two) + one_value(got[rows:])

    halves = total.reshape(2, rows // 2, -1)
    two = two_halves(small)
    got = across(jnp.concatenate([take(halves, 1 - near).astype(BF), two]), 2)
    total = take(halves, near) + got[: rows // 2].astype(F32)
    small = one_value(two) + one_value(got[rows // 2 :])

    bit = 4
    while bit < devices:
        sent = jnp.concatenate([total.astype(BF), two_halves(small)])
        mid = (mid.astype(F32) + mid_got.astype(F32)).astype(BF)
        if 2 * bit < devices:
            mid_got = across(mid, 2 * bit)
        got = across(sent, bit)
        total = sent[: rows // 2].astype(F32) + got[: rows // 2].astype(F32)
        small = one_value(sent[rows // 2 :]) + one_value(got[rows // 2 :])
        bit *= 2
    mid = in_order(mid, across(mid, 1), core)
    mid = in_order(after(mid, got), after(across(mid, 2), got), near)

    up = mid.shape[0] * 2 // 3
    mid = mid[:up // 2].astype(F32), mid[up // 2 : up].astype(F32), mid[up:].astype(F32)
    mid = mid[0], mid[1], jnp.concatenate([mid[2][:, : sent.shape[1]], mid[2][:, sent.shape[1] :]])

    total = total.astype(BF)
    total = in_order(total, across(total, 2), near)
    total = in_order(total, across(total, 1), core)
    return total.astype(F32), small, mid, result


def mask_parts(known, lengths, halves):
    tokens, slots = known.shape[0] // halves, lengths.shape[0]
    positions = jnp.arange(known.shape[0], dtype=jnp.int32)
    ends = jnp.cumsum(lengths)
    starts = ends - lengths
    inside = (positions[:, None] >= starts[None, :]) & (positions[:, None] < ends[None, :])
    opening = jnp.any((positions[:, None] == starts[None, :]) & (lengths[None, :] > 0), axis=1)
    live = ((known > 0) | opening).astype(jnp.int32).reshape(halves, 1, tokens)
    place = jnp.where(live > 0, jnp.cumsum(live, axis=2) - 1, -1)
    counts = jnp.sum(live, axis=2)
    before = lambda ats: jnp.sum(
        jnp.where(positions.reshape(halves, 1, tokens) < ats[None, :, None], live, 0), axis=2
    )
    past = jnp.full((halves, LANES - HD - slots - 1), tokens, jnp.int32)
    none = jnp.full((halves, HD), tokens, jnp.int32)
    low = jnp.concatenate([none, before(starts), counts, past], axis=1)
    high = jnp.concatenate([none, before(ends), jnp.full((halves, 1), tokens, jnp.int32), past], axis=1)
    queries = jnp.where(jnp.pad(inside, ((0, 0), (0, 1))), 0.0, -MASK_BIG)
    queries = jnp.pad(queries, ((0, 0), (0, HD - slots - 1))).T.astype(BF)
    return place, jnp.stack([low, high], axis=1), queries, jnp.max(counts)


def local(
    devices, layer_input, gene_known, cell_genes, w_qkv, bias_qv, w_out, b_out, ln1_gain, ln1_bias,
    w_up, b_up, w_down, b_down, ln2_gain, ln2_bias, cotangent,
):
    tokens, width = layer_input.shape
    shard = w_qkv.shape[2]
    side, index = lax.axis_index("tensor"), lax.axis_index("dp")
    core, near = lax.rem(index, 2), lax.rem(index // 2, 2)

    def swapped(values):
        return lax.ppermute(values, "tensor", [(0, 1), (1, 0)])

    def across(values, bit):
        return lax.ppermute(values, "dp", [(i, i ^ bit) for i in range(devices)])

    w_own = w_qkv.transpose(1, 0, 2)
    quarter = 3 * width // 4
    mine = lax.dynamic_slice_in_dim(w_own.reshape(3 * width, shard), (2 * core + near) * quarter, quarter, 0)
    got = swapped(jnp.concatenate([mine, jnp.pad(bias_qv, ((0, 14), (0, 0)))]))
    x_oth = swapped(layer_input)
    piece = got[:quarter]
    piece = in_order(piece, across(piece, 2), near)
    w_oth = in_order(piece, across(piece, 1), core).reshape(3, width, shard)
    bias = jnp.concatenate([bias_qv, got[quarter : quarter + 2]], axis=1).astype(F32)

    place, bounds, query_rows, most = mask_parts(gene_known, cell_genes[0], 2)
    query_own = lax.dynamic_slice_in_dim(query_rows, side * tokens, tokens, 1)
    place_own, place_oth, bounds_own, bounds_oth = take(place, side), take(place, 1 - side), take(bounds, side), take(bounds, 1 - side)
    live = jnp.stack([core, most])
    b_up_row = jnp.pad(b_up[None], ((0, 15), (0, shard)))
    mid_w = jnp.concatenate([w_out, w_down, jnp.concatenate([w_up[:shard], w_up[shard:]], axis=1), b_up_row])
    vectors = jnp.stack([b_out, ln1_gain, ln1_bias, b_down, ln2_gain, ln2_bias, b_out, b_out])

    k_own, v_own, x_live, qt, q = project(layer_input, w_own, w_oth, bias, place_own, bounds_own, query_own)
    x_oth, k_own, mid_w = lax.optimization_barrier((x_oth, k_own, mid_w))
    mid_w_oth = swapped(mid_w)
    probs, ot, linv, k_oth, v_oth, x_oth = attend(
        live, qt, k_own, v_own, x_oth, w_own, w_oth, bias, place_oth, bounds_oth
    )
    activations, res, dot_turned, dnat, mid_own, mid_oth, small = middle(
        layer_input, cotangent, ot, linv, mid_w, mid_w_oth, vectors
    )
    mid_got = swapped(mid_oth)
    dq, dx_oth, sums, value_grad = attend_backward(
        1, (live,), probs, dot_turned, dnat, q, k_oth, v_oth, x_oth, w_own, w_oth
    )
    mid_got, dq = lax.optimization_barrier((mid_got, dq))
    mid = (mid_own + mid_got.astype(F32)).reshape(2, 3 * shard // 2, width)
    mid_got = across(take(mid, 1 - near).astype(BF), 2)
    dx_got = swapped(dx_oth)
    sent, kept, dq, dk, dv = attend_backward(
        0, (live, small, value_grad), probs, dot_turned, dnat, q, k_own, v_own, x_live, dq, sums, layer_input
    )
    mid_got, dx_got, sent = lax.optimization_barrier((mid_got, dx_got, sent))
    mid = take(mid, near) + mid_got.astype(F32)

    def input_grad(token):
        return input_gradient(res, dx_got, after(dq, token), dk, dv, w_own, w_oth, place_own)

    qkv, small, mid, input_grad = sum_gradients(sent, kept, mid, input_grad, devices)
    qkv_g = qkv.reshape(3, width, shard).transpose(1, 0, 2)
    wide = jnp.concatenate([small[:6], small[8:14]], axis=1)
    out_g, down_g, up_g = mid
    return (
        activations, input_grad, qkv_g, jnp.stack([small[7], small[15]]), out_g, wide[0], wide[1], wide[2],
        up_g, small[6], down_g, wide[3], wide[4], wide[5],
    )


def solution(mesh):
    placed = (
        P(("dp", "tensor"), None),
        P("dp"),
        P("dp", None),
        P(None, None, "tensor"),
        P(None, "tensor"),
        P("tensor", None),
        P(),
        P(),
        P(),
        P(None, "tensor"),
        P("tensor"),
        P("tensor", None),
        P(),
        P(),
        P(),
        P(("dp", "tensor"), None),
    )
    return jax.shard_map(
        functools.partial(local, mesh.shape["dp"]),
        mesh=mesh,
        in_specs=placed,
        out_specs=(
            P(("dp", "tensor"), None),
            P(("dp", "tensor"), None),
            P(None, None, "tensor"),
            P(None, "tensor"),
            P("tensor", None),
            P(),
            P(),
            P(),
            P(None, "tensor"),
            P("tensor"),
            P("tensor", None),
            P(),
            P(),
            P(),
        ),
        check_vma=False,
    )
```

```python
import functools

import jax
import jax.numpy as jnp
from jax import lax
from jax.experimental import pallas as pl
from jax.experimental.pallas import tpu as pltpu
from jax.sharding import PartitionSpec as P

HD = 64
LANES = 128
NORM_EPS = 1e-05
MASK_BIG = 2.0**100
LOG2E = 1.4426950408889634
VMEM_BYTES = 58 * 2**20
BF = jnp.bfloat16
F32 = jnp.float32
VMEM = pl.BlockSpec(memory_space=pltpu.VMEM)
HBM = pl.BlockSpec(memory_space=pl.ANY)


def dot(left, right, left_dim, right_dim):
    return lax.dot_general(
        left, right, (((left_dim,), (right_dim,)), ((), ())), preferred_element_type=F32
    )


def params():
    return pltpu.CompilerParams(vmem_limit_bytes=VMEM_BYTES)


def cost(macs, moved):
    return pl.CostEstimate(flops=2 * macs, bytes_accessed=moved, transcendentals=0)


def values_columns(rows):
    lane = lax.broadcasted_iota(jnp.int32, (rows, LANES), 1)
    return jnp.where((lane == HD) | (lane == HD + 1), 1.0, 0.0)


def live_rows(place_ref, first, rows, columns=slice(None)):
    place = place_ref[:, columns]
    row = lax.broadcasted_iota(jnp.int32, (rows, place.shape[1]), 0) + first
    return jnp.where(row == place, 1.0, 0.0).astype(BF)


def key_value_block(x_ref, place_ref, bounds_ref, w_refs, bias_ref, x_out, k_ref, v_ref, first, rows, base=0):
    at, to = pl.ds(first, rows), pl.ds(base + first, rows)
    later = slice(first, None) if isinstance(first, int) else slice(None)
    x = dot(live_rows(place_ref, first, rows, later), x_ref[later, :], 1, 0).astype(BF)
    x_out[at, :] = x
    shard = w_refs[0].shape[2]
    row = lax.broadcasted_iota(jnp.int32, (rows, LANES), 0) + first
    extra_k = jnp.where((row >= bounds_ref[0:1, :]) & (row < bounds_ref[1:2, :]), 1.0, 0.0)
    extra_v = values_columns(rows)
    low = lax.broadcasted_iota(jnp.int32, (rows, LANES), 1) < HD
    for side, w_ref in enumerate(w_refs):
        mine = slice(side * shard, (side + 1) * shard)
        keys = dot(x, w_ref[1], 1, 0)
        values = dot(x, w_ref[2], 1, 0) + bias_ref[1:2, mine]
        for i in range(shard // HD):
            pair = slice((i // 2) * LANES, (i // 2 + 1) * LANES)
            k_pair, v_pair = keys[:, pair], values[:, pair]
            if i % 2:
                k_pair, v_pair = pltpu.roll(k_pair, HD, 1), pltpu.roll(v_pair, HD, 1)
            h = side * (shard // HD) + i
            k_ref[h, to, :] = jnp.where(low, k_pair, extra_k).astype(BF)
            v_ref[h, to, :] = jnp.where(low, v_pair, extra_v).astype(BF)


def project_kernel(x_ref, own_ref, oth_ref, bias_ref, place_ref, bounds_ref, extra_q_ref, k_ref, v_ref, x_out, qt_ref, q_ref):
    block = q_ref.shape[0]
    first = pl.multiple_of(pl.program_id(0) * block, block)
    shard = own_ref.shape[2]
    key_value_block(
        x_ref, place_ref, bounds_ref, (own_ref, oth_ref), bias_ref, x_out, k_ref, v_ref, first, block
    )
    x = x_ref[pl.ds(first, block), :]
    for side, w_ref in enumerate((own_ref, oth_ref)):
        mine = slice(side * shard, (side + 1) * shard)
        q = (dot(x, w_ref[0], 1, 0) + bias_ref[0:1, mine]).astype(BF)
        q_ref[:, mine] = q
        turned = q.T
        for i in range(shard // HD):
            h = side * (shard // HD) + i
            qt_ref[h, :HD, :] = turned[i * HD : (i + 1) * HD, :]
            qt_ref[h, HD:, :] = extra_q_ref[...]


def project(x, w_own, w_oth, bias, place, bounds, extra_q):
    tokens, width = x.shape
    heads = width // HD
    block = 256
    whole = lambda *shape: pl.BlockSpec(shape, lambda i: (0,) * len(shape))
    per_head = whole(heads, tokens, LANES)
    return pl.pallas_call(
        project_kernel,
        grid=(tokens // block,),
        out_shape=(
            jax.ShapeDtypeStruct((heads, tokens, LANES), BF),
            jax.ShapeDtypeStruct((heads, tokens, LANES), BF),
            jax.ShapeDtypeStruct((tokens, width), BF),
            jax.ShapeDtypeStruct((heads, LANES, tokens), BF),
            jax.ShapeDtypeStruct((tokens, width), BF),
        ),
        in_specs=[
            whole(*x.shape),
            whole(*w_own.shape),
            whole(*w_oth.shape),
            whole(*bias.shape),
            whole(*place.shape),
            whole(*bounds.shape),
            pl.BlockSpec((HD, block), lambda i: (0, i)),
        ],
        out_specs=(
            per_head,
            per_head,
            whole(tokens, width),
            pl.BlockSpec((heads, LANES, block), lambda i: (0, 0, i)),
            pl.BlockSpec((block, width), lambda i: (i, 0)),
        ),
        compiler_params=params(),
        cost_estimate=cost(5 * tokens * width * width, 12 * tokens * width),
        name="project",
    )(x, w_own, w_oth, bias, place, bounds, extra_q)


def key_sizes(keys):
    return (keys * 13 // 16, keys)


def for_size(live, keys, work):
    below = 0
    for n, size in enumerate(key_sizes(keys)):

        @pl.when((live > below) & (live <= size) if below else live <= size)
        def _():
            work(size, n > 0)

        below = size


def sweep(rolled, size, count, body, carry=0):
    rows = size // count
    if rolled:
        return lax.fori_loop(0, count, lambda i, held: body(pl.multiple_of(i * rows, rows), held), carry)
    for i in range(count):
        carry = body(i * rows, carry)
    return carry


def attend_kernel(
    count, chunk, live_ref, qt_hbm, k_hbm, v_hbm, x_ref, own_ref, oth_ref, bias_ref, place_ref, bounds_ref,
    p_hbm, ot_ref, linv_ref, k_oth_hbm, v_oth_hbm, x_oth_hbm,
    qt_ref, k_ref, v_ref, x1_ref,
    s0_scr, s1_scr, peak0_scr, peak1_scr, row_scr, acc_scr, p_scr, sem, in_sem, out_sem,
):
    heads, _, queries = qt_ref.shape
    half = x_ref.shape[0]
    parts = queries // chunk
    steps = heads * parts
    slots = p_scr.shape[0]

    def copies_in(h):
        return [
            pltpu.make_async_copy(src.at[h], dst, in_sem.at[h, n])
            for n, (src, dst) in enumerate(
                ((qt_hbm, qt_ref.at[h]), (k_hbm, k_ref.at[h, :half]), (v_hbm, v_ref.at[h, :half]))
            )
        ]

    for h in range(heads):
        for copy in copies_in(h):
            copy.start()

    def project_live(size, rolled):
        def block(first, carry):
            key_value_block(
                x_ref, place_ref, bounds_ref, (own_ref, oth_ref), bias_ref, x1_ref, k_ref, v_ref, first, size // count, half
            )
            return carry

        sweep(rolled, size, count, block)
        if size < half:
            x1_ref[size:, :] = jnp.zeros((half - size, x1_ref.shape[1]), BF)

    for_size(live_ref[1], half, project_live)

    copies_kv = [
        pltpu.make_async_copy(k_ref.at[:, half:, :], k_oth_hbm, out_sem.at[0]),
        pltpu.make_async_copy(v_ref.at[:, half:, :], v_oth_hbm, out_sem.at[1]),
        pltpu.make_async_copy(x1_ref, x_oth_hbm, out_sem.at[2]),
    ]
    for copy in copies_kv:
        copy.start()

    def columns(step):
        return pl.ds(pl.multiple_of(lax.rem(step, parts) * chunk, chunk), chunk)

    def copies_out(step, size):
        slot = lax.rem(step, slots)
        copies = []
        for part in range(2):
            rows = slice(part * half, part * half + size)
            to = p_hbm.at[step // parts, rows, columns(step)]
            copies.append(pltpu.make_async_copy(p_scr.at[slot, rows, :], to, sem.at[slot, part]))
        return copies

    def scores(step, s_ref, peak, rows):
        s = dot(k_ref[step // parts, rows, :], qt_ref[step // parts, :, columns(step)], 1, 0)
        s_ref[rows, :] = s
        return jnp.maximum(peak, jnp.max(s.reshape(-1, 8, chunk), axis=0))

    def mix(step, s_ref, rows):
        p = jnp.exp2((s_ref[rows, :] - row_scr[...]) * (LOG2E * HD**-0.5)).astype(BF)
        p_scr[lax.rem(step, slots), rows, :] = p
        return dot(v_ref[step // parts, rows, :], p, 0, 0)

    def over_keys(size, rolled, block, carry):
        if size == half:
            return sweep(rolled, 2 * half, 2 * count, lambda at, held: block(pl.ds(at, size // count), held), carry)
        for part in range(2):
            rows = lambda at, held: block(pl.ds(part * half + at, size // count), held)
            carry = sweep(rolled, size, count, rows, carry)
        return carry

    def run(size, rolled, step, s_ref, peak_ref, after, s_after, peak_after):
        row_scr[...] = jnp.max(peak_ref[...], axis=0, keepdims=True)

        @pl.when(step >= slots)
        def _():
            for copy in copies_out(step - slots, size):
                copy.wait()

        def block(rows, held):
            peak = scores(after, s_after, held[0], rows)
            return peak, held[1] + mix(step, s_ref, rows)

        start = (jnp.full((8, chunk), -jnp.inf, F32), jnp.zeros((LANES, chunk), F32))
        peak_after[...], acc_scr[...] = over_keys(size, rolled, block, start)
        for copy in copies_out(step, size):
            copy.start()
        inverse = 1.0 / acc_scr[HD : HD + 1, :]
        linv_ref[step // parts, :, columns(step)] = inverse
        ot_ref[step // parts, :, columns(step)] = acc_scr[:HD, :] * inverse

    for copy in copies_in(0):
        copy.wait()

    def work(size, rolled):
        def first_block(rows, peak):
            return scores(0, s0_scr, peak, rows)

        peak0_scr[...] = over_keys(size, rolled, first_block, jnp.full((8, chunk), -jnp.inf, F32))

        @pl.loop(0, steps // 2)
        def _(i):
            run(size, rolled, 2 * i, s0_scr, peak0_scr, 2 * i + 1, s1_scr, peak1_scr)
            after = 2 * i + 2

            @pl.when((after < steps) & (lax.rem(after, parts) == 0))
            def _():
                for copy in copies_in(after // parts):
                    copy.wait()

            run(size, rolled, 2 * i + 1, s1_scr, peak1_scr, jnp.minimum(after, steps - 1), s0_scr, peak0_scr)

        for slot in range(slots):
            for copy in copies_out(steps - slots + slot, size):
                copy.wait()

    for_size(live_ref[1], half, work)
    for copy in copies_kv:
        copy.wait()


def attend(live, qt, k_own, v_own, x_oth, w_own, w_oth, bias, place, bounds):
    heads, _, queries = qt.shape
    keys = 2 * queries
    count, chunk, slots = 4, 512, 4
    per_head = jax.ShapeDtypeStruct(k_own.shape, BF)
    return pl.pallas_call(
        functools.partial(attend_kernel, count, chunk),
        out_shape=(
            jax.ShapeDtypeStruct((heads, keys, queries), BF),
            jax.ShapeDtypeStruct((heads, HD, queries), F32),
            jax.ShapeDtypeStruct((heads, 1, queries), F32),
            per_head,
            per_head,
            jax.ShapeDtypeStruct(x_oth.shape, BF),
        ),
        in_specs=[pl.BlockSpec(memory_space=pltpu.SMEM)] + [HBM] * 3 + [VMEM] * 6,
        out_specs=(HBM, VMEM, VMEM, HBM, HBM, HBM),
        scratch_shapes=[
            pltpu.VMEM(qt.shape, BF),
            pltpu.VMEM((heads, keys, LANES), BF),
            pltpu.VMEM((heads, keys, LANES), BF),
            pltpu.VMEM(x_oth.shape, BF),
            pltpu.VMEM((keys, chunk), F32),
            pltpu.VMEM((keys, chunk), F32),
            pltpu.VMEM((8, chunk), F32),
            pltpu.VMEM((8, chunk), F32),
            pltpu.VMEM((1, chunk), F32),
            pltpu.VMEM((LANES, chunk), F32),
            pltpu.VMEM((slots, keys, chunk), BF),
            pltpu.SemaphoreType.DMA((slots, 2)),
            pltpu.SemaphoreType.DMA((heads, 3)),
            pltpu.SemaphoreType.DMA((3,)),
        ],
        compiler_params=params(),
        cost_estimate=cost(heads * keys * queries * 512, 2 * heads * keys * queries),
        name="attend",
    )(live, qt, k_own, v_own, x_oth, w_own, w_oth, bias, place, bounds)


def normalize(values):
    mean = jnp.mean(values, axis=-1, keepdims=True)
    centered = values - mean
    inverse = lax.rsqrt(jnp.mean(centered * centered, axis=-1, keepdims=True) + NORM_EPS)
    return centered * inverse, inverse


def norm_back(e, normed, inverse):
    return inverse * (
        e - jnp.mean(e, axis=-1, keepdims=True) - normed * jnp.mean(e * normed, axis=-1, keepdims=True)
    )


def middle_kernel(
    sub, x_ref, cot_ref, ot_ref, linv_ref, w_own_ref, w_oth_ref, vec_ref,
    act_ref, res_ref, dot_ref, dnat_ref, own_ref, oth_ref, small_ref,
    att_scr, w_out_ref, w_up_ref, w_down_ref, b_up_ref, gw_ref,
):
    block, width = x_ref.shape
    heads = width // HD
    shard = width // 2
    b_out, gain1, bias1, b_down, gain2, bias2 = (vec_ref[i : i + 1, :] for i in range(6))

    @pl.when(pl.program_id(0) == 0)
    def _():
        gw_ref[...] = jnp.zeros_like(gw_ref)
        small_ref[...] = jnp.zeros_like(small_ref)
        for side, ref in enumerate((w_own_ref, w_oth_ref)):
            mine = slice(side * shard, (side + 1) * shard)
            w_out_ref[mine, :] = ref[:shard, :]
            w_down_ref[mine, :] = ref[shard : 2 * shard, :]
            w_up_ref[:shard, mine] = ref[2 * shard : 3 * shard, :shard]
            w_up_ref[shard:, mine] = ref[2 * shard : 3 * shard, shard:]
            b_up_ref[:, mine] = ref[3 * shard : 3 * shard + 1, :shard].astype(F32)

    def col_sum(row, values):
        small_ref[row : row + 1, :] += jnp.sum(values, axis=0, keepdims=True)

    def chain(u):
        rows = slice(u * sub, (u + 1) * sub)
        for h in range(heads):
            att_scr[u, h * HD : (h + 1) * HD, :] = ot_ref[h, :, rows].astype(BF)
        branch = dot(att_scr[u], w_out_ref[...], 0, 0)
        yield
        n1, inv1 = normalize(x_ref[rows, :].astype(F32) + branch + b_out)
        first = n1 * gain1 + bias1
        first_low = first.astype(BF)
        yield
        pre = dot(first_low, w_up_ref[...], 1, 0) + b_up_ref[...]
        yield
        cdf = 0.5 * (1.0 + lax.erf(pre * 0.5**0.5))
        hidden = (pre * cdf).astype(BF)
        slope = cdf + pre * (0.3989422804014327 * jnp.exp(-0.5 * pre * pre))
        yield
        branch = dot(hidden, w_down_ref[...], 1, 0)
        yield
        n2, inv2 = normalize(first + branch + b_down)
        act_ref[rows, :] = (n2 * gain2 + bias2).astype(BF)
        cot = cot_ref[rows, :].astype(F32)
        two = norm_back(cot * gain2, n2, inv2)
        two_low = two.astype(BF)
        yield
        back = dot(two_low, w_down_ref[...], 1, 1)
        gw_ref[2] += dot(hidden, two_low, 0, 0)
        col_sum(3, two)
        col_sum(4, cot * n2)
        col_sum(5, cot)
        yield
        pre_grad = (back * slope).astype(BF)
        yield
        back = dot(pre_grad, w_up_ref[...], 1, 1)
        gw_ref[1] += dot(first_low, pre_grad, 0, 0)
        col_sum(6, pre_grad.astype(F32))
        yield
        one = two + back
        res = norm_back(one * gain1, n1, inv1)
        res_ref[rows, :] = res
        res_low = res.astype(BF)
        yield
        turned = dot(w_out_ref[...], res_low, 1, 1)
        gw_ref[0] += dot(att_scr[u], res_low, 1, 0)
        col_sum(1, one * n1)
        col_sum(2, one)
        col_sum(0, res)
        yield
        pick = lax.broadcasted_iota(jnp.int32, (HD, sub), 0)
        for h in range(heads):
            head = slice(h * HD, (h + 1) * HD)
            grad = (turned[head].astype(BF).astype(F32) * linv_ref[h, :, rows]).astype(BF)
            inner = -jnp.sum(grad.astype(F32) * ot_ref[h, :, rows], axis=0, keepdims=True)
            high = inner.astype(BF).astype(F32)
            dot_ref[h, :HD, rows] = grad
            dot_ref[h, HD:, rows] = jnp.where(pick == 0, high, jnp.where(pick == 1, inner - high, 0.0)).astype(BF)
            att_scr[u, head, :] = grad
        dnat_ref[rows, :] = att_scr[u].T
        yield

    for _ in zip(*(chain(u) for u in range(block // sub))):
        pass

    @pl.when(pl.program_id(0) == pl.num_programs(0) - 1)
    def _():
        for ref, mine in ((own_ref, slice(0, shard)), (oth_ref, slice(shard, width))):
            ref[:shard, :] = gw_ref[0, mine, :].astype(ref.dtype)
            ref[shard:width, :] = gw_ref[2, mine, :].astype(ref.dtype)
            ref[width:, :shard] = gw_ref[1, :shard, mine].astype(ref.dtype)
            ref[width:, shard:] = gw_ref[1, shard:, mine].astype(ref.dtype)


def middle(x, cot, ot, linv, w_own, w_oth, vectors):
    tokens, width = x.shape
    heads = width // HD
    block, sub = 512, 256
    whole = lambda *shape: pl.BlockSpec(shape, lambda i: (0,) * len(shape))
    rows = pl.BlockSpec((block, width), lambda i: (i, 0))
    columns = lambda n: pl.BlockSpec((heads, n, block), lambda i: (0, 0, i))
    square = pltpu.VMEM((width, width), BF)
    return pl.pallas_call(
        functools.partial(middle_kernel, sub),
        grid=(tokens // block,),
        out_shape=(
            jax.ShapeDtypeStruct((tokens, width), BF),
            jax.ShapeDtypeStruct((tokens, width), F32),
            jax.ShapeDtypeStruct((heads, LANES, tokens), BF),
            jax.ShapeDtypeStruct((tokens, width), BF),
            jax.ShapeDtypeStruct((3 * width // 2, width), F32),
            jax.ShapeDtypeStruct((3 * width // 2, width), BF),
            jax.ShapeDtypeStruct((8, width), F32),
        ),
        in_specs=[rows, rows, columns(HD), columns(1), whole(*w_own.shape), whole(*w_oth.shape), whole(*vectors.shape)],
        out_specs=(
            rows, rows, columns(LANES), rows,
            whole(3 * width // 2, width), whole(3 * width // 2, width), whole(8, width),
        ),
        scratch_shapes=[
            pltpu.VMEM((block // sub, width, sub), BF), square, square, square,
            pltpu.VMEM((1, width), F32), pltpu.VMEM((3, width, width), F32),
        ],
        compiler_params=params(),
        cost_estimate=cost(9 * tokens * width * width, 20 * tokens * width),
        name="middle",
    )(x, cot, ot, linv, w_own, w_oth, vectors)


def times_weights(grad, own_ref, oth_ref, third):
    shard = own_ref.shape[2]
    return dot(grad[:, :shard], own_ref[third], 1, 1) + dot(grad[:, shard:], oth_ref[third], 1, 1)


def backward_kernel(sub, part, *refs):
    if part:
        (live_ref, p_hbm, dot_hbm, dnat_hbm, q_hbm, k_hbm, v_hbm, x_hbm, own_hbm, oth_hbm,
         dq_hbm, dx_ref, gw_ref, bias_ref,
         dot_ref, dnat_ref, q_ref, k_ref, v_ref, x_ref, own_ref, oth_ref,
         dq_ref, dk_ref, dv_ref, acc_scr, p_scr, sem, pair_sem, last_sem, out_sem) = refs
        more = ((own_hbm, own_ref), (oth_hbm, oth_ref))
    else:
        (live_ref, small_ref, value_ref,
         p_hbm, dot_hbm, dnat_hbm, q_hbm, k_hbm, v_hbm, x_hbm, dq_hbm, gw_hbm, whole_hbm,
         sent_ref, kept_ref, dq_out, dk_hbm, dv_hbm,
         dot_ref, dnat_ref, q_ref, k_ref, v_ref, x_ref, before_ref, gw_ref, whole_ref,
         dq_ref, dk_ref, dv_ref, gq_ref, bias_ref, acc_scr, p_scr, sem, pair_sem, last_sem, out_sem) = refs
        more = ((dq_hbm, before_ref), (gw_hbm, gw_ref), (whole_hbm, whole_ref))
    heads, _, queries = dot_ref.shape
    keys = k_ref.shape[1]
    width = heads * HD
    shard = width // 2
    slots = p_scr.shape[0]
    pairs = heads // 2

    def copy_in(p, j, size):
        block = size // 2
        slot = lax.rem(p * 2 + j, slots)
        first = part * keys + j * block
        if not isinstance(j, int):
            first = pl.multiple_of(first, 16)
        src = p_hbm.at[pl.ds(2 * p, 2), pl.ds(first, block), :]
        return pltpu.make_async_copy(src, p_scr.at[slot, :, :block, :], sem.at[slot])

    def pair_copies(p):
        pair = pl.ds(2 * p, 2)
        lanes = pl.ds(pl.multiple_of(p * LANES, LANES), LANES)
        by_head = ((dot_hbm, dot_ref), (k_hbm, k_ref), (v_hbm, v_ref))
        by_lane = ((dnat_hbm, dnat_ref), (q_hbm, q_ref))
        return [
            pltpu.make_async_copy(src.at[pair], dst.at[pair], pair_sem.at[p, n]) for n, (src, dst) in enumerate(by_head)
        ] + [
            pltpu.make_async_copy(src.at[:, lanes], dst.at[:, lanes], pair_sem.at[p, 3 + n])
            for n, (src, dst) in enumerate(by_lane)
        ]

    last = ((x_hbm, x_ref),) + more

    def rows_out(p):
        rows = pl.ds(pl.multiple_of(p * 2 * HD, 2 * HD), 2 * HD)
        return pltpu.make_async_copy(dq_ref.at[rows, :], dq_hbm.at[rows, :], out_sem.at[p])

    last_copies = [pltpu.make_async_copy(src, dst, last_sem.at[n]) for n, (src, dst) in enumerate(last)]

    for copy in pair_copies(0):
        copy.start()

    def work(size, rolled):
        block, rows = size // 2, size // 2
        low = lax.broadcasted_iota(jnp.int32, (rows, LANES), 1) < HD
        if size < keys:
            dk_ref[size:, :] = jnp.zeros((keys - size, width), BF)
            dv_ref[size:, :] = jnp.zeros((keys - size, width), BF)
        for step in range(slots - 1):
            copy_in(step // 2, step % 2, size).start()

        @pl.loop(0, pairs)
        def _(p):
            lanes = pl.ds(pl.multiple_of(p * LANES, LANES), LANES)
            for copy in pair_copies(p):
                copy.wait()

            @pl.when(p + 1 < pairs)
            def _():
                for copy in pair_copies(p + 1):
                    copy.start()

            @pl.when(p == 1)
            def _():
                for copy in last_copies:
                    copy.start()

            acc_scr[...] = jnp.zeros_like(acc_scr)

            def one_block(j):
                slot = lax.rem(p * 2 + j, slots)
                copy_in(p, j, size).wait()
                ahead = 2 * p + j + slots - 1

                @pl.when(ahead < 2 * pairs)
                def _():
                    copy_in(ahead // 2, lax.rem(ahead, 2), size).start()

                def at_rows(at, total):
                    here = pl.ds(pl.multiple_of(j * block + at, 16), rows)
                    total, dks, dvs = list(total), [], []
                    for side in range(2):
                        h = 2 * p + side
                        prob = p_scr[slot, side, pl.ds(at, rows), :]
                        slope = dot(v_ref[h, here, :], dot_ref[h], 1, 0)
                        dvs.append(dot(prob, dnat_ref[:, lanes], 1, 0))
                        ds = (prob.astype(F32) * slope).astype(BF)
                        dks.append(dot(ds, q_ref[:, lanes], 1, 0))
                        total[side] = total[side] + dot(k_ref[h, here, :], ds, 0, 0)
                    dk_ref[here, lanes] = (jnp.where(low, dks[0], dks[1]) * HD**-0.5).astype(BF)
                    dv_ref[here, lanes] = jnp.where(low, dvs[0], dvs[1]).astype(BF)
                    return tuple(total)

                zero = jnp.zeros((LANES, queries), F32)
                for side, total in enumerate(sweep(rolled, block, 1, at_rows, (zero, zero))):
                    acc_scr[side] += total

            pl.loop(0, 2)(one_block)

            for side in range(2):
                dq_ref[pl.ds(pl.multiple_of((2 * p + side) * HD, HD), HD), :] = acc_scr[side, :HD, :]
            if part:
                rows_out(p).start()

    for_size(live_ref[1], keys, work)
    for copy in last_copies:
        copy.wait()
    if part:
        copies_out = [rows_out(p) for p in range(heads // 2)]
    else:
        copies_out = [
            pltpu.make_async_copy(dk_ref, dk_hbm, out_sem.at[0]),
            pltpu.make_async_copy(dv_ref, dv_hbm, out_sem.at[1]),
        ]
        for copy in copies_out:
            copy.start()

    for n, grad_ref in enumerate((dk_ref, dv_ref)):
        grad = dot(x_ref[...], grad_ref[...], 0, 0)
        gw_ref[n] = grad if part else gw_ref[n] + grad
    bias_ref[1:2, :] = jnp.sum(dv_ref[...].astype(F32), axis=0, keepdims=True)
    if part:
        bias_ref[0:1, :] = jnp.zeros((1, width), F32)

        @pl.loop(0, keys // sub)
        def _(i):
            rows = pl.ds(pl.multiple_of(i * sub, sub), sub)
            dk, dv = dk_ref[rows, :], dv_ref[rows, :]
            dx = times_weights(dk, own_ref, oth_ref, 1) + times_weights(dv, own_ref, oth_ref, 2)
            dx_ref[rows, :] = dx.astype(BF)
    else:
        dq_out[...] = ((before_ref[...] + dq_ref[...]) * HD**-0.5).astype(BF).T
        gq_ref[...] = dot(whole_ref[...], dq_out[...], 0, 0)
        bias_ref[0:1, :] = jnp.sum(dq_out[...].astype(F32), axis=0, keepdims=True)

    if not part:
        first = live_ref[0] == 0
        bias_ref[1:2, :] += value_ref[1:2, :]
        cut = 3 * width // 2
        for side in range(2):
            mine = slice(side * shard, (side + 1) * shard)
            pieces = [gq_ref[:, mine], gw_ref[0, :, mine], gw_ref[1, :, mine]]
            blocks = [piece[at : at + shard, :].astype(BF) for piece in pieces for at in (0, shard)]
            for n in range(3):
                to = slice(side * cut + n * shard, side * cut + (n + 1) * shard)
                kept_ref[to, :] = jnp.where(first, blocks[n], blocks[3 + n])
                sent_ref[to, :] = jnp.where(first, blocks[3 + n], blocks[n])
            rows16 = [small_ref[:6, :shard], small_ref[6:7, mine], bias_ref[0:1, mine]]
            rows16 += [small_ref[:6, shard:], jnp.zeros((1, shard), F32), bias_ref[1:2, mine]]
            value = jnp.concatenate(rows16, axis=0)
            high = value.astype(BF)
            for n, half in enumerate((high, (value - high.astype(F32)).astype(BF))):
                to = slice(2 * cut + (2 * side + n) * 16, 2 * cut + (2 * side + n + 1) * 16)
                kept_ref[to, :] = half
                sent_ref[to, :] = half

    for copy in copies_out:
        copy.wait()


def attend_backward(part, first, probs, dot_turned, dnat, q, k, v, x, *more):
    heads, keys, queries = probs.shape
    width = heads * HD
    sub, slots = 256, 4
    sums = jax.ShapeDtypeStruct((2, width, width), F32)
    turned = jax.ShapeDtypeStruct((width, queries), F32)
    grad = jax.ShapeDtypeStruct((queries, width), BF)
    inputs = (dot_turned, dnat, q, k, v, x) + more
    held = [pltpu.VMEM(a.shape, a.dtype) for a in inputs]
    held += [pltpu.VMEM(turned.shape, F32), pltpu.VMEM(grad.shape, BF), pltpu.VMEM(grad.shape, BF)]
    if part:
        out_shape = (turned, grad, sums, jax.ShapeDtypeStruct((2, width), F32))
        out_specs = (HBM, VMEM, VMEM, VMEM)
    else:
        payload = jax.ShapeDtypeStruct((3 * width + 64, width // 2), BF)
        out_shape = (payload, payload, grad, grad, grad)
        out_specs = (VMEM, VMEM, VMEM, HBM, HBM)
        held += [pltpu.VMEM((width, width), F32), pltpu.VMEM((2, width), F32)]
    first_specs = [pl.BlockSpec(memory_space=pltpu.SMEM), VMEM, VMEM][: len(first)]
    return pl.pallas_call(
        functools.partial(backward_kernel, sub, part),
        out_shape=out_shape,
        in_specs=first_specs + [HBM] * (1 + len(inputs)),
        out_specs=out_specs,
        scratch_shapes=held
        + [
            pltpu.VMEM((2, LANES, queries), F32),
            pltpu.VMEM((slots, 2, keys // 4, queries), BF),
            pltpu.SemaphoreType.DMA((slots,)),
            pltpu.SemaphoreType.DMA((heads // 2, 5)),
            pltpu.SemaphoreType.DMA((1 + len(more),)),
            pltpu.SemaphoreType.DMA((heads // 2,)),
        ],
        compiler_params=params(),
        cost_estimate=cost(heads * keys * queries * 512, heads * keys * queries),
        name="attend_back_own" if not part else "attend_back_other",
    )(*first, probs, *inputs)


def input_kernel(res_ref, got_ref, dq_ref, dk_ref, dv_ref, own_ref, oth_ref, place_ref, dx_ref, live_scr):
    block = res_ref.shape[0]
    step = pl.program_id(0)

    @pl.when(step == 0)
    def _():
        live_scr[...] = jnp.zeros_like(live_scr)

    live_scr[pl.ds(pl.multiple_of(step * block, block), block), :] = (
        times_weights(dk_ref[...], own_ref, oth_ref, 1)
        + times_weights(dv_ref[...], own_ref, oth_ref, 2)
        + got_ref[...].astype(F32)
    ).astype(BF)
    dx = res_ref[...] + times_weights(dq_ref[...], own_ref, oth_ref, 0)
    dx_ref[...] = dx + dot(live_rows(place_ref, 0, live_scr.shape[0]), live_scr[...], 0, 0)


def input_gradient(res, got, dq, dk, dv, w_own, w_oth, place):
    tokens, width = res.shape
    rows = pl.BlockSpec((256, width), lambda i: (i, 0))
    whole = lambda *shape: pl.BlockSpec(shape, lambda i: (0,) * len(shape))
    return pl.pallas_call(
        input_kernel,
        grid=(tokens // 256,),
        out_shape=jax.ShapeDtypeStruct((tokens, width), F32),
        in_specs=[rows] * 5 + [whole(*w_own.shape)] * 2 + [pl.BlockSpec((1, 256), lambda i: (0, i))],
        out_specs=rows,
        scratch_shapes=[pltpu.VMEM(dk.shape, BF)],
        compiler_params=params(),
        cost_estimate=cost(3 * tokens * width * width, 16 * tokens * width),
        name="input_gradient",
    )(res, got, dq, dk, dv, w_own, w_oth, place)


def after(values, *others):
    return lax.optimization_barrier((values,) + others)[0]


def two_halves(values):
    high = values.astype(BF)
    return jnp.concatenate([high, (values - high.astype(F32)).astype(BF)], axis=0)


def one_value(halves):
    rows = halves.shape[0] // 2
    return halves[:rows].astype(F32) + halves[rows:].astype(F32)


def take(values, which):
    return lax.dynamic_index_in_dim(values, which, 0, False)


def in_order(mine, theirs, which):
    return jnp.concatenate([jnp.where(which == 0, mine, theirs), jnp.where(which == 0, theirs, mine)])


def sum_gradients(sent, kept, mid, input_grad, devices):
    index = lax.axis_index("dp")
    core, near = lax.rem(index, 2), lax.rem(index // 2, 2)
    rows = (sent.shape[0] - 64) // 2

    def across(values, bit):
        return lax.ppermute(values, "dp", [(i, i ^ bit) for i in range(devices)])

    got = across(sent, 1)
    halves = mid.reshape(2, mid.shape[0] // 2, -1)
    mid_got = across(take(halves, 1 - core).astype(BF), 1)
    total = kept[: 2 * rows].astype(F32) + got[: 2 * rows].astype(F32)
    small_own = one_value(kept[2 * rows : 2 * rows + 32]) + one_value(got[2 * rows : 2 * rows + 32])
    small_oth = one_value(kept[2 * rows + 32 :]) + one_value(got[2 * rows + 32 :])
    mid = (take(halves, core) + mid_got.astype(F32)).astype(BF)
    oth_two = two_halves(small_oth)
    mid_got = across(after(mid, oth_two), 4)
    result = input_grad(got)

    own_two = two_halves(small_own)
    got = lax.ppermute(jnp.concatenate([total[rows:].astype(BF), oth_two]), "tensor", [(0, 1), (1, 0)])
    total = total[:rows] + got[:rows].astype(F32)
    small = one_value(own_two) + one_value(got[rows:])

    halves = total.reshape(2, rows // 2, -1)
    two = two_halves(small)
    got = across(jnp.concatenate([take(halves, 1 - near).astype(BF), two]), 2)
    total = take(halves, near) + got[: rows // 2].astype(F32)
    small = one_value(two) + one_value(got[rows // 2 :])

    bit = 4
    while bit < devices:
        sent = jnp.concatenate([total.astype(BF), two_halves(small)])
        mid = (mid.astype(F32) + mid_got.astype(F32)).astype(BF)
        if 2 * bit < devices:
            mid_got = across(mid, 2 * bit)
        got = across(sent, bit)
        total = sent[: rows // 2].astype(F32) + got[: rows // 2].astype(F32)
        small = one_value(sent[rows // 2 :]) + one_value(got[rows // 2 :])
        bit *= 2
    mid = in_order(mid, across(mid, 1), core)
    mid = in_order(after(mid, got), after(across(mid, 2), got), near)

    up = mid.shape[0] * 2 // 3
    mid = mid[:up // 2].astype(F32), mid[up // 2 : up].astype(F32), mid[up:].astype(F32)
    mid = mid[0], mid[1], jnp.concatenate([mid[2][:, : sent.shape[1]], mid[2][:, sent.shape[1] :]])

    total = total.astype(BF)
    total = in_order(total, across(total, 2), near)
    total = in_order(total, across(total, 1), core)
    return total.astype(F32), small, mid, result


def mask_parts(known, lengths, halves):
    tokens, slots = known.shape[0] // halves, lengths.shape[0]
    positions = jnp.arange(known.shape[0], dtype=jnp.int32)
    ends = jnp.cumsum(lengths)
    starts = ends - lengths
    inside = (positions[:, None] >= starts[None, :]) & (positions[:, None] < ends[None, :])
    opening = jnp.any((positions[:, None] == starts[None, :]) & (lengths[None, :] > 0), axis=1)
    live = ((known > 0) | opening).astype(jnp.int32).reshape(halves, 1, tokens)
    place = jnp.where(live > 0, jnp.cumsum(live, axis=2) - 1, -1)
    counts = jnp.sum(live, axis=2)
    before = lambda ats: jnp.sum(
        jnp.where(positions.reshape(halves, 1, tokens) < ats[None, :, None], live, 0), axis=2
    )
    past = jnp.full((halves, LANES - HD - slots - 1), tokens, jnp.int32)
    none = jnp.full((halves, HD), tokens, jnp.int32)
    low = jnp.concatenate([none, before(starts), counts, past], axis=1)
    high = jnp.concatenate([none, before(ends), jnp.full((halves, 1), tokens, jnp.int32), past], axis=1)
    queries = jnp.where(jnp.pad(inside, ((0, 0), (0, 1))), 0.0, -MASK_BIG)
    queries = jnp.pad(queries, ((0, 0), (0, HD - slots - 1))).T.astype(BF)
    return place, jnp.stack([low, high], axis=1), queries, jnp.max(counts)


def local(
    devices, layer_input, gene_known, cell_genes, w_qkv, bias_qv, w_out, b_out, ln1_gain, ln1_bias,
    w_up, b_up, w_down, b_down, ln2_gain, ln2_bias, cotangent,
):
    tokens, width = layer_input.shape
    shard = w_qkv.shape[2]
    side, index = lax.axis_index("tensor"), lax.axis_index("dp")
    core, near = lax.rem(index, 2), lax.rem(index // 2, 2)

    def swapped(values):
        return lax.ppermute(values, "tensor", [(0, 1), (1, 0)])

    def across(values, bit):
        return lax.ppermute(values, "dp", [(i, i ^ bit) for i in range(devices)])

    w_own = w_qkv.transpose(1, 0, 2)
    quarter = 3 * width // 4
    mine = lax.dynamic_slice_in_dim(w_own.reshape(3 * width, shard), (2 * core + near) * quarter, quarter, 0)
    got = swapped(jnp.concatenate([mine, jnp.pad(bias_qv, ((0, 14), (0, 0)))]))
    x_oth = swapped(layer_input)
    piece = got[:quarter]
    piece = in_order(piece, across(piece, 2), near)
    w_oth = in_order(piece, across(piece, 1), core).reshape(3, width, shard)
    bias = jnp.concatenate([bias_qv, got[quarter : quarter + 2]], axis=1).astype(F32)

    place, bounds, query_rows, most = mask_parts(gene_known, cell_genes[0], 2)
    query_own = lax.dynamic_slice_in_dim(query_rows, side * tokens, tokens, 1)
    place_own, place_oth, bounds_own, bounds_oth = take(place, side), take(place, 1 - side), take(bounds, side), take(bounds, 1 - side)
    live = jnp.stack([core, most])
    b_up_row = jnp.pad(b_up[None], ((0, 15), (0, shard)))
    mid_w = jnp.concatenate([w_out, w_down, jnp.concatenate([w_up[:shard], w_up[shard:]], axis=1), b_up_row])
    vectors = jnp.stack([b_out, ln1_gain, ln1_bias, b_down, ln2_gain, ln2_bias, b_out, b_out])

    k_own, v_own, x_live, qt, q = project(layer_input, w_own, w_oth, bias, place_own, bounds_own, query_own)
    x_oth, k_own, mid_w = lax.optimization_barrier((x_oth, k_own, mid_w))
    mid_w_oth = swapped(mid_w)
    probs, ot, linv, k_oth, v_oth, x_oth = attend(
        live, qt, k_own, v_own, x_oth, w_own, w_oth, bias, place_oth, bounds_oth
    )
    activations, res, dot_turned, dnat, mid_own, mid_oth, small = middle(
        layer_input, cotangent, ot, linv, mid_w, mid_w_oth, vectors
    )
    mid_got = swapped(mid_oth)
    dq, dx_oth, sums, value_grad = attend_backward(
        1, (live,), probs, dot_turned, dnat, q, k_oth, v_oth, x_oth, w_own, w_oth
    )
    mid_got, dq = lax.optimization_barrier((mid_got, dq))
    mid = (mid_own + mid_got.astype(F32)).reshape(2, 3 * shard // 2, width)
    mid_got = across(take(mid, 1 - near).astype(BF), 2)
    dx_got = swapped(dx_oth)
    sent, kept, dq, dk, dv = attend_backward(
        0, (live, small, value_grad), probs, dot_turned, dnat, q, k_own, v_own, x_live, dq, sums, layer_input
    )
    mid_got, dx_got, sent = lax.optimization_barrier((mid_got, dx_got, sent))
    mid = take(mid, near) + mid_got.astype(F32)

    def input_grad(token):
        return input_gradient(res, dx_got, after(dq, token), dk, dv, w_own, w_oth, place_own)

    qkv, small, mid, input_grad = sum_gradients(sent, kept, mid, input_grad, devices)
    qkv_g = qkv.reshape(3, width, shard).transpose(1, 0, 2)
    wide = jnp.concatenate([small[:6], small[8:14]], axis=1)
    out_g, down_g, up_g = mid
    return (
        activations, input_grad, qkv_g, jnp.stack([small[7], small[15]]), out_g, wide[0], wide[1], wide[2],
        up_g, small[6], down_g, wide[3], wide[4], wide[5],
    )


def solution(mesh):
    placed = (
        P(("dp", "tensor"), None),
        P("dp"),
        P("dp", None),
        P(None, None, "tensor"),
        P(None, "tensor"),
        P("tensor", None),
        P(),
        P(),
        P(),
        P(None, "tensor"),
        P("tensor"),
        P("tensor", None),
        P(),
        P(),
        P(),
        P(("dp", "tensor"), None),
    )
    return jax.shard_map(
        functools.partial(local, mesh.shape["dp"]),
        mesh=mesh,
        in_specs=placed,
        out_specs=(
            P(("dp", "tensor"), None),
            P(("dp", "tensor"), None),
            P(None, None, "tensor"),
            P(None, "tensor"),
            P("tensor", None),
            P(),
            P(),
            P(),
            P(None, "tensor"),
            P("tensor"),
            P("tensor", None),
            P(),
            P(),
            P(),
        ),
        check_vma=False,
    )
```
